32 devices in a mesh: fsdp: 8 (over z, core), seq: 4 (over y, x).
Axes of the slice: x: 2, y: 2, z: 4, core: 2. Of those that a mesh axis runs over, the one named last changes fastest.
Arguments:
- inputs: bfloat16 [16, 1024, 1152], P('fsdp', 'seq'), may hold values from -24 to 24
- key_mask: int32 [16, 1024], P('fsdp'), may hold values from 0 to 1, as said below
- w_qkv: bfloat16 [1152, 3456], P('fsdp'), may hold values from -1 to 1
- w_out: bfloat16 [1152, 1152], P('fsdp'), may hold values from -2 to 2
- w_up: bfloat16 [1152, 4304], P('fsdp'), may hold values from -0.1875 to 0.1875
- w_down: bfloat16 [4304, 1152], P(None, 'fsdp'), may hold values from -0.09375 to 0.09375
- norm_gains: bfloat16 [2, 1152], P(None, 'fsdp'), may hold values from 0.099609375 to 1.8984375
- biases: bfloat16 [6, 1152], P(None, 'fsdp'), may hold values from -3 to 3
- up_bias: bfloat16 [4304], P('fsdp'), may hold values from -3 to 3
- cotangent: bfloat16 [16, 1024, 1152], P('fsdp', 'seq'), may hold values from -6 to 6
Outputs:
- layer_out: bfloat16 [16, 1024, 1152], P('fsdp', 'seq')
- grad_in: bfloat16 [16, 1024, 1152], P('fsdp', 'seq')
- grad_qkv: float32 [1152, 3456], P('fsdp')
- grad_proj: float32 [1152, 1152], P('fsdp')
- grad_up: float32 [1152, 4304], P('fsdp')
- grad_down: float32 [4304, 1152], P(None, 'fsdp')
- grad_gains: float32 [2, 1152], P(None, 'fsdp')
- grad_biases: float32 [6, 1152], P(None, 'fsdp')
- grad_upbias: float32 [4304], P('fsdp')
The draws below stay inside these ranges and needn't reach their ends.
Inputs may be any that keep to these rules, and one draw needn't show every extreme that they name: `key_mask`: in each image the live keys are its first L tokens, with L between 512 and 1024; image 0 has L = 512.
All inputs are finite; a program needn't handle non-finite values.
Results may differ from the reference program's by a relative error of at most 0.012.
Values may be sent and summed in bfloat16 or wider, within the bound.
No kernel may reach another device: no remote copies, remote signals or barrier semaphores. Data moves between devices by JAX's collectives and lax.ppermute only.
A program may use at most 256 MiB of HBM per device.

```python
import math
import jax
import jax.numpy as jnp
from jax import lax

D = 1152
HEADS = 16
HEAD_DIM = 72
FF = 4304
SEQ = 1024
IMAGES = 16


def draw_inputs(key, part):
    key = jax.random.fold_in(key, 101)
    base = jnp.clip(jax.random.normal(key, (IMAGES, SEQ, D), jnp.float32), -6.0, 6.0)
    return base.astype(jnp.bfloat16)


def draw_w_qkv(key, part):
    key = jax.random.fold_in(key, 202)
    result = jax.random.normal(key, (D, 3 * D), jnp.float32) / jnp.sqrt(jnp.float32(D))
    return jnp.clip(result, -1.0, 1.0).astype(jnp.bfloat16)


def draw_key_mask(key, part):
    key = jax.random.fold_in(key, 303)
    image_index = jnp.arange(IMAGES, dtype=jnp.int32)[:, None]
    position = jnp.arange(SEQ, dtype=jnp.int32)[None, :]
    lengths = SEQ - jax.random.randint(key, (IMAGES, 1), 0, SEQ // 2 + 1, dtype=jnp.int32)
    lengths = jnp.where(image_index == 0, SEQ // 2, lengths)
    return (position < lengths).astype(jnp.int32)


def strengthened(values, stream_key, source, target, shards_of, factor):
    def block_of(axis_at):
        return (jnp.arange(values.shape[axis_at]) // (values.shape[axis_at] // shards_of)).reshape((-1,) + (1,) * (values.ndim - 1 - axis_at))

    near = jax.random.permutation(stream_key, shards_of)[block_of(target)]
    other_side = (block_of(target) + shards_of // 2) % shards_of
    return jnp.where((block_of(source) == near) | (block_of(source) == other_side), factor * values, values)


def block_levels(key, shape, cuts, low, top_value):
    def one(dim, blocks):
        draws = jax.random.uniform(jax.random.fold_in(jax.random.fold_in(key, 6), dim), (blocks,), jnp.float32, low / len(cuts), top_value / len(cuts))
        return jnp.repeat(jnp.exp(draws), shape[dim] // blocks).reshape((-1,) + (1,) * (len(shape) - dim - 1))

    loudness = one(*cuts[0])
    for cut in cuts[1:]:
        loudness = loudness * one(*cut)
    return loudness


def scatter_about(stream_key, shape, spread, bound, cuts=(), kind=jnp.bfloat16):
    values = spread * jax.random.normal(stream_key, shape, jnp.float32)
    if cuts:
        values = values * block_levels(stream_key, shape, cuts, -0.22, 0.18)
    return jnp.clip(values, -bound, bound).astype(kind)


def bell_draw_with(stream_key, shape, scale, reach, split, heavy, held_as=jnp.bfloat16):
    drawn = scale * jax.random.normal(stream_key, shape, jnp.float32)
    if split:
        drawn = drawn * block_levels(stream_key, shape, split, -0.22, 0.18)
    return jnp.clip(strengthened(drawn, jax.random.fold_in(stream_key, 3), *heavy), -reach, reach).astype(held_as)


def setup_inputs(seed: int = 0) -> dict:
    seeds = jax.random.split(jax.random.key(seed), 11)
    inputs = draw_inputs(jax.random.fold_in(seeds[10], 71), 0)
    key_mask = draw_key_mask(jax.random.fold_in(seeds[10], 71), 0)
    w_qkv = draw_w_qkv(jax.random.fold_in(seeds[10], 71), 0)
    w_out = scatter_about(seeds[3], (D, D), 8 ** -0.5, 2.0, ((0, 8),))
    w_up = scatter_about(seeds[4], (D, FF), D ** -0.5, 0.1875, ((0, 8),))
    w_down = scatter_about(seeds[5], (FF, D), FF ** -0.5, 0.09375, ((1, 8),))
    norm_gains = jnp.clip(1.0 + 0.18 * jax.random.normal(seeds[6], (2, D), jnp.float32), 0.099609375, 1.8984375).astype(jnp.bfloat16)
    biases = scatter_about(seeds[7], (6, D), 0.5, 3.0, ((1, 8),))
    up_bias = scatter_about(seeds[8], (FF,), 0.5, 3.0, ((0, 8),))
    cotangent = bell_draw_with(seeds[9], (IMAGES, SEQ, D), 1.0, 6.0, ((0, 8), (1, 4)), (0, 2, 8, 2.0))
    return dict(inputs=inputs, key_mask=key_mask, w_qkv=w_qkv, w_out=w_out, w_up=w_up, w_down=w_down, norm_gains=norm_gains, biases=biases, up_bias=up_bias, cotangent=cotangent)


EPSILON = 1e-06
NEG_FILL = -1e+30
GELU_CUBE = 0.044715
GELU_SCALE = math.sqrt(2.0 / math.pi)

def layer_norm(values, gain_row, shift_row):
    row_mean = lax.optimization_barrier(jnp.mean(values, axis=-1, keepdims=True))
    centred = values - row_mean
    variance = lax.optimization_barrier(jnp.mean(centred * centred, axis=-1, keepdims=True))
    inv_std = lax.rsqrt(variance + EPSILON)
    normed = centred * inv_std
    return (normed * gain_row + shift_row, normed, inv_std)

def norm_back(upstream, normed, inv_std, gain_row):
    scaled = upstream * gain_row
    first_mean = lax.optimization_barrier(jnp.mean(scaled, axis=-1, keepdims=True))
    second_mean = lax.optimization_barrier(jnp.mean(scaled * normed, axis=-1, keepdims=True))
    return inv_std * (scaled - first_mean - normed * second_mean)

def gelu_tanh(values):
    return 0.5 * values * (1.0 + jnp.tanh(GELU_SCALE * (values + GELU_CUBE * values * values * values)))

def gelu_slope(values):
    tangent = jnp.tanh(GELU_SCALE * (values + GELU_CUBE * values * values * values))
    return 0.5 * (1.0 + tangent) + 0.5 * values * (1.0 - tangent * tangent) * GELU_SCALE * (1.0 + 3.0 * GELU_CUBE * values * values)

def widen(low_values):
    return lax.optimization_barrier(low_values).astype(jnp.float32)

def reference(inputs, key_mask, w_qkv, w_out, w_up, w_down, norm_gains, biases, up_bias, cotangent):
    score_scale = 1.0 / math.sqrt(HEAD_DIM)
    gain_rows = norm_gains.astype(jnp.float32)
    bias_rows = biases.astype(jnp.float32)
    up_shift = up_bias.astype(jnp.float32)
    qkv_shift = jnp.concatenate([bias_rows[2], jnp.zeros((D,), jnp.float32), bias_rows[3]])

    def one_image(totals, pieces):
        tokens, live, upstream = pieces
        tok_wide = tokens.astype(jnp.float32)
        first_out, first_normed, first_inv = layer_norm(tok_wide, gain_rows[0], bias_rows[0])
        first_low = first_out.astype(jnp.bfloat16)
        packed = (jnp.dot(first_low, w_qkv, preferred_element_type=jnp.float32) + qkv_shift).astype(jnp.bfloat16)
        heads_all = widen(packed).reshape(SEQ, 3, HEADS, HEAD_DIM)
        query = heads_all[:, 0]
        keys_full = heads_all[:, 1]
        values_full = heads_all[:, 2]
        scores = jnp.einsum('qhd,khd->hqk', query, keys_full) * score_scale
        masked = jnp.where(live[None, None, :] > 0, scores, NEG_FILL)
        top_score = lax.optimization_barrier(jnp.max(masked, axis=-1, keepdims=True))
        log_total = top_score + jnp.log(lax.optimization_barrier(jnp.sum(jnp.exp(masked - top_score), axis=-1, keepdims=True)))
        probs = jnp.exp(masked - log_total)
        probs_wide = widen(probs.astype(jnp.bfloat16))
        attended = jnp.einsum('hqk,khd->qhd', probs_wide, values_full).astype(jnp.bfloat16).reshape(SEQ, D)
        residual = tok_wide + jnp.dot(attended, w_out, preferred_element_type=jnp.float32) + bias_rows[4]
        second_out, second_normed, second_inv = layer_norm(residual, gain_rows[1], bias_rows[1])
        second_low = second_out.astype(jnp.bfloat16)
        upper = jnp.dot(second_low, w_up, preferred_element_type=jnp.float32) + up_shift
        active = gelu_tanh(upper).astype(jnp.bfloat16)
        layer_out = (residual + jnp.dot(active, w_down, preferred_element_type=jnp.float32) + bias_rows[5]).astype(jnp.bfloat16)
        grad_wide = upstream.astype(jnp.float32)
        d_active = jnp.dot(upstream, w_down.T, preferred_element_type=jnp.float32)
        dw_down = jnp.dot(active.T, upstream, preferred_element_type=jnp.float32)
        d_upper = (d_active * gelu_slope(upper)).astype(jnp.bfloat16)
        dw_up = jnp.dot(second_low.T, d_upper, preferred_element_type=jnp.float32)
        d_second = jnp.dot(d_upper, w_up.T, preferred_element_type=jnp.float32)
        d_resid = grad_wide + norm_back(d_second, second_normed, second_inv, gain_rows[1])
        d_resid_low = d_resid.astype(jnp.bfloat16)
        dw_out = jnp.dot(attended.T, d_resid_low, preferred_element_type=jnp.float32)
        d_attended = jnp.dot(d_resid_low, w_out.T, preferred_element_type=jnp.float32).astype(jnp.bfloat16)
        d_heads = widen(d_attended).reshape(SEQ, HEADS, HEAD_DIM)
        d_probs = jnp.einsum('qhd,khd->hqk', d_heads, values_full)
        row_dot = lax.optimization_barrier(jnp.sum(probs * d_probs, axis=-1, keepdims=True))
        d_scores = widen((probs * (d_probs - row_dot)).astype(jnp.bfloat16))
        dq_full = jnp.einsum('hqk,khd->qhd', d_scores, keys_full) * score_scale
        dk_full = jnp.einsum('hqk,qhd->khd', d_scores, query) * score_scale
        dv_full = jnp.einsum('hqk,qhd->khd', probs_wide, d_heads)
        d_packed = jnp.concatenate([dq_full.reshape(SEQ, D).astype(jnp.bfloat16), dk_full.reshape(SEQ, D).astype(jnp.bfloat16), dv_full.reshape(SEQ, D).astype(jnp.bfloat16)], axis=1)
        d_pack_wide = d_packed.astype(jnp.float32)
        dw_qkv = jnp.dot(first_low.T, d_packed, preferred_element_type=jnp.float32)
        d_first = jnp.dot(d_packed, w_qkv.T, preferred_element_type=jnp.float32)
        grad_in = (d_resid + norm_back(d_first, first_normed, first_inv, gain_rows[0])).astype(jnp.bfloat16)
        d_gains = jnp.stack([lax.optimization_barrier(jnp.sum(d_first * first_normed, axis=0)), lax.optimization_barrier(jnp.sum(d_second * second_normed, axis=0))])
        d_biases = jnp.stack([lax.optimization_barrier(jnp.sum(d_first, axis=0)), lax.optimization_barrier(jnp.sum(d_second, axis=0)), lax.optimization_barrier(jnp.sum(d_pack_wide[:, :D], axis=0)), lax.optimization_barrier(jnp.sum(d_pack_wide[:, 2 * D:], axis=0)), lax.optimization_barrier(jnp.sum(d_resid, axis=0)), lax.optimization_barrier(jnp.sum(grad_wide, axis=0))])
        d_upbias = lax.optimization_barrier(jnp.sum(d_upper.astype(jnp.float32), axis=0))
        new_totals = (totals[0] + dw_qkv, totals[1] + dw_out, totals[2] + dw_up, totals[3] + dw_down, totals[4] + d_gains, totals[5] + d_biases, totals[6] + d_upbias)
        return (new_totals, (layer_out, grad_in))
    start_totals = (jnp.zeros((D, 3 * D), jnp.float32), jnp.zeros((D, D), jnp.float32), jnp.zeros((D, FF), jnp.float32), jnp.zeros((FF, D), jnp.float32), jnp.zeros((2, D), jnp.float32), jnp.zeros((6, D), jnp.float32), jnp.zeros((FF,), jnp.float32))
    totals, outputs = lax.scan(one_image, start_totals, (inputs, key_mask, cotangent))
    return (outputs[0], outputs[1], totals[0], totals[1], totals[2], totals[3], totals[4], totals[5], totals[6])
```

```python
import functools
import math

import jax
import jax.numpy as jnp
from jax import lax
from jax.experimental import pallas as pl
from jax.experimental.pallas import tpu as pltpu
from jax.sharding import PartitionSpec as P

HEAD_DIM = 72
QBLOCK = 512
EPSILON = 1e-06
NEG_FILL = -1e30
GELU_CUBE = 0.044715
GELU_SCALE = math.sqrt(2.0 / math.pi)
LOG2E = math.log2(math.e)
LANES = 128
F32 = jnp.float32
BF16 = jnp.bfloat16
MIB = 2**20


def attention_forward_kernel(block, heads, qkv_ref, bias_ref, out_ref, probs_ref, inv_ref, by_row, out_rows):
    head = pl.program_id(0)
    width = heads * HEAD_DIM
    seq = qkv_ref.shape[0]

    @pl.when(head == 0)
    def _():
        by_row[...] = qkv_ref[...].astype(F32).T

    def rows(which):
        return pl.ds(pl.multiple_of(which * width + head * HEAD_DIM, 8), HEAD_DIM)

    query = by_row[rows(0), :].astype(BF16)
    keys = by_row[rows(1), :].T.astype(BF16)
    values = by_row[rows(2), :].astype(BF16)
    bias = bias_ref[...]
    for start in range(0, seq, block):
        part = slice(start, start + block)
        scores = jnp.dot(keys, query[:, part], preferred_element_type=F32) * (LOG2E / math.sqrt(HEAD_DIM)) + bias
        top = jnp.max(scores, axis=0, keepdims=True)
        raised = jnp.exp2(scores - top)
        inv = 1.0 / jnp.sum(raised, axis=0, keepdims=True)
        raised_low = raised.astype(BF16)
        probs_ref[0, :, part] = raised_low
        inv_ref[0, :, part] = inv
        out_rows[rows(0), part] = jnp.dot(values, raised_low, preferred_element_type=F32) * inv

    @pl.when(head == heads - 1)
    def _():
        out_ref[...] = out_rows[...].T.astype(BF16)


def attention_forward(qkv, bias, block=QBLOCK):
    seq, triple = qkv.shape
    width = triple // 3
    heads = width // HEAD_DIM
    return pl.pallas_call(
        functools.partial(attention_forward_kernel, block, heads),
        grid=(heads,),
        in_specs=[pl.BlockSpec((seq, triple), lambda h: (0, 0)), pl.BlockSpec((seq, 1), lambda h: (0, 0))],
        out_specs=[
            pl.BlockSpec((seq, width), lambda h: (0, 0)),
            pl.BlockSpec((1, seq, seq), lambda h: (h, 0, 0)),
            pl.BlockSpec((1, 1, seq), lambda h: (h, 0, 0)),
        ],
        out_shape=[
            jax.ShapeDtypeStruct((seq, width), BF16),
            jax.ShapeDtypeStruct((heads, seq, seq), BF16),
            jax.ShapeDtypeStruct((heads, 1, seq), F32),
        ],
        scratch_shapes=[pltpu.VMEM((triple, seq), F32), pltpu.VMEM((width, seq), F32)],
        compiler_params=pltpu.CompilerParams(vmem_limit_bytes=48 * MIB),
        cost_estimate=pl.CostEstimate(
            flops=10 * heads * seq * seq * 256, bytes_accessed=2 * heads * seq * seq, transcendentals=heads * seq * seq
        ),
    )(qkv, bias)


def attention_backward_kernel(
    block, heads, qkv_ref, d_out_ref, out_ref, probs_ref, inv_ref, grad_ref, by_row, d_rows, o_rows, grad_rows
):
    head = pl.program_id(0)
    width = heads * HEAD_DIM
    seq = qkv_ref.shape[0]
    scale = 1.0 / math.sqrt(HEAD_DIM)

    @pl.when(head == 0)
    def _():
        by_row[...] = qkv_ref[...].astype(F32).T
        d_rows[...] = d_out_ref[...].astype(F32).T
        o_rows[...] = out_ref[...].astype(F32).T

    def rows(which):
        return pl.ds(pl.multiple_of(which * width + head * HEAD_DIM, 8), HEAD_DIM)

    query = by_row[rows(0), :].T.astype(BF16)
    keys = by_row[rows(1), :].astype(BF16)
    values = by_row[rows(2), :].T.astype(BF16)
    d_out = d_rows[rows(0), :]
    inv = inv_ref[0]
    row_dot = jnp.sum(d_out * o_rows[rows(0), :], axis=0, keepdims=True) * inv
    d_scaled = d_out * inv
    d_tokens = d_scaled.T.astype(BF16)
    d_scaled = d_scaled.astype(BF16)
    d_keys = jnp.zeros((seq, HEAD_DIM), F32)
    d_values = jnp.zeros((seq, HEAD_DIM), F32)
    for start in range(0, seq, block):
        part = slice(start, start + block)
        raised = probs_ref[0, :, part]
        d_probs = jnp.dot(values, d_scaled[:, part], preferred_element_type=F32)
        d_scores = (raised.astype(F32) * (d_probs - row_dot[:, part])).astype(BF16)
        d_values += jnp.dot(raised, d_tokens[part, :], preferred_element_type=F32)
        d_keys += jnp.dot(d_scores, query[part, :], preferred_element_type=F32)
        grad_rows[rows(0), part] = jnp.dot(keys, d_scores, preferred_element_type=F32) * scale
    grad_rows[rows(1), :] = d_keys.T * scale
    grad_rows[rows(2), :] = d_values.T

    @pl.when(head == heads - 1)
    def _():
        grad_ref[...] = grad_rows[...].T.astype(BF16)


def attention_backward(qkv, d_out, out, probs, inv, block=QBLOCK):
    seq, triple = qkv.shape
    width = triple // 3
    heads = width // HEAD_DIM
    whole = lambda h: (0, 0)
    return pl.pallas_call(
        functools.partial(attention_backward_kernel, block, heads),
        grid=(heads,),
        in_specs=[
            pl.BlockSpec((seq, triple), whole),
            pl.BlockSpec((seq, width), whole),
            pl.BlockSpec((seq, width), whole),
            pl.BlockSpec((1, seq, seq), lambda h: (h, 0, 0)),
            pl.BlockSpec((1, 1, seq), lambda h: (h, 0, 0)),
        ],
        out_specs=pl.BlockSpec((seq, triple), whole),
        out_shape=jax.ShapeDtypeStruct((seq, triple), BF16),
        scratch_shapes=[
            pltpu.VMEM((triple, seq), F32),
            pltpu.VMEM((width, seq), F32),
            pltpu.VMEM((width, seq), F32),
            pltpu.VMEM((triple, seq), F32),
        ],
        compiler_params=pltpu.CompilerParams(vmem_limit_bytes=56 * MIB),
        cost_estimate=pl.CostEstimate(
            flops=12 * heads * seq * seq * 256, bytes_accessed=2 * heads * seq * seq, transcendentals=0
        ),
    )(qkv, d_out, out, probs, inv)


class Place:
    def __init__(self):
        self.planes = lax.axis_size("fsdp") // 2
        f = lax.axis_index("fsdp")
        k = lax.axis_index("seq")
        self.z, self.c = f // 2, f % 2
        self.k, self.y, self.x = k, k // 2, k % 2

    def send(self, value, to):
        pairs = []
        for z in range(self.planes):
            for c in range(2):
                for y in range(2):
                    for x in range(2):
                        tz, tc, ty, tx = to(z, c, y, x)
                        pairs.append((((z * 2 + c) * 2 + y) * 2 + x, ((tz * 2 + tc) * 2 + ty) * 2 + tx))
        return lax.ppermute(value, ("fsdp", "seq"), pairs)

    def core(self, value):
        return self.send(value, lambda z, c, y, x: (z, 1 - c, y, x))

    def along_x(self, value):
        return self.send(value, lambda z, c, y, x: (z, c, y, 1 - x))

    def along_y(self, value):
        return self.send(value, lambda z, c, y, x: (z, c, 1 - y, x))

    def across(self, value):
        return self.send(value, lambda z, c, y, x: (z, c, 1 - y, 1 - x))

    def along_z(self, value, step):
        return self.send(value, lambda z, c, y, x: (z ^ step, c, y, x))

    def turn(self, value, step):
        return self.send(value, lambda z, c, y, x: (z, y, c, x ^ step))


def after(value, *others):
    return lax.optimization_barrier((value, *others))[0]


def pick(stack, index):
    return lax.dynamic_index_in_dim(stack, index, 0, keepdims=False)


def in_order(flag, mine, other):
    return jnp.where(flag == 0, jnp.concatenate([mine, other]), jnp.concatenate([other, mine]))


def to_image(place, parts):
    near = place.turn(pick(parts, place.x), 0)
    far = place.turn(pick(parts, 1 - place.x), 1)
    return in_order(place.x, near, far)


def from_image(place, half):
    parts = half.reshape(2, half.shape[0] // 2, half.shape[1])
    near = place.turn(pick(parts, place.x), 0)
    far = place.turn(pick(parts, 1 - place.x), 1)
    return in_order(place.x, near[None], far[None])


def both_halves(place, half):
    return in_order(place.c, half, place.core(half))


def lane_cut(columns):
    return columns // 2 // LANES * LANES


def spread(place, give, keep):
    block = in_order(place.c, keep, place.core(give))
    rows, columns = block.shape[0] // 4, block.shape[1]
    quarters = block.reshape(4, rows, columns)
    mine = pick(quarters, place.k)
    own = jnp.stack([place.along_z(mine, step) for step in range(1, place.planes)])
    cut = lane_cut(columns)
    x_part = place.along_x(own)
    y_part = place.along_y(own)
    far_low = place.along_x(y_part[:, :, :cut])
    far_high = place.along_y(x_part[:, :, cut:])
    return assemble(place, quarters, own, x_part, y_part, far_low, far_high), own


def assemble_kernel(planes, cut, scalars, block, own, x_part, y_part, far_low, far_high, out, sems):
    z, k = scalars[0], scalars[1]
    copies = [(block, out.at[pl.ds(z * 4, 4)])]
    for step in range(1, planes):
        at = (z ^ step) * 4
        copies.append((own.at[step - 1], out.at[at + k]))
        copies.append((x_part.at[step - 1], out.at[at + (k ^ 1)]))
        copies.append((y_part.at[step - 1], out.at[at + (k ^ 2)]))
        copies.append((far_low.at[step - 1], out.at[at + (k ^ 3), :, pl.ds(0, cut)]))
        copies.append((far_high.at[step - 1], out.at[at + (k ^ 3), :, pl.ds(cut, out.shape[2] - cut)]))
    started = [pltpu.make_async_copy(source, target, sems.at[i]) for i, (source, target) in enumerate(copies)]
    for copy in started:
        copy.start()
    for copy in started:
        copy.wait()


def assemble(place, block, own, x_part, y_part, far_low, far_high):
    rows, columns = block.shape[1:]
    planes = place.planes
    anywhere = pl.BlockSpec(memory_space=pl.ANY)
    out = pl.pallas_call(
        functools.partial(assemble_kernel, planes, lane_cut(columns)),
        in_specs=[pl.BlockSpec(memory_space=pltpu.SMEM)] + [anywhere] * 6,
        out_specs=pl.BlockSpec(memory_space=pltpu.VMEM),
        out_shape=jax.ShapeDtypeStruct((planes * 4, rows, columns), block.dtype),
        scratch_shapes=[pltpu.SemaphoreType.DMA((1 + 5 * (planes - 1),))],
        compiler_params=pltpu.CompilerParams(vmem_limit_bytes=32 * MIB),
        cost_estimate=pl.CostEstimate(
            flops=0, bytes_accessed=4 * planes * 4 * rows * columns, transcendentals=0
        ),
    )(jnp.stack([place.z, place.k]).astype(jnp.int32), block, own, x_part, y_part, far_low, far_high)
    return out.reshape(planes * 4 * rows, columns)


def collect(place, partial):
    planes = place.planes
    columns = partial.shape[1]
    rows = partial.shape[0] // planes // 4
    cut = lane_cut(columns)
    parts = partial.reshape(planes, 2, 2, rows, columns)
    low, high = parts[..., :cut], parts[..., cut:]

    def take(value, axis, index):
        return lax.dynamic_index_in_dim(value, index, axis, keepdims=False)

    def add(mine, arrived):
        return (mine.astype(F32) + arrived.astype(F32)).astype(BF16)

    low = add(take(low, 2, place.x), place.along_x(take(low, 2, 1 - place.x)))
    high = add(take(high, 1, place.y), place.along_y(take(high, 1, 1 - place.y)))
    low = add(take(low, 1, place.y), place.along_y(take(low, 1, 1 - place.y)))
    high = add(take(high, 1, place.x), place.along_x(take(high, 1, 1 - place.x)))
    plane = jnp.concatenate([low, high], axis=-1)
    total = pick(plane, place.z).astype(F32)
    for step in range(1, planes):
        total = total + place.along_z(pick(plane, place.z ^ step), step).astype(F32)
    mine = total.astype(BF16)
    x_part = place.along_x(mine)
    y_part = place.along_y(mine)
    far = jnp.concatenate([place.along_x(y_part[:, :cut]), place.along_y(x_part[:, cut:])], axis=-1)
    near_pair = in_order(place.x, mine, x_part)
    far_pair = in_order(place.x, y_part, far)
    matches = place.y == place.c
    keep = jnp.where(matches, near_pair, far_pair)
    give = jnp.where(matches, far_pair, near_pair)
    return keep, place.core(give)


def sum_chips(place, value):
    value = value + place.along_x(value) + place.along_y(value) + place.across(value)
    total = value
    for step in range(1, place.planes):
        total = total + place.along_z(value, step)
    return total


def own_columns(place, rows_of_columns):
    n, width = rows_of_columns.shape
    size = width // lax.axis_size("fsdp")
    return lax.dynamic_slice_in_dim(rows_of_columns, lax.axis_index("fsdp") * size, size, axis=1)


def norm_stats(values):
    row_mean = jnp.mean(values, axis=-1, keepdims=True)
    centred = values - row_mean
    variance = jnp.mean(centred * centred, axis=-1, keepdims=True)
    return row_mean, lax.rsqrt(variance + EPSILON)


def layer_norm(values, gain_row, shift_row):
    row_mean = jnp.mean(values, axis=-1, keepdims=True)
    centred = values - row_mean
    variance = jnp.mean(centred * centred, axis=-1, keepdims=True)
    inv_std = lax.rsqrt(variance + EPSILON)
    normed = centred * inv_std
    return (normed * gain_row + shift_row, normed, inv_std)


def norm_back(upstream, normed, inv_std, gain_row):
    scaled = upstream * gain_row
    first_mean = jnp.mean(scaled, axis=-1, keepdims=True)
    second_mean = jnp.mean(scaled * normed, axis=-1, keepdims=True)
    return inv_std * (scaled - first_mean - normed * second_mean)


def gelu_and_slope(values):
    square = values * values
    tangent = jnp.tanh(GELU_SCALE * values * (1.0 + GELU_CUBE * square))
    half = 0.5 * (1.0 + tangent)
    slope = half + 0.5 * values * (1.0 - tangent * tangent) * GELU_SCALE * (1.0 + 3.0 * GELU_CUBE * square)
    return values * half, slope


def dot(a, b):
    return jnp.dot(a, b, preferred_element_type=F32)


def dot_t(a, b):
    return lax.dot_general(a, b, (((1,), (1,)), ((), ())), preferred_element_type=F32)


def t_dot(a, b):
    return lax.dot_general(a, b, (((0,), (0,)), ((), ())), preferred_element_type=F32)


def image_on_chip(inputs, key_mask, w_qkv, w_out, w_up, w_down, norm_gains, biases, up_bias, cotangent):
    place = Place()
    img_count, tok_count, width = inputs.shape
    shard = w_qkv.shape[0]
    fsdp = lax.axis_size("fsdp")
    half_width = width // 2
    hidden = w_up.shape[1]
    half_hidden = -(-hidden // 2 // LANES) * LANES
    up_shard = up_bias.shape[0]
    up_cols = -(-up_shard // shard)

    def halves_qkv(w):
        return jnp.moveaxis(w.reshape(w.shape[0], 3, 2, half_width), 2, 0).reshape(2, w.shape[0], 3 * half_width)

    def halves_hidden(w):
        padded = jnp.pad(w, ((0, 0), (0, 2 * half_hidden - hidden)))
        return jnp.stack([padded[:, :half_hidden], padded[:, half_hidden:]])

    small = jnp.concatenate(
        [
            norm_gains,
            biases,
            jnp.pad(up_bias, (0, up_cols * shard - up_shard)).reshape(up_cols, shard),
        ]
    )
    n_small = small.shape[0]
    spare = -(3 * half_width) % LANES
    extra = jnp.pad(small.T, ((0, 0), (0, spare - n_small)))
    qkv_halves = halves_qkv(w_qkv)
    give = jnp.concatenate([pick(qkv_halves, 1 - place.c), extra], axis=1)
    keep = jnp.concatenate([pick(qkv_halves, place.c), extra], axis=1)

    tokens = both_halves(place, to_image(place, inputs))
    full_first, own_first = spread(place, give, keep)
    full_qkv = full_first[:, : 3 * half_width]
    small_rows = full_first[:, 3 * half_width : 3 * half_width + n_small].astype(F32).T
    gain_rows, bias_rows = small_rows[:2], small_rows[2:8]
    up_shift = (
        small_rows[8:].reshape(up_cols, fsdp, shard).transpose(1, 0, 2).reshape(fsdp, up_cols * shard)[:, :up_shard]
    ).reshape(hidden)
    up_shift = pick(jnp.pad(up_shift, (0, 2 * half_hidden - hidden)).reshape(2, half_hidden), place.c)

    out_halves = jnp.moveaxis(w_out.reshape(shard, 2, half_width), 1, 0)
    up_halves = halves_hidden(w_up)
    down_halves = halves_hidden(w_down.T)
    out_up = jnp.concatenate([up_halves, jnp.pad(out_halves, ((0, 0), (0, 0), (0, -half_width % LANES)))], axis=2)
    out_up = after(out_up, own_first)
    full_out_up, own_out_up = spread(place, pick(out_up, 1 - place.c), pick(out_up, place.c))
    full_up = full_out_up[:, :half_hidden]
    half_out = full_out_up[:, half_hidden : half_hidden + half_width]
    other_out = place.core(half_out)
    full_out = jnp.where(
        place.c == 0,
        jnp.concatenate([half_out, other_out], axis=1),
        jnp.concatenate([other_out, half_out], axis=1),
    )
    down_halves = after(down_halves, own_out_up)
    full_down, _ = spread(place, pick(down_halves, 1 - place.c), pick(down_halves, place.c))
    upstream = both_halves(place, to_image(place, after(cotangent, full_first)))

    other_mask = place.core(key_mask)
    live = pick(jnp.where(place.c == place.y, key_mask, other_mask), place.x)
    mask_bias = jnp.where(live > 0, 0.0, NEG_FILL).astype(F32)[:, None]

    shift_halves = bias_rows.reshape(6, 2, half_width)
    qkv_shift = jnp.concatenate(
        [pick(shift_halves[2], place.c), jnp.zeros((half_width,), F32), pick(shift_halves[3], place.c)]
    )
    tok_wide = tokens.astype(F32)
    first_out, first_normed, first_inv = layer_norm(tok_wide, gain_rows[0], bias_rows[0])
    first_low = first_out.astype(BF16)
    packed = (dot(first_low, full_qkv) + qkv_shift).astype(BF16)
    attended_half, raised, inv_total = attention_forward(packed, mask_bias)
    other_half = place.core(attended_half)
    attended = jnp.where(
        place.c == 0,
        jnp.concatenate([attended_half, other_half], axis=1),
        jnp.concatenate([other_half, attended_half], axis=1),
    )
    residual = tok_wide + dot(attended, full_out) + bias_rows[4]
    second_out, second_normed, second_inv = layer_norm(residual, gain_rows[1], bias_rows[1])
    second_low = second_out.astype(BF16)
    upper = dot(second_low, full_up) + up_shift
    active, slope = gelu_and_slope(upper)
    active = active.astype(BF16)
    slope = slope.astype(BF16)

    def own_half(value):
        return pick(value.reshape(2, value.shape[0] // 2, value.shape[1]), place.c)

    def other_half_of(value):
        return pick(value.reshape(2, value.shape[0] // 2, value.shape[1]), 1 - place.c)

    down_part = dot_t(active, full_down)
    down_sum = own_half(down_part) + place.core(other_half_of(down_part).astype(BF16)).astype(F32)
    layer_half = (own_half(residual) + down_sum + bias_rows[5]).astype(BF16)
    layer_out = from_image(place, layer_half)

    grad_wide = upstream.astype(F32)
    d_active = dot(upstream, full_down)
    d_upper = (d_active * slope.astype(F32)).astype(BF16)
    dw_down = t_dot(upstream, active).astype(BF16)
    down_sums = collect(place, dw_down)
    d_second_part = dot_t(d_upper, full_up)
    d_second = d_second_part + place.core(d_second_part.astype(BF16)).astype(F32)
    dw_up = t_dot(second_low, d_upper).astype(BF16)
    up_sums = collect(place, dw_up)
    d_resid = grad_wide + norm_back(d_second, second_normed, second_inv, gain_rows[1])
    d_resid_low = d_resid.astype(BF16)
    d_attended = dot_t(d_resid_low, pick(full_out.reshape(2, half_width, width), place.c)).astype(BF16)
    d_packed = attention_backward(packed, d_attended, attended_half, raised, inv_total)
    dw_out = t_dot(
        attended, jnp.where(place.c == 0, d_resid_low[:, :half_width], d_resid_low[:, half_width:])
    ).astype(BF16)
    by_hidden = jnp.sum(d_upper.astype(F32), axis=0)
    by_hidden = jnp.where(
        place.c == 0,
        jnp.pad(by_hidden, (0, half_hidden)),
        jnp.pad(by_hidden, (half_hidden, 0)),
    )[:hidden].reshape(fsdp, up_shard)
    by_hidden = jnp.pad(by_hidden, ((0, 0), (0, up_cols * shard - up_shard))).reshape(fsdp, up_cols, shard)
    by_hidden = by_hidden.transpose(1, 0, 2).reshape(up_cols, width)
    by_width = jnp.stack(
        [
            jnp.sum(d_second * second_normed, axis=0),
            jnp.sum(d_second, axis=0),
            jnp.sum(d_resid, axis=0),
            jnp.sum(grad_wide, axis=0),
        ]
    )
    by_width = jnp.where(place.c == 0, by_width, 0.0)
    riders = jnp.concatenate([by_width, by_hidden])
    riders = jnp.pad(riders, ((0, -half_width % LANES - riders.shape[0]), (0, 0))).T.astype(BF16)
    out_sums = collect(place, jnp.concatenate([dw_out, riders], axis=1))
    rider_sums = (out_sums[0][:, half_width:].astype(F32) + out_sums[1][:, half_width:].astype(F32)).T
    out_sums = [part[:, :half_width] for part in out_sums]
    second_sums = rider_sums[:4]
    grad_upbias = rider_sums[4 : 4 + up_cols].reshape(up_cols * shard)[:up_shard]
    dw_qkv = t_dot(first_low, d_packed).astype(BF16)
    qkv_sums = collect(place, dw_qkv)
    d_first_part = dot_t(d_packed, full_qkv)
    d_first = own_half(d_first_part) + place.core(other_half_of(d_first_part).astype(BF16)).astype(F32)
    normed_half = own_half(first_normed)
    grad_half = (
        own_half(d_resid) + norm_back(d_first, normed_half, own_half(first_inv), gain_rows[0])
    ).astype(BF16)
    grad_in = from_image(place, grad_half)

    pack_wide = d_packed.astype(F32)
    q_sum = jnp.sum(pack_wide[:, :half_width], axis=0)
    v_sum = jnp.sum(pack_wide[:, 2 * half_width :], axis=0)
    late = jnp.concatenate([jnp.sum(d_first * normed_half, axis=0), jnp.sum(d_first, axis=0), q_sum, v_sum])
    late = sum_chips(place, late.reshape(-1, LANES)).reshape(-1)
    late_other = place.core(late)
    first_sums = (late[: 2 * width] + late_other[: 2 * width]).reshape(2, width)
    qv_mine = late[2 * width :].reshape(2, 1, half_width)
    qv_other = late_other[2 * width :].reshape(2, 1, half_width)
    qv_sums = jnp.where(
        place.c == 0, jnp.concatenate([qv_mine, qv_other], axis=1), jnp.concatenate([qv_other, qv_mine], axis=1)
    ).reshape(2, width)
    first_own = own_columns(place, first_sums)
    qv_own = own_columns(place, qv_sums)
    grad_gains = jnp.stack([first_own[0], second_sums[0]])
    grad_biases = jnp.stack([first_own[1], second_sums[1], qv_own[0], qv_own[1], second_sums[2], second_sums[3]])

    def side_by_side(sums):
        mine, other = (part.astype(F32) for part in sums)
        return jnp.where(place.c == 0, mine, other), jnp.where(place.c == 0, other, mine)

    lower, higher = side_by_side(qkv_sums)
    grad_qkv = jnp.stack([lower.reshape(shard, 3, half_width), higher.reshape(shard, 3, half_width)], axis=2)
    grad_qkv = grad_qkv.reshape(shard, 3 * width)
    grad_proj = jnp.concatenate(side_by_side(out_sums), axis=1)
    grad_up = jnp.concatenate(side_by_side(up_sums), axis=1)[:, :hidden]
    grad_down = jnp.concatenate(side_by_side(down_sums), axis=1)[:, :hidden].T
    return (
        layer_out,
        grad_in,
        grad_qkv,
        grad_proj,
        grad_up,
        grad_down,
        grad_gains,
        grad_biases,
        grad_upbias,
    )


def for_sending(array):
    return jax.tree.map(lambda a: a.astype(jnp.bfloat16) if a.dtype == jnp.float32 else a, array)


def gelu_tanh(values):
    return (
        0.5
        * values
        * (1.0 + jnp.tanh(GELU_SCALE * (values + GELU_CUBE * values * values * values)))
    )


def gelu_slope(values):
    tangent = jnp.tanh(GELU_SCALE * (values + GELU_CUBE * values * values * values))
    return 0.5 * (1.0 + tangent) + 0.5 * values * (1.0 - tangent * tangent) * GELU_SCALE * (
        1.0 + 3.0 * GELU_CUBE * values * values
    )


def block_scores(q_block, keys_full, live, score_scale):
    scores = (
        jnp.einsum("qhd,khd->hqk", q_block, keys_full, preferred_element_type=jnp.float32)
        * score_scale
    )
    return jnp.where(live[None, None, :] > 0, scores, NEG_FILL)


def forward_image(pieces, block_rows, score_scale):
    query, keys_full, values_full, live = pieces
    out_parts = []
    total_parts = []
    for start in range(0, query.shape[0], block_rows):
        masked = block_scores(query[start : start + block_rows], keys_full, live, score_scale)
        top_score = jnp.max(masked, axis=-1, keepdims=True)
        log_total = top_score + jnp.log(
            jnp.sum(jnp.exp(masked - top_score), axis=-1, keepdims=True)
        )
        probs_low = jnp.exp(masked - log_total).astype(jnp.bfloat16)
        out_parts.append(
            jnp.einsum(
                "hqk,khd->qhd", probs_low, values_full, preferred_element_type=jnp.float32
            ).astype(jnp.bfloat16)
        )
        total_parts.append(log_total)
    return (jnp.concatenate(out_parts, axis=0), jnp.concatenate(total_parts, axis=1))


def backward_image(pieces, block_rows, score_scale):
    query, keys_full, values_full, live, log_totals, d_heads = pieces
    dq_parts = []
    dk_total = jnp.zeros(keys_full.shape, jnp.float32)
    dv_total = jnp.zeros(values_full.shape, jnp.float32)
    for start in range(0, query.shape[0], block_rows):
        q_block = query[start : start + block_rows]
        d_block = d_heads[start : start + block_rows]
        masked = block_scores(q_block, keys_full, live, score_scale)
        probs = jnp.exp(masked - log_totals[:, start : start + block_rows])
        probs_low = probs.astype(jnp.bfloat16)
        d_probs = jnp.einsum(
            "qhd,khd->hqk", d_block, values_full, preferred_element_type=jnp.float32
        )
        row_dot = jnp.sum(probs * d_probs, axis=-1, keepdims=True)
        d_scores = (probs * (d_probs - row_dot)).astype(jnp.bfloat16)
        dq_block = (
            jnp.einsum("hqk,khd->qhd", d_scores, keys_full, preferred_element_type=jnp.float32)
            * score_scale
        )
        dq_parts.append(dq_block.astype(jnp.bfloat16))
        dk_total = dk_total + jnp.einsum(
            "hqk,qhd->khd", d_scores, q_block, preferred_element_type=jnp.float32
        )
        dv_total = dv_total + jnp.einsum(
            "hqk,qhd->khd", probs_low, d_block, preferred_element_type=jnp.float32
        )
    return (
        jnp.concatenate(dq_parts, axis=0),
        (dk_total * score_scale).astype(jnp.bfloat16),
        dv_total.astype(jnp.bfloat16),
    )


def heads_over_seq(inputs, key_mask, w_qkv, w_out, w_up, w_down, norm_gains, biases, up_bias, cotangent):
    img_count, tok_count, width = inputs.shape
    seq_len = key_mask.shape[1]
    row_count = img_count * tok_count
    head_cols = width // lax.axis_size("seq")
    local_heads = head_cols // HEAD_DIM
    block_rows = min(QBLOCK, seq_len)
    score_scale = 1.0 / math.sqrt(HEAD_DIM)
    gathered = (
        lax.all_gather(w_qkv, "fsdp", axis=0, tiled=True),
        lax.all_gather(w_out, "fsdp", axis=0, tiled=True),
        lax.all_gather(w_up, "fsdp", axis=0, tiled=True),
        lax.all_gather(w_down, "fsdp", axis=1, tiled=True),
        lax.all_gather(norm_gains, "fsdp", axis=1, tiled=True),
        lax.all_gather(biases, "fsdp", axis=1, tiled=True),
        lax.all_gather(up_bias, "fsdp", axis=0, tiled=True),
    )
    full_qkv, full_out, full_up, full_down, full_gains, full_biases, full_upbias = gathered
    gain_rows = full_gains.astype(jnp.float32)
    bias_rows = full_biases.astype(jnp.float32)
    up_shift = full_upbias.astype(jnp.float32)
    qkv_shift = jnp.concatenate([bias_rows[2], jnp.zeros((width,), jnp.float32), bias_rows[3]])
    tok_wide = inputs.reshape(row_count, width).astype(jnp.float32)
    first_out, first_normed, first_inv = layer_norm(tok_wide, gain_rows[0], bias_rows[0])
    first_low = first_out.astype(jnp.bfloat16)
    packed = (jnp.dot(first_low, full_qkv, preferred_element_type=jnp.float32) + qkv_shift).astype(
        jnp.bfloat16
    )
    by_heads = lax.all_to_all(
        packed.reshape(img_count, tok_count, 3, width),
        "seq",
        split_axis=3,
        concat_axis=1,
        tiled=True,
    )
    query = by_heads[:, :, 0].reshape(img_count, seq_len, local_heads, HEAD_DIM)
    keys_full = by_heads[:, :, 1].reshape(img_count, seq_len, local_heads, HEAD_DIM)
    values_full = by_heads[:, :, 2].reshape(img_count, seq_len, local_heads, HEAD_DIM)

    def run_forward(pieces):
        return forward_image(pieces, block_rows, score_scale)

    attended_heads, log_totals = lax.map(run_forward, (query, keys_full, values_full, key_mask))
    attended = lax.all_to_all(
        for_sending(attended_heads.reshape(img_count, seq_len, head_cols)),
        "seq",
        split_axis=1,
        concat_axis=2,
        tiled=True,
    ).reshape(row_count, width)
    residual = (
        tok_wide + jnp.dot(attended, full_out, preferred_element_type=jnp.float32) + bias_rows[4]
    )
    second_out, second_normed, second_inv = layer_norm(residual, gain_rows[1], bias_rows[1])
    second_low = second_out.astype(jnp.bfloat16)
    upper = jnp.dot(second_low, full_up, preferred_element_type=jnp.float32) + up_shift
    active = gelu_tanh(upper).astype(jnp.bfloat16)
    layer_out = (
        residual + jnp.dot(active, full_down, preferred_element_type=jnp.float32) + bias_rows[5]
    ).astype(jnp.bfloat16)
    back_qkv, back_out, back_up, back_down, back_gains, back_biases, back_upbias = gathered
    back_gain_rows = back_gains.astype(jnp.float32)
    upstream = cotangent.reshape(row_count, width)
    grad_wide = upstream.astype(jnp.float32)
    d_active = jnp.dot(upstream, back_down.T, preferred_element_type=jnp.float32)
    dw_down = jnp.dot(active.T, upstream, preferred_element_type=jnp.float32)
    d_upper = (d_active * gelu_slope(upper)).astype(jnp.bfloat16)
    dw_up = jnp.dot(second_low.T, d_upper, preferred_element_type=jnp.float32)
    d_second = jnp.dot(d_upper, back_up.T, preferred_element_type=jnp.float32)
    d_resid = grad_wide + norm_back(d_second, second_normed, second_inv, back_gain_rows[1])
    d_resid_low = d_resid.astype(jnp.bfloat16)
    dw_out = jnp.dot(attended.T, d_resid_low, preferred_element_type=jnp.float32)
    d_attended = jnp.dot(d_resid_low, back_out.T, preferred_element_type=jnp.float32).astype(
        jnp.bfloat16
    )
    d_heads = lax.all_to_all(
        d_attended.reshape(img_count, tok_count, width),
        "seq",
        split_axis=2,
        concat_axis=1,
        tiled=True,
    ).reshape(img_count, seq_len, local_heads, HEAD_DIM)

    def run_backward(pieces):
        return backward_image(pieces, block_rows, score_scale)

    dq_heads, dk_heads, dv_heads = lax.map(
        run_backward, (query, keys_full, values_full, key_mask, log_totals, d_heads)
    )
    stacked = jnp.stack(
        [
            dq_heads.reshape(img_count, seq_len, head_cols),
            dk_heads.reshape(img_count, seq_len, head_cols),
            dv_heads.reshape(img_count, seq_len, head_cols),
        ],
        axis=2,
    )
    d_packed = (
        lax.all_to_all(for_sending(stacked), "seq", split_axis=1, concat_axis=3, tiled=True)
        .astype(stacked.dtype)
        .reshape(row_count, 3 * width)
    )
    d_pack_wide = d_packed.astype(jnp.float32)
    dw_qkv = jnp.dot(first_low.T, d_packed, preferred_element_type=jnp.float32)
    d_first = jnp.dot(d_packed, back_qkv.T, preferred_element_type=jnp.float32)
    grad_in = (d_resid + norm_back(d_first, first_normed, first_inv, back_gain_rows[0])).astype(
        jnp.bfloat16
    )
    d_gains = jnp.stack(
        [jnp.sum(d_first * first_normed, axis=0), jnp.sum(d_second * second_normed, axis=0)]
    )
    d_biases = jnp.stack(
        [
            jnp.sum(d_first, axis=0),
            jnp.sum(d_second, axis=0),
            jnp.sum(d_pack_wide[:, :width], axis=0),
            jnp.sum(d_pack_wide[:, 2 * width :], axis=0),
            jnp.sum(d_resid, axis=0),
            jnp.sum(grad_wide, axis=0),
        ]
    )
    d_upbias = jnp.sum(d_upper.astype(jnp.float32), axis=0)
    owned = (
        lax.psum_scatter(dw_qkv, "fsdp", scatter_dimension=0, tiled=True),
        lax.psum_scatter(dw_out, "fsdp", scatter_dimension=0, tiled=True),
        lax.psum_scatter(dw_up, "fsdp", scatter_dimension=0, tiled=True),
        lax.psum_scatter(dw_down, "fsdp", scatter_dimension=1, tiled=True),
        lax.psum_scatter(d_gains, "fsdp", scatter_dimension=1, tiled=True),
        lax.psum_scatter(d_biases, "fsdp", scatter_dimension=1, tiled=True),
        lax.psum_scatter(d_upbias, "fsdp", scatter_dimension=0, tiled=True),
    )
    summed = lax.psum((owned[0], owned[1], owned[2], owned[3], owned[4], owned[5], owned[6]), "seq")
    grad_qkv, grad_proj, grad_up, grad_down, grad_gains, grad_biases, grad_upbias = summed
    return (
        layer_out.reshape(img_count, tok_count, width),
        grad_in.reshape(img_count, tok_count, width),
        grad_qkv,
        grad_proj,
        grad_up,
        grad_down,
        grad_gains,
        grad_biases,
        grad_upbias,
    )


def solution(mesh):
    in_specs = (
        P("fsdp", "seq", None),
        P("fsdp", None),
        P("fsdp", None),
        P("fsdp", None),
        P("fsdp", None),
        P(None, "fsdp"),
        P(None, "fsdp"),
        P(None, "fsdp"),
        P("fsdp"),
        P("fsdp", "seq", None),
    )
    out_specs = (
        P("fsdp", "seq", None),
        P("fsdp", "seq", None),
        P("fsdp", None),
        P("fsdp", None),
        P("fsdp", None),
        P(None, "fsdp"),
        P(None, "fsdp"),
        P(None, "fsdp"),
        P("fsdp"),
    )

    def layer(*args):
        images = args[0].shape[0] // mesh.shape["fsdp"]
        planes = mesh.shape["fsdp"] // 2
        fits = mesh.shape["seq"] == 4 and images == 2 and planes * 2 == mesh.shape["fsdp"] and planes & (planes - 1) == 0
        plan = image_on_chip if fits else heads_over_seq
        return jax.shard_map(plan, mesh=mesh, in_specs=in_specs, out_specs=out_specs, check_vma=False)(*args)

    return layer
```

```python
import functools
import math

import jax
import jax.numpy as jnp
from jax import lax
from jax.experimental import pallas as pl
from jax.experimental.pallas import tpu as pltpu
from jax.sharding import PartitionSpec as P

HEAD_DIM = 72
QBLOCK = 512
EPSILON = 1e-06
NEG_FILL = -1e30
GELU_CUBE = 0.044715
GELU_SCALE = math.sqrt(2.0 / math.pi)
LOG2E = math.log2(math.e)
LANES = 128
F32 = jnp.float32
BF16 = jnp.bfloat16
MIB = 2**20


def attention_forward_kernel(block, heads, qkv_ref, bias_ref, out_ref, probs_ref, inv_ref, by_row, out_rows):
    head = pl.program_id(0)
    width = heads * HEAD_DIM
    seq = qkv_ref.shape[0]

    @pl.when(head == 0)
    def _():
        by_row[...] = qkv_ref[...].astype(F32).T

    def rows(which):
        return pl.ds(pl.multiple_of(which * width + head * HEAD_DIM, 8), HEAD_DIM)

    query = by_row[rows(0), :].astype(BF16)
    keys = by_row[rows(1), :].T.astype(BF16)
    values = by_row[rows(2), :].astype(BF16)
    bias = bias_ref[...]
    for start in range(0, seq, block):
        part = slice(start, start + block)
        scores = jnp.dot(keys, query[:, part], preferred_element_type=F32) * (LOG2E / math.sqrt(HEAD_DIM)) + bias
        top = jnp.max(scores, axis=0, keepdims=True)
        raised = jnp.exp2(scores - top)
        inv = 1.0 / jnp.sum(raised, axis=0, keepdims=True)
        raised_low = raised.astype(BF16)
        probs_ref[0, :, part] = raised_low
        inv_ref[0, :, part] = inv
        out_rows[rows(0), part] = jnp.dot(values, raised_low, preferred_element_type=F32) * inv

    @pl.when(head == heads - 1)
    def _():
        out_ref[:, :width] = out_rows[...].T.astype(BF16)


def attention_forward(qkv, bias, block=QBLOCK):
    seq, triple = qkv.shape
    width = triple // 3
    heads = width // HEAD_DIM
    whole_tiles = -(-width // LANES) * LANES
    return pl.pallas_call(
        functools.partial(attention_forward_kernel, block, heads),
        grid=(heads,),
        in_specs=[pl.BlockSpec((seq, triple), lambda h: (0, 0)), pl.BlockSpec((seq, 1), lambda h: (0, 0))],
        out_specs=[
            pl.BlockSpec((seq, whole_tiles), lambda h: (0, 0)),
            pl.BlockSpec((1, seq, seq), lambda h: (h, 0, 0)),
            pl.BlockSpec((1, 1, seq), lambda h: (h, 0, 0)),
        ],
        out_shape=[
            jax.ShapeDtypeStruct((seq, whole_tiles), BF16),
            jax.ShapeDtypeStruct((heads, seq, seq), BF16),
            jax.ShapeDtypeStruct((heads, 1, seq), F32),
        ],
        scratch_shapes=[pltpu.VMEM((triple, seq), F32), pltpu.VMEM((width, seq), F32)],
        compiler_params=pltpu.CompilerParams(vmem_limit_bytes=48 * MIB),
        cost_estimate=pl.CostEstimate(
            flops=heads * seq * seq, bytes_accessed=seq * triple, transcendentals=0
        ),
    )(qkv, bias)


def attention_backward_kernel(
    block, heads, qkv_ref, d_out_ref, out_ref, probs_ref, inv_ref, grad_ref, by_row, d_rows, o_rows, grad_rows
):
    head = pl.program_id(0)
    width = heads * HEAD_DIM
    seq = qkv_ref.shape[0]
    scale = 1.0 / math.sqrt(HEAD_DIM)

    @pl.when(head == 0)
    def _():
        by_row[...] = qkv_ref[...].astype(F32).T
        d_rows[...] = d_out_ref[...].astype(F32).T
        o_rows[...] = out_ref[:, :width].astype(F32).T

    def rows(which):
        return pl.ds(pl.multiple_of(which * width + head * HEAD_DIM, 8), HEAD_DIM)

    query = by_row[rows(0), :].T.astype(BF16)
    keys = by_row[rows(1), :].astype(BF16)
    values = by_row[rows(2), :].T.astype(BF16)
    d_out = d_rows[rows(0), :]
    inv = inv_ref[0]
    row_dot = jnp.sum(d_out * o_rows[rows(0), :], axis=0, keepdims=True) * inv
    d_scaled = d_out * inv
    d_tokens = d_scaled.T.astype(BF16)
    d_scaled = d_scaled.astype(BF16)
    d_keys = jnp.zeros((seq, HEAD_DIM), F32)
    d_values = jnp.zeros((seq, HEAD_DIM), F32)
    for start in range(0, seq, block):
        part = slice(start, start + block)
        raised = probs_ref[0, :, part]
        d_probs = jnp.dot(values, d_scaled[:, part], preferred_element_type=F32)
        d_scores = (raised.astype(F32) * (d_probs - row_dot[:, part])).astype(BF16)
        d_values += jnp.dot(raised, d_tokens[part, :], preferred_element_type=F32)
        d_keys += jnp.dot(d_scores, query[part, :], preferred_element_type=F32)
        grad_rows[rows(0), part] = jnp.dot(keys, d_scores, preferred_element_type=F32) * scale
    grad_rows[rows(1), :] = d_keys.T * scale
    grad_rows[rows(2), :] = d_values.T

    @pl.when(head == heads - 1)
    def _():
        grad_ref[...] = grad_rows[...].T.astype(BF16)


def attention_backward(qkv, d_out, out, probs, inv, block=QBLOCK):
    seq, triple = qkv.shape
    width = triple // 3
    heads = width // HEAD_DIM
    whole = lambda h: (0, 0)
    return pl.pallas_call(
        functools.partial(attention_backward_kernel, block, heads),
        grid=(heads,),
        in_specs=[
            pl.BlockSpec((seq, triple), whole),
            pl.BlockSpec((seq, width), whole),
            pl.BlockSpec(out.shape, whole),
            pl.BlockSpec((1, seq, seq), lambda h: (h, 0, 0)),
            pl.BlockSpec((1, 1, seq), lambda h: (h, 0, 0)),
        ],
        out_specs=pl.BlockSpec((seq, triple), whole),
        out_shape=jax.ShapeDtypeStruct((seq, triple), BF16),
        scratch_shapes=[
            pltpu.VMEM((triple, seq), F32),
            pltpu.VMEM((width, seq), F32),
            pltpu.VMEM((width, seq), F32),
            pltpu.VMEM((triple, seq), F32),
        ],
        compiler_params=pltpu.CompilerParams(vmem_limit_bytes=56 * MIB),
        cost_estimate=pl.CostEstimate(
            flops=heads * seq * seq, bytes_accessed=seq * triple, transcendentals=0
        ),
    )(qkv, d_out, out, probs, inv)


class Place:
    def __init__(self):
        self.planes = lax.axis_size("fsdp") // 2
        f = lax.axis_index("fsdp")
        k = lax.axis_index("seq")
        self.z, self.c = f // 2, f % 2
        self.k, self.y, self.x = k, k // 2, k % 2
        self.z_lines = [[2 * z + c for z in range(self.planes)] for c in range(2)]
        self.spot = jnp.stack([self.c, self.z, self.y, self.x, self.k]).astype(jnp.int32)

    def send(self, value, to):
        pairs = []
        for z in range(self.planes):
            for c in range(2):
                for y in range(2):
                    for x in range(2):
                        tz, tc, ty, tx = to(z, c, y, x)
                        pairs.append((((z * 2 + c) * 2 + y) * 2 + x, ((tz * 2 + tc) * 2 + ty) * 2 + tx))
        return lax.ppermute(value, ("fsdp", "seq"), pairs)

    def core(self, value):
        return self.send(value, lambda z, c, y, x: (z, 1 - c, y, x))

    def along_x(self, value):
        return self.send(value, lambda z, c, y, x: (z, c, y, 1 - x))

    def along_y(self, value):
        return self.send(value, lambda z, c, y, x: (z, c, 1 - y, x))

    def across(self, value):
        return self.send(value, lambda z, c, y, x: (z, c, 1 - y, 1 - x))

    def along_z(self, value, step):
        return self.send(value, lambda z, c, y, x: (z ^ step, c, y, x))

    def over_z(self, value):
        return lax.all_to_all(value, "fsdp", 0, 0, axis_index_groups=self.z_lines, tiled=True)

    def turn(self, value, step):
        return self.send(value, lambda z, c, y, x: (z, y, c, x ^ step))


def pick(stack, index):
    return lax.dynamic_index_in_dim(stack, index, 0, keepdims=False)


def in_order(flag, mine, other):
    return jnp.where(flag == 0, jnp.concatenate([mine, other]), jnp.concatenate([other, mine]))


def to_image(place, parts):
    near = place.turn(pick(parts, place.x), 0)
    far = place.turn(pick(parts, 1 - place.x), 1)
    near, far = yield near, far
    half = jnp.concatenate([near, far])
    half, other = yield half, place.core(half)
    return half, other


def image_order(place, row):
    blocks = row.reshape(4, -1)
    first = 2 * place.c + place.x
    return jnp.concatenate([pick(blocks, first ^ i) for i in range(4)])


def from_image(place, half):
    size = half.shape[0] // 2
    near = place.turn(half[:size], 0)
    far = place.turn(half[size:], 1)
    near, far = yield near, far
    return in_order(place.x, near[None], far[None])


def other_order(value):
    size = value.shape[0] // 2
    return jnp.concatenate([value[size:], value[:size]])


def lane_cut(columns):
    return columns // 2 // LANES * LANES


class Transfer:
    def __init__(self, steps):
        self.steps = steps
        self.arrays = next(steps)
        self.result = None


def close_round(*transfers, hold=()):
    arrays, held = lax.optimization_barrier(([transfer.arrays for transfer in transfers], list(hold)))
    for transfer, arrived in zip(transfers, arrays):
        try:
            transfer.arrays = transfer.steps.send(arrived)
        except StopIteration as end:
            transfer.result = end.value
    return held


def spread(place, give, keep):
    arrived = place.core(give)
    keep, arrived = yield keep, arrived
    block = in_order(place.c, keep, arrived)
    rows, columns = block.shape[0] // 4, block.shape[1]
    quarters = block.reshape(4, rows, columns)
    mine = pick(quarters, place.k)
    planes = place.over_z(jnp.broadcast_to(mine[None], (place.planes, rows, columns)))
    quarters, planes = yield quarters, planes
    own = jnp.stack([pick(planes, place.z ^ step) for step in range(1, place.planes)])
    x_part, y_part = place.along_x(own), place.along_y(own)
    quarters, own, x_part, y_part = yield quarters, own, x_part, y_part
    cut = lane_cut(columns)
    far_low = place.along_x(y_part[:, :, :cut])
    far_high = place.along_y(x_part[:, :, cut:])
    pieces = yield quarters, own, x_part, y_part, far_low, far_high
    return pieces


def assemble_kernel(planes, spans, scalars, *refs):
    out, sems = refs[-2:]
    z, k = scalars[1], scalars[4]
    copies = []
    for i, (start, size, to, cut) in enumerate(spans):
        block, own, x_part, y_part, far_low, far_high = refs[6 * i : 6 * i + 6]
        here, there = pl.ds(start, size), pl.ds(to, size)
        copies.append((block.at[:, :, here], out.at[pl.ds(z * 4, 4), :, there]))
        for step in range(1, planes):
            at = (z ^ step) * 4
            copies.append((own.at[step - 1, :, here], out.at[at + k, :, there]))
            copies.append((x_part.at[step - 1, :, here], out.at[at + (k ^ 1), :, there]))
            copies.append((y_part.at[step - 1, :, here], out.at[at + (k ^ 2), :, there]))
            low, high = max(0, min(start + size, cut) - start), max(0, start + size - max(start, cut))
            if low:
                copies.append((far_low.at[step - 1, :, pl.ds(start, low)], out.at[at + (k ^ 3), :, pl.ds(to, low)]))
            if high:
                copies.append(
                    (
                        far_high.at[step - 1, :, pl.ds(start + size - high - cut, high)],
                        out.at[at + (k ^ 3), :, pl.ds(to + size - high, high)],
                    )
                )
    started = [pltpu.make_async_copy(source, target, sems.at[i]) for i, (source, target) in enumerate(copies)]
    for copy in started:
        copy.start()
    for copy in started:
        copy.wait()


def assemble(place, *parts):
    planes = place.planes
    rows = parts[0][0][0].shape[1]
    spans, to, operands = [], 0, []
    for pieces, start, size in parts:
        spans.append((start, size, to, lane_cut(pieces[0].shape[2])))
        operands += list(pieces)
        to += size
    anywhere = pl.BlockSpec(memory_space=pl.ANY)
    out = pl.pallas_call(
        functools.partial(assemble_kernel, planes, spans),
        in_specs=[pl.BlockSpec(memory_space=pltpu.SMEM)] + [anywhere] * len(operands),
        out_specs=pl.BlockSpec(memory_space=pltpu.VMEM),
        out_shape=jax.ShapeDtypeStruct((planes * 4, rows, to), BF16),
        scratch_shapes=[pltpu.SemaphoreType.DMA((len(parts) * (1 + 5 * (planes - 1)),))],
        compiler_params=pltpu.CompilerParams(vmem_limit_bytes=32 * MIB),
        cost_estimate=pl.CostEstimate(flops=0, bytes_accessed=4 * planes * 4 * rows * to, transcendentals=0),
    )(place.spot, *operands)
    return out.reshape(planes * 4 * rows, to)


def whole_spec():
    return pl.BlockSpec(memory_space=pltpu.VMEM)


def scalar_spec():
    return pl.BlockSpec(memory_space=pltpu.SMEM)


def vmem(mib):
    return pltpu.CompilerParams(vmem_limit_bytes=mib * MIB)


def join_kernel(turn, where, mine, other, out):
    rows, width = out.shape[0], out.shape[1] // 2
    half = rows // 2

    for core in range(2):

        @pl.when(where[0] == core)
        def _():
            out[:, core * width : (core + 1) * width] = mine[:, :width]
            low, high = (1 - core) * width, (2 - core) * width
            if turn:
                out[:half, low:high] = other[half:, :width]
                out[half:, low:high] = other[:half, :width]
            else:
                out[:, low:high] = other[:, :width]


def join(place, mine, other, width, turn):
    return pl.pallas_call(
        functools.partial(join_kernel, turn),
        in_specs=[scalar_spec(), whole_spec(), whole_spec()],
        out_specs=whole_spec(),
        out_shape=jax.ShapeDtypeStruct((mine.shape[0], 2 * width), BF16),
        compiler_params=vmem(24),
    )(place.spot, mine, other)


def weight_grad_kernel(cut, group, rows, pair_count, with_riders, with_sums, where, *refs):
    lefts, rights, refs = refs[:pair_count], refs[pair_count : 2 * pair_count], refs[2 * pair_count :]
    riders, refs = (refs[0], refs[1:]) if with_riders else (None, refs)
    low_keep, low_send, high_keep, high_send, *refs = refs
    sums, refs = (refs[0], refs[1:]) if with_sums else (None, refs)
    total, *turned = refs
    step = pl.program_id(0)
    y, x = where[2], where[3]
    block = group * 4 * rows

    @pl.when(step == 0)
    def _():
        for left, by_row in zip(lefts, turned):
            by_row[...] = left[...].astype(F32).T.astype(BF16)
        if with_sums:
            sums[...] = jnp.broadcast_to(jnp.sum(rights[0][...].astype(F32), axis=0, keepdims=True), sums.shape)

    at = 0
    for right, by_row in zip(rights, turned):
        left = by_row[pl.ds(pl.multiple_of(step * block, 16), block), :]
        columns = right.shape[1]
        for start in range(0, columns, 4 * LANES):
            end = min(start + 4 * LANES, columns)
            total[:, at + start : at + end] = jnp.dot(left, right[:, start:end], preferred_element_type=F32)
        at += columns
    if with_riders:
        total[:, at:] = riders[...]
    for plane in range(group):
        for dy in range(2):
            for dx in range(2):
                row = (plane * 4 + (y ^ dy) * 2 + (x ^ dx)) * rows
                part = total[pl.ds(pl.multiple_of(row, 8), rows), :].astype(BF16)
                (low_send if dx else low_keep)[dy, plane] = part[:, :cut]
                (high_send if dy else high_keep)[dx, plane] = part[:, cut:]


def weight_grad(place, pairs, riders=None, with_sums=False):
    planes = place.planes
    tokens, width = pairs[0][0].shape
    rows = width // planes // 4
    group = 2
    columns = sum(right.shape[1] for _, right in pairs) + (0 if riders is None else riders.shape[1])
    rider_list = [] if riders is None else [riders]
    cut = lane_cut(columns)
    still = lambda shape: pl.BlockSpec(shape, lambda i: (0, 0), pipeline_mode=pl.Buffered(1))
    low = jax.ShapeDtypeStruct((2, planes, rows, cut), BF16)
    high = jax.ShapeDtypeStruct((2, planes, rows, columns - cut), BF16)
    low_spec = pl.BlockSpec((2, group, rows, cut), lambda i: (0, i, 0, 0))
    high_spec = pl.BlockSpec((2, group, rows, columns - cut), lambda i: (0, i, 0, 0))
    sum_shapes = [jax.ShapeDtypeStruct((8, pairs[0][1].shape[1]), F32)] if with_sums else []
    return pl.pallas_call(
        functools.partial(weight_grad_kernel, cut, group, rows, len(pairs), riders is not None, with_sums),
        grid=(planes // group,),
        in_specs=[scalar_spec()]
        + [still(left.shape) for left, _ in pairs]
        + [still(right.shape) for _, right in pairs]
        + [pl.BlockSpec((group * 4 * rows, extra.shape[1]), lambda i: (i, 0)) for extra in rider_list],
        out_specs=[low_spec, low_spec, high_spec, high_spec] + [pl.BlockSpec(s.shape, lambda i: (0, 0)) for s in sum_shapes],
        out_shape=[low, low, high, high] + sum_shapes,
        scratch_shapes=[pltpu.VMEM((group * 4 * rows, columns), F32)] + [pltpu.VMEM((width, tokens), BF16) for _ in pairs],
        compiler_params=vmem(56),
        cost_estimate=pl.CostEstimate(flops=tokens * width, bytes_accessed=width * columns, transcendentals=0),
    )(place.spot, *[left for left, _ in pairs], *[right for _, right in pairs], *rider_list)


def add_first_kernel(low, from_x, high, from_y, low_keep, low_send, high_keep, high_send):
    for kept, arrived, outs in ((low, from_x, (low_keep, low_send)), (high, from_y, (high_keep, high_send))):
        for i, out in enumerate(outs):
            out[...] = (kept[i].astype(F32) + arrived[i].astype(F32)).astype(BF16)


def add_first(low, from_x, high, from_y):
    planes = low.shape[1]
    ins = lambda a: pl.BlockSpec((2, 1, *a.shape[2:]), lambda i: (0, i, 0, 0))
    out = lambda a: pl.BlockSpec((1, *a.shape[2:]), lambda i: (i, 0, 0))
    shape = lambda a: jax.ShapeDtypeStruct(a.shape[1:], BF16)
    return pl.pallas_call(
        add_first_kernel,
        grid=(planes,),
        in_specs=[ins(low), ins(from_x), ins(high), ins(from_y)],
        out_specs=[out(low), out(low), out(high), out(high)],
        out_shape=[shape(low), shape(low), shape(high), shape(high)],
        compiler_params=vmem(24),
    )(low, from_x, high, from_y)


def add_second_kernel(low, from_y, high, from_x, out):
    cut = low.shape[2]
    out[:, :, :cut] = (low[...].astype(F32) + from_y[...].astype(F32)).astype(BF16)
    out[:, :, cut:] = (high[...].astype(F32) + from_x[...].astype(F32)).astype(BF16)


def add_second(low, from_y, high, from_x):
    planes, rows, cut = low.shape
    spec = lambda columns: pl.BlockSpec((1, rows, columns), lambda i: (i, 0, 0))
    rest = high.shape[2]
    return pl.pallas_call(
        add_second_kernel,
        grid=(planes,),
        in_specs=[spec(cut), spec(cut), spec(rest), spec(rest)],
        out_specs=spec(cut + rest),
        out_shape=jax.ShapeDtypeStruct((planes, rows, cut + rest), BF16),
        compiler_params=vmem(24),
    )(low, from_y, high, from_x)


def quarter_of(where, parts, core, side, store):
    mine, x_part, y_part, far_low, far_high = parts
    near, same = where[2] == core, where[3] == side

    @pl.when(near & same)
    def _():
        store(mine[...])

    @pl.when(near & ~same)
    def _():
        store(x_part[...])

    @pl.when(~near & same)
    def _():
        store(y_part[...])

    @pl.when(~near & ~same)
    def _():
        store(jnp.concatenate([far_low[...], far_high[...]], axis=1))


def give_kernel(where, *refs):
    out = refs[-1]
    for core in range(2):

        @pl.when(where[0] != core)
        def _():
            for side in range(2):

                def store(value):
                    out[side] = value

                quarter_of(where, refs[:-1], core, side, store)


def give_rows(place, parts):
    rows, columns = parts[0].shape
    return pl.pallas_call(
        give_kernel,
        in_specs=[scalar_spec()] + [whole_spec()] * 5,
        out_specs=whole_spec(),
        out_shape=jax.ShapeDtypeStruct((2, rows, columns), BF16),
        compiler_params=vmem(24),
    )(place.spot, *parts)


def finish_kernel(write, where, *refs):
    parts, arrived = refs[:5], refs[5]
    outs, kept = refs[6:-1], refs[-1]
    for core in range(2):

        @pl.when(where[0] == core)
        def _():
            for side in range(2):

                def store(value):
                    kept[side] = value

                quarter_of(where, parts, core, side, store)
            halves = [kept[...], arrived[...]]
            if core:
                halves = halves[::-1]
            lower, higher = (half.astype(F32).reshape(-1, half.shape[2]) for half in halves)
            write(lower, higher, *outs)


def lay_kernel(write, where, mine, other, out):
    for core in range(2):

        @pl.when(where[0] == core)
        def _():
            halves = [mine[...].astype(F32), other[...].astype(F32)]
            if core:
                halves = halves[::-1]
            write(*halves, out)


def lay(place, mine, other, write, shape):
    return pl.pallas_call(
        functools.partial(lay_kernel, write),
        in_specs=[scalar_spec()] + [whole_spec()] * 2,
        out_specs=whole_spec(),
        out_shape=jax.ShapeDtypeStruct(shape, F32),
        compiler_params=vmem(24),
    )(place.spot, mine, other)


def finish(place, pieces, write, shapes):
    *parts, arrived = pieces
    return pl.pallas_call(
        functools.partial(finish_kernel, write),
        in_specs=[scalar_spec()] + [whole_spec()] * 6,
        out_specs=[whole_spec()] * len(shapes),
        out_shape=[jax.ShapeDtypeStruct(shape, F32) for shape in shapes],
        scratch_shapes=[pltpu.VMEM(arrived.shape, BF16)],
        compiler_params=vmem(40),
    )(place.spot, *parts, arrived)


def collect(place, pieces):
    low, low_send, high, high_send = pieces
    low, high, from_x, from_y = yield low, high, place.along_x(low_send), place.along_y(high_send)
    low, low_send, high, high_send = add_first(low, from_x, high, from_y)
    low, high, from_y, from_x = yield low, high, place.along_y(low_send), place.along_x(high_send)
    cut = low.shape[2]
    arrived = yield place.over_z(add_second(low, from_y, high, from_x))
    mine = jnp.sum(arrived.astype(F32), axis=0).astype(BF16)
    mine, x_part, y_part = yield mine, place.along_x(mine), place.along_y(mine)
    far_low, far_high = place.along_x(y_part[:, :cut]), place.along_y(x_part[:, cut:])
    parts = yield mine, x_part, y_part, far_low, far_high
    parts, arrived = yield parts, place.core(give_rows(place, parts))
    return (*parts, arrived)


def first_norm_kernel(half, other, tokens, normed, inv_std):
    size = half.shape[0]
    for i, part in enumerate((half, other)):
        rows = slice(i * size, (i + 1) * size)
        values = part[...]
        tokens[rows, :] = values
        normed[rows, :], inv_std[rows, :] = normalize(values.astype(F32))


def first_norm(half, other):
    size, width = half.shape
    return pl.pallas_call(
        first_norm_kernel,
        in_specs=[whole_spec()] * 2,
        out_specs=[whole_spec()] * 3,
        out_shape=[
            jax.ShapeDtypeStruct((2 * size, width), BF16),
            jax.ShapeDtypeStruct((2 * size, width), F32),
            jax.ShapeDtypeStruct((2 * size, 1), F32),
        ],
        compiler_params=vmem(32),
    )(half, other)


def sum_plane(place, rows):
    cut = lane_cut(rows.shape[1])
    low, high = rows[:, :cut], rows[:, cut:]
    low, high, from_x, from_y = yield low, high, place.along_x(low), place.along_y(high)
    low, high = add(low, from_x), add(high, from_y)
    low, high, from_y, from_x = yield low, high, place.along_y(low), place.along_x(high)
    return jnp.concatenate([add(low, from_y), add(high, from_x)], axis=1)


def sum_devices(place, value):
    value, other = yield value, place.core(value)
    value = value + other
    value, others = yield value, [place.along_x(value), place.along_y(value), place.across(value)]
    value = value + others[0] + others[1] + others[2]
    value, others = yield value, [place.along_z(value, step) for step in range(1, place.planes)]
    return functools.reduce(jnp.add, others, value)


def add(mine, arrived):
    return (mine.astype(F32) + arrived.astype(F32)).astype(BF16)


def norm_back_kernel(half, where, part, arrived, upstream, normed, inv_std, gain, low, own_columns, own_rows, sums):
    step = pl.program_id(0)
    e = part[...] + arrived[...].astype(F32)
    n = normed[...].astype(F32)
    scaled = e * gain[...]
    first_mean = jnp.mean(scaled, axis=-1, keepdims=True)
    second_mean = jnp.mean(scaled * n, axis=-1, keepdims=True)
    cot = upstream[...].astype(F32)
    d = cot + inv_std[...] * (scaled - first_mean - n * second_mean)
    d_low = d.astype(BF16)
    low[...] = d_low
    for core in range(2):

        @pl.when(where[0] == core)
        def _():
            own_columns[...] = d_low[:, core * half : (core + 1) * half]

    @pl.when(step < pl.num_programs(0) // 2)
    def _():
        own_rows[...] = d

    rows = jnp.concatenate([jnp.sum(v, axis=0, keepdims=True) for v in (e * n, e, d, cot)] + [jnp.zeros((4, e.shape[1]), F32)])

    @pl.when(step == 0)
    def _():
        sums[...] = rows

    @pl.when(step > 0)
    def _():
        sums[...] += rows


def norm_back_second(place, part, arrived, upstream, normed, inv_std, gain):
    tokens, width = part.shape
    size = tokens // 8
    by_row = pl.BlockSpec((size, width), lambda i: (i, 0))
    turned = pl.BlockSpec((size, width), lambda i: ((i + 4) % 8, 0))
    return pl.pallas_call(
        functools.partial(norm_back_kernel, width // 2),
        grid=(8,),
        in_specs=[
            scalar_spec(),
            by_row,
            turned,
            by_row,
            by_row,
            pl.BlockSpec((size, 1), lambda i: (i, 0)),
            pl.BlockSpec((1, width), lambda i: (0, 0)),
        ],
        out_specs=[
            by_row,
            pl.BlockSpec((size, width // 2), lambda i: (i, 0)),
            pl.BlockSpec((size, width), lambda i: (jnp.minimum(i, 3), 0)),
            pl.BlockSpec((8, width), lambda i: (0, 0)),
        ],
        out_shape=[
            jax.ShapeDtypeStruct((tokens, width), BF16),
            jax.ShapeDtypeStruct((tokens, width // 2), BF16),
            jax.ShapeDtypeStruct((tokens // 2, width), F32),
            jax.ShapeDtypeStruct((8, width), F32),
        ],
        compiler_params=vmem(24),
    )(place.spot, part, arrived, upstream, normed, inv_std, gain)


def norm_back_first_kernel(part, arrived, d_resid, normed, inv_std, gain, grad, sums):
    e = part[...] + arrived[...].astype(F32)
    n = normed[...].astype(F32)
    scaled = e * gain[...]
    first_mean = jnp.mean(scaled, axis=-1, keepdims=True)
    second_mean = jnp.mean(scaled * n, axis=-1, keepdims=True)
    grad[...] = (d_resid[...] + inv_std[...] * (scaled - first_mean - n * second_mean)).astype(BF16)
    rows = jnp.concatenate([jnp.sum(v, axis=0, keepdims=True) for v in (e * n, e)] + [jnp.zeros((6, e.shape[1]), F32)])

    @pl.when(pl.program_id(0) == 0)
    def _():
        sums[...] = rows

    @pl.when(pl.program_id(0) > 0)
    def _():
        sums[...] += rows


def norm_back_first(part, arrived, d_resid, normed, inv_std, gain):
    tokens, width = arrived.shape
    size = tokens // 4
    by_row = pl.BlockSpec((size, width), lambda i: (i, 0))
    return pl.pallas_call(
        norm_back_first_kernel,
        grid=(4,),
        in_specs=[by_row] * 4 + [pl.BlockSpec((size, 1), lambda i: (i, 0)), pl.BlockSpec((1, width), lambda i: (0, 0))],
        out_specs=[by_row, pl.BlockSpec((8, width), lambda i: (0, 0))],
        out_shape=[jax.ShapeDtypeStruct((tokens, width), BF16), jax.ShapeDtypeStruct((8, width), F32)],
        compiler_params=vmem(24),
    )(part, arrived, d_resid, normed, inv_std, gain)


def normalize(values):
    row_mean = jnp.mean(values, axis=-1, keepdims=True)
    centred = values - row_mean
    variance = jnp.mean(centred * centred, axis=-1, keepdims=True)
    inv_std = lax.rsqrt(variance + EPSILON)
    return centred * inv_std, inv_std


def layer_norm(values, gain_row, shift_row):
    row_mean = jnp.mean(values, axis=-1, keepdims=True)
    centred = values - row_mean
    variance = jnp.mean(centred * centred, axis=-1, keepdims=True)
    inv_std = lax.rsqrt(variance + EPSILON)
    normed = centred * inv_std
    return (normed * gain_row + shift_row, normed, inv_std)


def norm_back(upstream, normed, inv_std, gain_row):
    scaled = upstream * gain_row
    first_mean = jnp.mean(scaled, axis=-1, keepdims=True)
    second_mean = jnp.mean(scaled * normed, axis=-1, keepdims=True)
    return inv_std * (scaled - first_mean - normed * second_mean)


def gelu_and_slope(values):
    square = values * values
    tangent = jnp.tanh(GELU_SCALE * values * (1.0 + GELU_CUBE * square))
    half = 0.5 * (1.0 + tangent)
    slope = half + 0.5 * values * (1.0 - tangent * tangent) * GELU_SCALE * (1.0 + 3.0 * GELU_CUBE * square)
    return values * half, slope


def dot(a, b):
    return jnp.dot(a, b, preferred_element_type=F32)


def dot_t(a, b):
    return lax.dot_general(a, b, (((1,), (1,)), ((), ())), preferred_element_type=F32)


def t_dot(a, b):
    return lax.dot_general(a, b, (((0,), (0,)), ((), ())), preferred_element_type=F32)


def image_on_chip(inputs, key_mask, w_qkv, w_out, w_up, w_down, norm_gains, biases, up_bias, cotangent):
    place = Place()
    img_count, tok_count, width = inputs.shape
    shard = w_qkv.shape[0]
    fsdp = lax.axis_size("fsdp")
    half_width = width // 2
    hidden = w_up.shape[1]
    half_hidden = -(-hidden // 2 // LANES) * LANES
    up_shard = up_bias.shape[0]
    up_cols = -(-up_shard // shard)

    def halves_qkv(w):
        return jnp.moveaxis(w.reshape(w.shape[0], 3, 2, half_width), 2, 0).reshape(2, w.shape[0], 3 * half_width)

    def halves_hidden(w):
        padded = jnp.pad(w, ((0, 0), (0, 2 * half_hidden - hidden)))
        return jnp.stack([padded[:, :half_hidden], padded[:, half_hidden:]])

    small = jnp.concatenate(
        [
            norm_gains,
            biases,
            jnp.pad(up_bias, (0, up_cols * shard - up_shard)).reshape(up_cols, shard),
        ]
    )
    n_small = small.shape[0]
    spare = -(3 * half_width) % LANES
    extra = jnp.pad(small.T, ((0, 0), (0, spare - n_small)))
    c = place.c

    qkv_halves = halves_qkv(w_qkv)
    give = jnp.concatenate([pick(qkv_halves, 1 - c), extra], axis=1)
    keep = jnp.concatenate([pick(qkv_halves, c), extra], axis=1)
    qkv = Transfer(spread(place, give, keep))
    tokens_in = Transfer(to_image(place, inputs))
    other_mask = place.core(key_mask)
    w_out, w_up, w_down = close_round(qkv, hold=(w_out, w_up, w_down))

    out_pad = -half_width % LANES
    out_cols = half_width + out_pad
    out_halves = jnp.pad(jnp.moveaxis(w_out.reshape(shard, 2, half_width), 1, 0), ((0, 0), (0, 0), (0, out_pad)))
    down_halves = halves_hidden(w_down.T)
    down = Transfer(spread(place, pick(down_halves, 1 - c), pick(down_halves, c)))
    rest = jnp.concatenate([out_halves, halves_hidden(w_up)], axis=2)
    out_up = Transfer(spread(place, pick(rest, 1 - c), pick(rest, c)))
    close_round(qkv, tokens_in, out_up)
    close_round(qkv, tokens_in)

    live_keys = image_order(place, pick(jnp.where(c == place.y, key_mask, other_mask), place.x))
    mask_bias = jnp.where(live_keys > 0, 0.0, NEG_FILL).astype(F32)[:, None]
    tokens, first_normed, first_inv = first_norm(*tokens_in.result)
    (first_normed,) = close_round(qkv, out_up, down, hold=(first_normed,))

    full_first = assemble(place, (qkv.result, 0, 3 * half_width + spare))
    full_qkv = full_first[:, : 3 * half_width]
    small_rows = full_first[:, 3 * half_width : 3 * half_width + n_small].astype(F32).T
    gain_rows, bias_rows = small_rows[:2], small_rows[2:8]
    up_shift = (
        small_rows[8:].reshape(up_cols, fsdp, shard).transpose(1, 0, 2).reshape(fsdp, up_cols * shard)[:, :up_shard]
    ).reshape(hidden)
    up_shift = pick(jnp.pad(up_shift, (0, 2 * half_hidden - hidden)).reshape(2, half_hidden), c)
    shift_halves = bias_rows.reshape(6, 2, half_width)
    qkv_shift = jnp.concatenate(
        [pick(shift_halves[2], c), jnp.zeros((half_width,), F32), pick(shift_halves[3], c)]
    )
    first_low = (first_normed * gain_rows[0] + bias_rows[0]).astype(BF16)
    packed = (dot(first_low, full_qkv) + qkv_shift).astype(BF16)
    packed, cotangent = close_round(out_up, hold=(packed, cotangent))

    upstream_in = Transfer(to_image(place, cotangent))
    attended_half, raised, inv_total = attention_forward(packed, mask_bias)
    (attended_half,) = close_round(out_up, upstream_in, down, hold=(attended_half,))

    half_out = assemble(place, (out_up.result, 0, out_cols))
    full_out = join(place, half_out, place.core(half_out), half_width, False)
    attended = join(place, attended_half, place.core(attended_half), half_width, True)
    residual = tokens.astype(F32) + dot(attended, full_out) + bias_rows[4]
    second_normed, second_inv = normalize(residual)
    second_low = (second_normed * gain_rows[1] + bias_rows[1]).astype(BF16)
    second_normed = second_normed.astype(BF16)
    half = residual.shape[0] // 2
    residual_half = residual[:half]
    (second_low,) = close_round(upstream_in, down, hold=(second_low,))

    full_up = assemble(place, (out_up.result, out_cols, half_hidden))
    active, slope = gelu_and_slope(dot(second_low, full_up) + up_shift)
    active, slope = active.astype(BF16), slope.astype(BF16)
    active, slope = close_round(down, hold=(active, slope))

    upstream = jnp.concatenate(upstream_in.result)
    dw_down = t_dot(upstream, active).astype(BF16)
    down_rows = lax.psum_scatter(dw_down, "fsdp", scatter_dimension=0, tiled=True, axis_index_groups=place.z_lines)
    full_down = assemble(place, (down.result, 0, half_hidden))
    d_active = dot(upstream, full_down)
    d_upper = (d_active * slope.astype(F32)).astype(BF16)
    d_second_part = dot_t(d_upper, full_up)
    (d_second_part,) = close_round(hold=(d_second_part,))

    d_second_other = place.core(d_second_part.astype(BF16))
    *dw_up, d_upper_sums = weight_grad(place, [(second_low, d_upper)], with_sums=True)
    down_part = dot_t(active, full_down)
    down_sum = down_part[:half] + place.core(down_part[half:].astype(BF16)).astype(F32)
    layer_half = (residual_half + down_sum + bias_rows[5]).astype(BF16)
    *dw_up, d_second_other, layer_half = close_round(hold=(*dw_up, d_second_other, layer_half))

    up_grad = Transfer(collect(place, dw_up))
    layer_out = Transfer(from_image(place, layer_half))
    d_resid_low, d_resid_columns, d_resid_half, by_width = norm_back_second(
        place, d_second_part, d_second_other, upstream, second_normed, second_inv, gain_rows[1:]
    )
    out_rows = lax.dynamic_slice_in_dim(full_out, c * half_width, half_width)
    d_attended = dot_t(d_resid_low, out_rows).astype(BF16)
    d_packed = attention_backward(packed, d_attended, attended_half, raised, inv_total)
    d_packed, down_rows = close_round(up_grad, layer_out, hold=(d_packed, down_rows))

    down_grad = Transfer(sum_plane(place, down_rows))

    def own_part(row):
        size = row.shape[0]
        return jnp.where(c == 0, jnp.pad(row, (0, size)), jnp.pad(row, (size, 0)))

    by_hidden = own_part(d_upper_sums[0])[:hidden].reshape(fsdp, up_shard)
    by_hidden = jnp.pad(by_hidden, ((0, 0), (0, up_cols * shard - up_shard))).reshape(fsdp, up_cols, shard)
    by_hidden = by_hidden.transpose(1, 0, 2).reshape(up_cols, width)
    pack_wide = d_packed.astype(F32)
    riders = jnp.concatenate(
        [
            own_part(jnp.sum(pack_wide[:, :half_width], axis=0))[None],
            own_part(jnp.sum(pack_wide[:, 2 * half_width :], axis=0))[None],
            jnp.where(c == 0, by_width[:4], 0.0),
            by_hidden,
        ]
    )
    riders = jnp.pad(riders, ((0, LANES - riders.shape[0]), (0, 0))).T
    dw_last = weight_grad(place, [(first_low, d_packed), (attended, d_resid_columns)], riders)
    *dw_last, d_packed = close_round(up_grad, down_grad, hold=(*dw_last, d_packed))

    last_grad = Transfer(collect(place, dw_last))
    d_first_part = dot_t(d_packed, full_qkv)
    grad_half, first_sums = norm_back_first(
        d_first_part,
        place.core(d_first_part[half:].astype(BF16)),
        d_resid_half,
        first_normed,
        first_inv,
        gain_rows[:1],
    )
    grad_half, first_sums = close_round(up_grad, last_grad, hold=(grad_half, first_sums))

    def write_hidden(lower, higher, out):
        out[:, :half_hidden] = lower[:, :half_hidden]
        out[:, half_hidden:] = higher[:, : hidden - half_hidden]

    def write_last(lower, higher, qkv_out, proj, rest):
        for i in range(3):
            here = slice(i * half_width, (i + 1) * half_width)
            qkv_out[:, i * width : i * width + half_width] = lower[:, here]
            qkv_out[:, i * width + half_width : (i + 1) * width] = higher[:, here]
        here = slice(3 * half_width, 4 * half_width)
        proj[:, :half_width] = lower[:, here]
        proj[:, half_width:] = higher[:, here]
        rest[...] = lower[:, 4 * half_width :] + higher[:, 4 * half_width :]

    late = Transfer(sum_devices(place, first_sums[:2].reshape(-1, LANES)))
    close_round(up_grad, last_grad, late, down_grad)
    grad_in = Transfer(from_image(place, grad_half))
    down_rows = down_grad.result.reshape(2, shard, half_hidden)
    down_other = place.core(pick(down_rows, 1 - c))
    grad_down = lay(place, pick(down_rows, c), down_other, write_hidden, (shard, hidden))
    (grad_down,) = close_round(up_grad, last_grad, late, grad_in, hold=(grad_down,))
    grad_in, layer_out = close_round(up_grad, last_grad, late, hold=(grad_in.result, layer_out.result))
    (grad_up,) = finish(place, up_grad.result, write_hidden, [(shard, hidden)])
    (grad_up,) = close_round(last_grad, hold=(grad_up,))
    close_round(last_grad)
    grad_qkv, grad_proj, rest_sums = finish(
        place, last_grad.result, write_last, [(shard, 3 * width), (shard, width), (shard, LANES)]
    )
    rows = rest_sums[:, : 6 + up_cols].T
    first_rows = lax.dynamic_slice_in_dim(late.result.reshape(2, width), lax.axis_index("fsdp") * shard, shard, axis=1)
    grad_upbias = rows[6:].reshape(up_cols * shard)[:up_shard]
    grad_gains = jnp.stack([first_rows[0], rows[2]])
    grad_biases = jnp.stack([first_rows[1], rows[3], rows[0], rows[1], rows[4], rows[5]])
    return (layer_out, grad_in, grad_qkv, grad_proj, grad_up, grad_down.T, grad_gains, grad_biases, grad_upbias)


def for_sending(array):
    return jax.tree.map(lambda a: a.astype(jnp.bfloat16) if a.dtype == jnp.float32 else a, array)


def gelu_tanh(values):
    return (
        0.5
        * values
        * (1.0 + jnp.tanh(GELU_SCALE * (values + GELU_CUBE * values * values * values)))
    )


def gelu_slope(values):
    tangent = jnp.tanh(GELU_SCALE * (values + GELU_CUBE * values * values * values))
    return 0.5 * (1.0 + tangent) + 0.5 * values * (1.0 - tangent * tangent) * GELU_SCALE * (
        1.0 + 3.0 * GELU_CUBE * values * values
    )


def block_scores(q_block, keys_full, live, score_scale):
    scores = (
        jnp.einsum("qhd,khd->hqk", q_block, keys_full, preferred_element_type=jnp.float32)
        * score_scale
    )
    return jnp.where(live[None, None, :] > 0, scores, NEG_FILL)


def forward_image(pieces, block_rows, score_scale):
    query, keys_full, values_full, live = pieces
    out_parts = []
    total_parts = []
    for start in range(0, query.shape[0], block_rows):
        masked = block_scores(query[start : start + block_rows], keys_full, live, score_scale)
        top_score = jnp.max(masked, axis=-1, keepdims=True)
        log_total = top_score + jnp.log(
            jnp.sum(jnp.exp(masked - top_score), axis=-1, keepdims=True)
        )
        probs_low = jnp.exp(masked - log_total).astype(jnp.bfloat16)
        out_parts.append(
            jnp.einsum(
                "hqk,khd->qhd", probs_low, values_full, preferred_element_type=jnp.float32
            ).astype(jnp.bfloat16)
        )
        total_parts.append(log_total)
    return (jnp.concatenate(out_parts, axis=0), jnp.concatenate(total_parts, axis=1))


def backward_image(pieces, block_rows, score_scale):
    query, keys_full, values_full, live, log_totals, d_heads = pieces
    dq_parts = []
    dk_total = jnp.zeros(keys_full.shape, jnp.float32)
    dv_total = jnp.zeros(values_full.shape, jnp.float32)
    for start in range(0, query.shape[0], block_rows):
        q_block = query[start : start + block_rows]
        d_block = d_heads[start : start + block_rows]
        masked = block_scores(q_block, keys_full, live, score_scale)
        probs = jnp.exp(masked - log_totals[:, start : start + block_rows])
        probs_low = probs.astype(jnp.bfloat16)
        d_probs = jnp.einsum(
            "qhd,khd->hqk", d_block, values_full, preferred_element_type=jnp.float32
        )
        row_dot = jnp.sum(probs * d_probs, axis=-1, keepdims=True)
        d_scores = (probs * (d_probs - row_dot)).astype(jnp.bfloat16)
        dq_block = (
            jnp.einsum("hqk,khd->qhd", d_scores, keys_full, preferred_element_type=jnp.float32)
            * score_scale
        )
        dq_parts.append(dq_block.astype(jnp.bfloat16))
        dk_total = dk_total + jnp.einsum(
            "hqk,qhd->khd", d_scores, q_block, preferred_element_type=jnp.float32
        )
        dv_total = dv_total + jnp.einsum(
            "hqk,qhd->khd", probs_low, d_block, preferred_element_type=jnp.float32
        )
    return (
        jnp.concatenate(dq_parts, axis=0),
        (dk_total * score_scale).astype(jnp.bfloat16),
        dv_total.astype(jnp.bfloat16),
    )


def heads_over_seq(inputs, key_mask, w_qkv, w_out, w_up, w_down, norm_gains, biases, up_bias, cotangent):
    img_count, tok_count, width = inputs.shape
    seq_len = key_mask.shape[1]
    row_count = img_count * tok_count
    head_cols = width // lax.axis_size("seq")
    local_heads = head_cols // HEAD_DIM
    block_rows = min(QBLOCK, seq_len)
    score_scale = 1.0 / math.sqrt(HEAD_DIM)
    gathered = (
        lax.all_gather(w_qkv, "fsdp", axis=0, tiled=True),
        lax.all_gather(w_out, "fsdp", axis=0, tiled=True),
        lax.all_gather(w_up, "fsdp", axis=0, tiled=True),
        lax.all_gather(w_down, "fsdp", axis=1, tiled=True),
        lax.all_gather(norm_gains, "fsdp", axis=1, tiled=True),
        lax.all_gather(biases, "fsdp", axis=1, tiled=True),
        lax.all_gather(up_bias, "fsdp", axis=0, tiled=True),
    )
    full_qkv, full_out, full_up, full_down, full_gains, full_biases, full_upbias = gathered
    gain_rows = full_gains.astype(jnp.float32)
    bias_rows = full_biases.astype(jnp.float32)
    up_shift = full_upbias.astype(jnp.float32)
    qkv_shift = jnp.concatenate([bias_rows[2], jnp.zeros((width,), jnp.float32), bias_rows[3]])
    tok_wide = inputs.reshape(row_count, width).astype(jnp.float32)
    first_out, first_normed, first_inv = layer_norm(tok_wide, gain_rows[0], bias_rows[0])
    first_low = first_out.astype(jnp.bfloat16)
    packed = (jnp.dot(first_low, full_qkv, preferred_element_type=jnp.float32) + qkv_shift).astype(
        jnp.bfloat16
    )
    by_heads = lax.all_to_all(
        packed.reshape(img_count, tok_count, 3, width),
        "seq",
        split_axis=3,
        concat_axis=1,
        tiled=True,
    )
    query = by_heads[:, :, 0].reshape(img_count, seq_len, local_heads, HEAD_DIM)
    keys_full = by_heads[:, :, 1].reshape(img_count, seq_len, local_heads, HEAD_DIM)
    values_full = by_heads[:, :, 2].reshape(img_count, seq_len, local_heads, HEAD_DIM)

    def run_forward(pieces):
        return forward_image(pieces, block_rows, score_scale)

    attended_heads, log_totals = lax.map(run_forward, (query, keys_full, values_full, key_mask))
    attended = lax.all_to_all(
        for_sending(attended_heads.reshape(img_count, seq_len, head_cols)),
        "seq",
        split_axis=1,
        concat_axis=2,
        tiled=True,
    ).reshape(row_count, width)
    residual = (
        tok_wide + jnp.dot(attended, full_out, preferred_element_type=jnp.float32) + bias_rows[4]
    )
    second_out, second_normed, second_inv = layer_norm(residual, gain_rows[1], bias_rows[1])
    second_low = second_out.astype(jnp.bfloat16)
    upper = jnp.dot(second_low, full_up, preferred_element_type=jnp.float32) + up_shift
    active = gelu_tanh(upper).astype(jnp.bfloat16)
    layer_out = (
        residual + jnp.dot(active, full_down, preferred_element_type=jnp.float32) + bias_rows[5]
    ).astype(jnp.bfloat16)
    back_qkv, back_out, back_up, back_down, back_gains, back_biases, back_upbias = gathered
    back_gain_rows = back_gains.astype(jnp.float32)
    upstream = cotangent.reshape(row_count, width)
    grad_wide = upstream.astype(jnp.float32)
    d_active = jnp.dot(upstream, back_down.T, preferred_element_type=jnp.float32)
    dw_down = jnp.dot(active.T, upstream, preferred_element_type=jnp.float32)
    d_upper = (d_active * gelu_slope(upper)).astype(jnp.bfloat16)
    dw_up = jnp.dot(second_low.T, d_upper, preferred_element_type=jnp.float32)
    d_second = jnp.dot(d_upper, back_up.T, preferred_element_type=jnp.float32)
    d_resid = grad_wide + norm_back(d_second, second_normed, second_inv, back_gain_rows[1])
    d_resid_low = d_resid.astype(jnp.bfloat16)
    dw_out = jnp.dot(attended.T, d_resid_low, preferred_element_type=jnp.float32)
    d_attended = jnp.dot(d_resid_low, back_out.T, preferred_element_type=jnp.float32).astype(
        jnp.bfloat16
    )
    d_heads = lax.all_to_all(
        d_attended.reshape(img_count, tok_count, width),
        "seq",
        split_axis=2,
        concat_axis=1,
        tiled=True,
    ).reshape(img_count, seq_len, local_heads, HEAD_DIM)

    def run_backward(pieces):
        return backward_image(pieces, block_rows, score_scale)

    dq_heads, dk_heads, dv_heads = lax.map(
        run_backward, (query, keys_full, values_full, key_mask, log_totals, d_heads)
    )
    stacked = jnp.stack(
        [
            dq_heads.reshape(img_count, seq_len, head_cols),
            dk_heads.reshape(img_count, seq_len, head_cols),
            dv_heads.reshape(img_count, seq_len, head_cols),
        ],
        axis=2,
    )
    d_packed = (
        lax.all_to_all(for_sending(stacked), "seq", split_axis=1, concat_axis=3, tiled=True)
        .astype(stacked.dtype)
        .reshape(row_count, 3 * width)
    )
    d_pack_wide = d_packed.astype(jnp.float32)
    dw_qkv = jnp.dot(first_low.T, d_packed, preferred_element_type=jnp.float32)
    d_first = jnp.dot(d_packed, back_qkv.T, preferred_element_type=jnp.float32)
    grad_in = (d_resid + norm_back(d_first, first_normed, first_inv, back_gain_rows[0])).astype(
        jnp.bfloat16
    )
    d_gains = jnp.stack(
        [jnp.sum(d_first * first_normed, axis=0), jnp.sum(d_second * second_normed, axis=0)]
    )
    d_biases = jnp.stack(
        [
            jnp.sum(d_first, axis=0),
            jnp.sum(d_second, axis=0),
            jnp.sum(d_pack_wide[:, :width], axis=0),
            jnp.sum(d_pack_wide[:, 2 * width :], axis=0),
            jnp.sum(d_resid, axis=0),
            jnp.sum(grad_wide, axis=0),
        ]
    )
    d_upbias = jnp.sum(d_upper.astype(jnp.float32), axis=0)
    owned = (
        lax.psum_scatter(dw_qkv, "fsdp", scatter_dimension=0, tiled=True),
        lax.psum_scatter(dw_out, "fsdp", scatter_dimension=0, tiled=True),
        lax.psum_scatter(dw_up, "fsdp", scatter_dimension=0, tiled=True),
        lax.psum_scatter(dw_down, "fsdp", scatter_dimension=1, tiled=True),
        lax.psum_scatter(d_gains, "fsdp", scatter_dimension=1, tiled=True),
        lax.psum_scatter(d_biases, "fsdp", scatter_dimension=1, tiled=True),
        lax.psum_scatter(d_upbias, "fsdp", scatter_dimension=0, tiled=True),
    )
    summed = lax.psum((owned[0], owned[1], owned[2], owned[3], owned[4], owned[5], owned[6]), "seq")
    grad_qkv, grad_proj, grad_up, grad_down, grad_gains, grad_biases, grad_upbias = summed
    return (
        layer_out.reshape(img_count, tok_count, width),
        grad_in.reshape(img_count, tok_count, width),
        grad_qkv,
        grad_proj,
        grad_up,
        grad_down,
        grad_gains,
        grad_biases,
        grad_upbias,
    )


def solution(mesh):
    in_specs = (
        P("fsdp", "seq", None),
        P("fsdp", None),
        P("fsdp", None),
        P("fsdp", None),
        P("fsdp", None),
        P(None, "fsdp"),
        P(None, "fsdp"),
        P(None, "fsdp"),
        P("fsdp"),
        P("fsdp", "seq", None),
    )
    out_specs = (
        P("fsdp", "seq", None),
        P("fsdp", "seq", None),
        P("fsdp", None),
        P("fsdp", None),
        P("fsdp", None),
        P(None, "fsdp"),
        P(None, "fsdp"),
        P(None, "fsdp"),
        P("fsdp"),
    )

    def layer(*args):
        images = args[0].shape[0] // mesh.shape["fsdp"]
        planes = mesh.shape["fsdp"] // 2
        fits = mesh.shape["seq"] == 4 and images == 2 and planes * 2 == mesh.shape["fsdp"] and planes & (planes - 1) == 0
        plan = image_on_chip if fits else heads_over_seq
        return jax.shard_map(plan, mesh=mesh, in_specs=in_specs, out_specs=out_specs, check_vma=False)(*args)

    return layer
```

```python
import functools
import math

import jax
import jax.numpy as jnp
from jax import lax
from jax.experimental import pallas as pl
from jax.experimental.pallas import tpu as pltpu
from jax.sharding import PartitionSpec as P

HEAD_DIM = 72
QBLOCK = 512
EPSILON = 1e-06
NEG_FILL = -1e30
GELU_CUBE = 0.044715
GELU_SCALE = math.sqrt(2.0 / math.pi)
LOG2E = math.log2(math.e)
LANES = 128
F32 = jnp.float32
BF16 = jnp.bfloat16
MIB = 2**20


def attention_forward_kernel(block, heads, qkv_ref, bias_ref, out_ref, probs_ref, inv_ref, by_row, out_rows):
    head = pl.program_id(0)
    width = heads * HEAD_DIM
    seq = qkv_ref.shape[0]

    @pl.when(head == 0)
    def _():
        by_row[...] = qkv_ref[...].astype(F32).T

    def rows(which):
        return pl.ds(pl.multiple_of(which * width + head * HEAD_DIM, 8), HEAD_DIM)

    query = by_row[rows(0), :].astype(BF16)
    keys = by_row[rows(1), :].T.astype(BF16)
    values = by_row[rows(2), :].astype(BF16)
    bias = bias_ref[...]
    for start in range(0, seq, block):
        part = slice(start, start + block)
        scores = jnp.dot(keys, query[:, part], preferred_element_type=F32) * (LOG2E / math.sqrt(HEAD_DIM)) + bias
        top = jnp.max(scores, axis=0, keepdims=True)
        raised = jnp.exp2(scores - top)
        inv = 1.0 / jnp.sum(raised, axis=0, keepdims=True)
        raised_low = raised.astype(BF16)
        probs_ref[0, :, part] = raised_low
        inv_ref[0, :, part] = inv
        out_rows[rows(0), part] = jnp.dot(values, raised_low, preferred_element_type=F32) * inv

    @pl.when(head == heads - 1)
    def _():
        out_ref[:, :width] = out_rows[...].T.astype(BF16)


def attention_forward(qkv, bias, block=QBLOCK):
    seq, triple = qkv.shape
    width = triple // 3
    heads = width // HEAD_DIM
    whole_tiles = -(-width // LANES) * LANES
    return pl.pallas_call(
        functools.partial(attention_forward_kernel, block, heads),
        grid=(heads,),
        in_specs=[pl.BlockSpec((seq, triple), lambda h: (0, 0)), pl.BlockSpec((seq, 1), lambda h: (0, 0))],
        out_specs=[
            pl.BlockSpec((seq, whole_tiles), lambda h: (0, 0)),
            pl.BlockSpec((1, seq, seq), lambda h: (h, 0, 0)),
            pl.BlockSpec((1, 1, seq), lambda h: (h, 0, 0)),
        ],
        out_shape=[
            jax.ShapeDtypeStruct((seq, whole_tiles), BF16),
            jax.ShapeDtypeStruct((heads, seq, seq), BF16),
            jax.ShapeDtypeStruct((heads, 1, seq), F32),
        ],
        scratch_shapes=[pltpu.VMEM((triple, seq), F32), pltpu.VMEM((width, seq), F32)],
        compiler_params=pltpu.CompilerParams(vmem_limit_bytes=48 * MIB),
        cost_estimate=pl.CostEstimate(
            flops=heads * seq * seq, bytes_accessed=seq * triple, transcendentals=0
        ),
    )(qkv, bias)


def attention_backward_kernel(
    block, heads, qkv_ref, d_out_ref, out_ref, probs_ref, inv_ref, grad_ref, by_row, d_rows, o_rows, grad_rows
):
    head = pl.program_id(0)
    width = heads * HEAD_DIM
    seq = qkv_ref.shape[0]
    scale = 1.0 / math.sqrt(HEAD_DIM)

    @pl.when(head == 0)
    def _():
        by_row[...] = qkv_ref[...].astype(F32).T
        d_rows[...] = d_out_ref[...].astype(F32).T
        o_rows[...] = out_ref[:, :width].astype(F32).T

    def rows(which):
        return pl.ds(pl.multiple_of(which * width + head * HEAD_DIM, 8), HEAD_DIM)

    query = by_row[rows(0), :].T.astype(BF16)
    keys = by_row[rows(1), :].astype(BF16)
    values = by_row[rows(2), :].T.astype(BF16)
    d_out = d_rows[rows(0), :]
    inv = inv_ref[0]
    row_dot = jnp.sum(d_out * o_rows[rows(0), :], axis=0, keepdims=True) * inv
    d_scaled = d_out * inv
    d_tokens = d_scaled.T.astype(BF16)
    d_scaled = d_scaled.astype(BF16)
    d_keys = jnp.zeros((seq, HEAD_DIM), F32)
    d_values = jnp.zeros((seq, HEAD_DIM), F32)
    for start in range(0, seq, block):
        part = slice(start, start + block)
        raised = probs_ref[0, :, part]
        d_probs = jnp.dot(values, d_scaled[:, part], preferred_element_type=F32)
        d_scores = (raised.astype(F32) * (d_probs - row_dot[:, part])).astype(BF16)
        d_values += jnp.dot(raised, d_tokens[part, :], preferred_element_type=F32)
        d_keys += jnp.dot(d_scores, query[part, :], preferred_element_type=F32)
        grad_rows[rows(0), part] = jnp.dot(keys, d_scores, preferred_element_type=F32) * scale
    grad_rows[rows(1), :] = d_keys.T * scale
    grad_rows[rows(2), :] = d_values.T

    @pl.when(head == heads - 1)
    def _():
        grad_ref[...] = grad_rows[...].T.astype(BF16)


def attention_backward(qkv, d_out, out, probs, inv, block=QBLOCK):
    seq, triple = qkv.shape
    width = triple // 3
    heads = width // HEAD_DIM
    whole = lambda h: (0, 0)
    return pl.pallas_call(
        functools.partial(attention_backward_kernel, block, heads),
        grid=(heads,),
        in_specs=[
            pl.BlockSpec((seq, triple), whole),
            pl.BlockSpec((seq, width), whole),
            pl.BlockSpec(out.shape, whole),
            pl.BlockSpec((1, seq, seq), lambda h: (h, 0, 0)),
            pl.BlockSpec((1, 1, seq), lambda h: (h, 0, 0)),
        ],
        out_specs=pl.BlockSpec((seq, triple), whole),
        out_shape=jax.ShapeDtypeStruct((seq, triple), BF16),
        scratch_shapes=[
            pltpu.VMEM((triple, seq), F32),
            pltpu.VMEM((width, seq), F32),
            pltpu.VMEM((width, seq), F32),
            pltpu.VMEM((triple, seq), F32),
        ],
        compiler_params=pltpu.CompilerParams(vmem_limit_bytes=56 * MIB),
        cost_estimate=pl.CostEstimate(
            flops=heads * seq * seq, bytes_accessed=seq * triple, transcendentals=0
        ),
    )(qkv, d_out, out, probs, inv)


class Place:
    def __init__(self):
        self.planes = lax.axis_size("fsdp") // 2
        f = lax.axis_index("fsdp")
        k = lax.axis_index("seq")
        self.z, self.c = f // 2, f % 2
        self.k, self.y, self.x = k, k // 2, k % 2
        self.z_lines = [[2 * z + c for z in range(self.planes)] for c in range(2)]
        self.spot = jnp.stack([self.c, self.z, self.y, self.x, self.k]).astype(jnp.int32)

    def send(self, value, to):
        pairs = []
        for z in range(self.planes):
            for c in range(2):
                for y in range(2):
                    for x in range(2):
                        tz, tc, ty, tx = to(z, c, y, x)
                        here, there = ((z * 2 + c) * 2 + y) * 2 + x, ((tz * 2 + tc) * 2 + ty) * 2 + tx
                        if here != there:
                            pairs.append((here, there))
        return lax.ppermute(value, ("fsdp", "seq"), pairs)

    def core(self, value):
        return self.send(value, lambda z, c, y, x: (z, 1 - c, y, x))

    def along_x(self, value):
        return self.send(value, lambda z, c, y, x: (z, c, y, 1 - x))

    def along_y(self, value):
        return self.send(value, lambda z, c, y, x: (z, c, 1 - y, x))

    def across(self, value):
        return self.send(value, lambda z, c, y, x: (z, c, 1 - y, 1 - x))

    def along_z(self, value, step):
        return self.send(value, lambda z, c, y, x: (z ^ step, c, y, x))

    def over_z(self, value):
        return lax.all_to_all(value, "fsdp", 0, 0, axis_index_groups=self.z_lines, tiled=True)

    def turn(self, value, step):
        return self.send(value, lambda z, c, y, x: (z, y, c, x ^ step))


def pick(stack, index):
    return lax.dynamic_index_in_dim(stack, index, 0, keepdims=False)


def in_order(flag, mine, other):
    return jnp.where(flag == 0, jnp.concatenate([mine, other]), jnp.concatenate([other, mine]))


def to_image(place, here, there):
    near, far = place.turn(here, 0), place.turn(there, 1)
    here, near, far = yield here, near, far
    half = jnp.concatenate([jnp.where(place.c == place.y, here, near), far])
    half, other = yield half, place.core(half)
    return half, other


def image_order(place, row):
    blocks = row.reshape(4, -1)
    first = 2 * place.c + place.x
    return jnp.concatenate([pick(blocks, first ^ i) for i in range(4)])


def from_image(place, half):
    size = half.shape[0] // 2
    here = half[:size]
    near, far = place.turn(here, 0), place.turn(half[size:], 1)
    here, near, far = yield here, near, far
    return in_order(place.x, jnp.where(place.c == place.y, here, near)[None], far[None])


def other_order(value):
    size = value.shape[0] // 2
    return jnp.concatenate([value[size:], value[:size]])


def lane_cut(columns):
    return columns // 2 // LANES * LANES


class Transfer:
    def __init__(self, steps):
        self.steps = steps
        self.arrays = next(steps)
        self.result = None


def close_round(*transfers, rest=(), hold=()):
    every = (*transfers, *rest)
    arrays, held = lax.optimization_barrier(([transfer.arrays for transfer in every], list(hold)))
    for transfer, arrived in zip(every, arrays):
        if transfer in rest:
            transfer.arrays = arrived
            continue
        try:
            transfer.arrays = transfer.steps.send(arrived)
        except StopIteration as end:
            transfer.result = end.value
    return held


def spread(place, give, keep, corner=False):
    arrived = place.core(give)
    keep, arrived = yield keep, arrived
    block = in_order(place.c, keep, arrived)
    rows, columns = block.shape[0] // 4, block.shape[1]
    quarters = block.reshape(4, rows, columns)
    wide = jnp.broadcast_to(pick(quarters, place.k)[None], (place.planes, rows, columns))
    quarters, wide = yield quarters, wide
    quarters, planes = yield quarters, place.over_z(wide)
    own = jnp.stack([pick(planes, place.z ^ step) for step in range(1, place.planes)])
    x_part, y_part = place.along_x(own), place.along_y(own)
    quarters, own, x_part, y_part = yield quarters, own, x_part, y_part
    cut = lane_cut(columns)
    if corner:
        far = [place.across(own)]
    else:
        far = [place.along_x(y_part[:, :, :cut]), place.along_y(x_part[:, :, cut:])]
    pieces = yield quarters, own, x_part, y_part, *far
    return pieces


def assemble_kernel(planes, start, size, where, block, own, x_part, y_part, *refs):
    *far, out, sems = refs
    z, k = where[1], where[4]
    here = pl.ds(start, size)
    copies = [(block.at[:, :, here], out.at[pl.ds(z * 4, 4)])]
    for step in range(1, planes):
        at = (z ^ step) * 4
        for turn, part in enumerate((own, x_part, y_part)):
            copies.append((part.at[step - 1, :, here], out.at[at + (k ^ turn)]))
        first = 0
        for part in far:
            low, high = max(start, first), min(start + size, first + part.shape[2])
            if low < high:
                source = part.at[step - 1, :, pl.ds(low - first, high - low)]
                copies.append((source, out.at[at + (k ^ 3), :, pl.ds(low - start, high - low)]))
            first += part.shape[2]
    started = [pltpu.make_async_copy(source, target, sems.at[i]) for i, (source, target) in enumerate(copies)]
    for copy in started:
        copy.start()
    for copy in started:
        copy.wait()


def assemble(place, pieces, start, size):
    planes = place.planes
    rows = pieces[0].shape[1]
    out = pl.pallas_call(
        functools.partial(assemble_kernel, planes, start, size),
        in_specs=[scalar_spec()] + [pl.BlockSpec(memory_space=pltpu.HBM)] * len(pieces),
        out_specs=whole_spec(),
        out_shape=jax.ShapeDtypeStruct((planes * 4, rows, size), BF16),
        scratch_shapes=[pltpu.SemaphoreType.DMA((1 + 5 * (planes - 1),))],
        compiler_params=vmem(12),
        cost_estimate=pl.CostEstimate(flops=0, bytes_accessed=planes * 4 * rows * size, transcendentals=0),
    )(place.spot, *pieces)
    return out.reshape(planes * 4 * rows, size)


def whole_spec():
    return pl.BlockSpec(memory_space=pltpu.VMEM)


def scalar_spec():
    return pl.BlockSpec(memory_space=pltpu.SMEM)


def vmem(mib):
    return pltpu.CompilerParams(vmem_limit_bytes=mib * MIB)


def join_kernel(turn, where, mine, other, out):
    rows, width = out.shape[0], out.shape[1] // 2
    half = rows // 2

    for core in range(2):

        @pl.when(where[0] == core)
        def _():
            out[:, core * width : (core + 1) * width] = mine[:, :width]
            low, high = (1 - core) * width, (2 - core) * width
            if turn:
                out[:half, low:high] = other[half:, :width]
                out[half:, low:high] = other[:half, :width]
            else:
                out[:, low:high] = other[:, :width]


def join(place, mine, other, width, turn):
    return pl.pallas_call(
        functools.partial(join_kernel, turn),
        in_specs=[scalar_spec(), whole_spec(), whole_spec()],
        out_specs=whole_spec(),
        out_shape=jax.ShapeDtypeStruct((mine.shape[0], 2 * width), BF16),
        compiler_params=vmem(24),
    )(place.spot, mine, other)


def weight_grad_kernel(cut, group, rows, pair_count, with_riders, with_sums, where, *refs):
    lefts, rights, refs = refs[:pair_count], refs[pair_count : 2 * pair_count], refs[2 * pair_count :]
    riders, refs = (refs[0], refs[1:]) if with_riders else (None, refs)
    low_keep, low_send, high_keep, high_send, *refs = refs
    sums, refs = (refs[0], refs[1:]) if with_sums else (None, refs)
    total, *turned = refs
    step = pl.program_id(0)
    y, x = where[2], where[3]
    block = group * 4 * rows

    @pl.when(step == 0)
    def _():
        for left, by_row in zip(lefts, turned):
            by_row[...] = left[...].astype(F32).T.astype(BF16)
        if with_sums:
            sums[...] = jnp.broadcast_to(jnp.sum(rights[0][...].astype(F32), axis=0, keepdims=True), sums.shape)

    at = 0
    for right, by_row in zip(rights, turned):
        left = by_row[pl.ds(pl.multiple_of(step * block, 16), block), :]
        columns = right.shape[1]
        for start in range(0, columns, 4 * LANES):
            end = min(start + 4 * LANES, columns)
            total[:, at + start : at + end] = jnp.dot(left, right[:, start:end], preferred_element_type=F32)
        at += columns
    if with_riders:
        total[:, at:] = riders[...]
    for plane in range(group):
        for dy in range(2):
            for dx in range(2):
                row = (plane * 4 + (y ^ dy) * 2 + (x ^ dx)) * rows
                part = total[pl.ds(pl.multiple_of(row, 8), rows), :].astype(BF16)
                (low_send if dx else low_keep)[dy, plane] = part[:, :cut]
                (high_send if dy else high_keep)[dx, plane] = part[:, cut:]


def weight_grad(place, pairs, riders=None, with_sums=False):
    planes = place.planes
    tokens, width = pairs[0][0].shape
    rows = width // planes // 4
    group = 2
    columns = sum(right.shape[1] for _, right in pairs) + (0 if riders is None else riders.shape[1])
    rider_list = [] if riders is None else [riders]
    cut = lane_cut(columns)
    still = lambda shape: pl.BlockSpec(shape, lambda i: (0, 0), pipeline_mode=pl.Buffered(1))
    low = jax.ShapeDtypeStruct((2, planes, rows, cut), BF16)
    high = jax.ShapeDtypeStruct((2, planes, rows, columns - cut), BF16)
    low_spec = pl.BlockSpec((2, group, rows, cut), lambda i: (0, i, 0, 0))
    high_spec = pl.BlockSpec((2, group, rows, columns - cut), lambda i: (0, i, 0, 0))
    sum_shapes = [jax.ShapeDtypeStruct((8, pairs[0][1].shape[1]), F32)] if with_sums else []
    return pl.pallas_call(
        functools.partial(weight_grad_kernel, cut, group, rows, len(pairs), riders is not None, with_sums),
        grid=(planes // group,),
        in_specs=[scalar_spec()]
        + [still(left.shape) for left, _ in pairs]
        + [still(right.shape) for _, right in pairs]
        + [pl.BlockSpec((group * 4 * rows, extra.shape[1]), lambda i: (i, 0)) for extra in rider_list],
        out_specs=[low_spec, low_spec, high_spec, high_spec] + [pl.BlockSpec(s.shape, lambda i: (0, 0)) for s in sum_shapes],
        out_shape=[low, low, high, high] + sum_shapes,
        scratch_shapes=[pltpu.VMEM((group * 4 * rows, columns), F32)] + [pltpu.VMEM((width, tokens), BF16) for _ in pairs],
        compiler_params=vmem(56),
        cost_estimate=pl.CostEstimate(flops=tokens * width, bytes_accessed=width * columns, transcendentals=0),
    )(place.spot, *[left for left, _ in pairs], *[right for _, right in pairs], *rider_list)


def add_first_kernel(low, from_x, high, from_y, low_keep, low_send, high_keep, high_send):
    for kept, arrived, outs in ((low, from_x, (low_keep, low_send)), (high, from_y, (high_keep, high_send))):
        for i, out in enumerate(outs):
            out[...] = (kept[i].astype(F32) + arrived[i].astype(F32)).astype(BF16)


def add_first(low, from_x, high, from_y):
    planes = low.shape[1]
    ins = lambda a: pl.BlockSpec((2, 1, *a.shape[2:]), lambda i: (0, i, 0, 0))
    out = lambda a: pl.BlockSpec((1, *a.shape[2:]), lambda i: (i, 0, 0))
    shape = lambda a: jax.ShapeDtypeStruct(a.shape[1:], BF16)
    return pl.pallas_call(
        add_first_kernel,
        grid=(planes,),
        in_specs=[ins(low), ins(from_x), ins(high), ins(from_y)],
        out_specs=[out(low), out(low), out(high), out(high)],
        out_shape=[shape(low), shape(low), shape(high), shape(high)],
        compiler_params=vmem(24),
    )(low, from_x, high, from_y)


def add_second_kernel(low, from_y, high, from_x, out):
    cut = low.shape[2]
    out[:, :, :cut] = (low[...].astype(F32) + from_y[...].astype(F32)).astype(BF16)
    out[:, :, cut:] = (high[...].astype(F32) + from_x[...].astype(F32)).astype(BF16)


def add_second(low, from_y, high, from_x):
    planes, rows, cut = low.shape
    spec = lambda columns: pl.BlockSpec((1, rows, columns), lambda i: (i, 0, 0))
    rest = high.shape[2]
    return pl.pallas_call(
        add_second_kernel,
        grid=(planes,),
        in_specs=[spec(cut), spec(cut), spec(rest), spec(rest)],
        out_specs=spec(cut + rest),
        out_shape=jax.ShapeDtypeStruct((planes, rows, cut + rest), BF16),
        compiler_params=vmem(24),
    )(low, from_y, high, from_x)


def quarter_of(where, parts, core, side, store):
    mine, x_part, y_part, far_low, far_high = parts
    near, same = where[2] == core, where[3] == side

    @pl.when(near & same)
    def _():
        store(mine[...])

    @pl.when(near & ~same)
    def _():
        store(x_part[...])

    @pl.when(~near & same)
    def _():
        store(y_part[...])

    @pl.when(~near & ~same)
    def _():
        store(jnp.concatenate([far_low[...], far_high[...]], axis=1))


def give_kernel(where, *refs):
    out = refs[-1]
    for core in range(2):

        @pl.when(where[0] != core)
        def _():
            for side in range(2):

                def store(value):
                    out[side] = value

                quarter_of(where, refs[:-1], core, side, store)


def give_rows(place, parts):
    rows, columns = parts[0].shape
    return pl.pallas_call(
        give_kernel,
        in_specs=[scalar_spec()] + [whole_spec()] * 5,
        out_specs=whole_spec(),
        out_shape=jax.ShapeDtypeStruct((2, rows, columns), BF16),
        compiler_params=vmem(24),
    )(place.spot, *parts)


def finish_kernel(write, where, *refs):
    parts, arrived = refs[:5], refs[5]
    outs, kept = refs[6:-1], refs[-1]
    for core in range(2):

        @pl.when(where[0] == core)
        def _():
            for side in range(2):

                def store(value):
                    kept[side] = value

                quarter_of(where, parts, core, side, store)
            halves = [kept[...], arrived[...]]
            if core:
                halves = halves[::-1]
            lower, higher = (half.astype(F32).reshape(-1, half.shape[2]) for half in halves)
            write(lower, higher, *outs)


def lay_kernel(write, where, mine, other, *outs):
    for core in range(2):

        @pl.when(where[0] == core)
        def _():
            halves = [mine[...].astype(F32), other[...].astype(F32)]
            if core:
                halves = halves[::-1]
            write(*halves, *outs)


def lay(place, mine, other, write, shapes):
    return pl.pallas_call(
        functools.partial(lay_kernel, write),
        in_specs=[scalar_spec()] + [whole_spec()] * 2,
        out_specs=[whole_spec()] * len(shapes),
        out_shape=[jax.ShapeDtypeStruct(shape, F32) for shape in shapes],
        compiler_params=vmem(24),
    )(place.spot, mine, other)


def finish(place, pieces, write, shapes):
    *parts, arrived = pieces
    return pl.pallas_call(
        functools.partial(finish_kernel, write),
        in_specs=[scalar_spec()] + [whole_spec()] * 6,
        out_specs=[whole_spec()] * len(shapes),
        out_shape=[jax.ShapeDtypeStruct(shape, F32) for shape in shapes],
        scratch_shapes=[pltpu.VMEM(arrived.shape, BF16)],
        compiler_params=vmem(40),
    )(place.spot, *parts, arrived)


def collect(place, pieces):
    low, low_send, high, high_send = pieces
    low, high, from_x, from_y = yield low, high, place.along_x(low_send), place.along_y(high_send)
    low, low_send, high, high_send = add_first(low, from_x, high, from_y)
    low, high, from_y, from_x = yield low, high, place.along_y(low_send), place.along_x(high_send)
    cut = low.shape[2]
    arrived = yield place.over_z(add_second(low, from_y, high, from_x))
    mine = jnp.sum(arrived.astype(F32), axis=0).astype(BF16)
    mine, x_part, y_part = yield mine, place.along_x(mine), place.along_y(mine)
    far_low, far_high = place.along_x(y_part[:, :cut]), place.along_y(x_part[:, cut:])
    parts = yield mine, x_part, y_part, far_low, far_high
    parts, arrived = yield parts, place.core(give_rows(place, parts))
    return (*parts, arrived)


def vectors_kernel(first, half, where, block, rows, shift):
    turned = block[...].astype(F32).T
    rows[...] = turned[first : first + rows.shape[0]]
    shift[...] = jnp.zeros_like(shift)
    for core in range(2):

        @pl.when(where[0] == core)
        def _():
            for row, at in ((4, 0), (5, 2 * half)):
                shift[:, at : at + half] = turned[first + row : first + row + 1, core * half : (core + 1) * half]


def vectors(place, full, at, count):
    width = full.shape[0]
    tile = at // LANES
    return pl.pallas_call(
        functools.partial(vectors_kernel, at - tile * LANES, width // 2),
        grid=(1,),
        in_specs=[scalar_spec(), pl.BlockSpec((width, LANES), lambda i: (0, tile))],
        out_specs=[pl.BlockSpec((count, width), lambda i: (0, 0)), pl.BlockSpec((1, 3 * width // 2), lambda i: (0, 0))],
        out_shape=[jax.ShapeDtypeStruct((count, width), F32), jax.ShapeDtypeStruct((1, 3 * width // 2), F32)],
        compiler_params=vmem(24),
    )(place.spot, full)


def first_norm_kernel(half, other, gain, shift, tokens, normed, inv_std, low):
    size = half.shape[0]
    for i, part in enumerate((half, other)):
        rows = slice(i * size, (i + 1) * size)
        values = part[...]
        tokens[rows, :] = values
        n, inv_std[rows, :] = normalize(values.astype(F32))
        normed[rows, :] = n.astype(BF16)
        low[rows, :] = (n * gain[...] + shift[...]).astype(BF16)


def first_norm(half, other, gain, shift):
    size, width = half.shape
    wide = jax.ShapeDtypeStruct((2 * size, width), BF16)
    return pl.pallas_call(
        first_norm_kernel,
        in_specs=[whole_spec()] * 4,
        out_specs=[whole_spec()] * 4,
        out_shape=[wide, wide, jax.ShapeDtypeStruct((2 * size, 1), F32), wide],
        compiler_params=vmem(32),
    )(half, other, gain, shift)


def sum_plane(place, rows):
    half = rows.shape[0] // 2
    low, high = rows[:half], rows[half:]
    low, high, from_x, from_y = yield low, high, place.along_x(low), place.along_y(high)
    low, high = add_both(low, from_x, high, from_y)
    low, high, from_y, from_x = yield low, high, place.along_y(low), place.along_x(high)
    return add_both(low, from_y, high, from_x)


def sum_lines(place, partial):
    rows = partial.shape[0] // place.planes
    arrived = yield place.over_z(partial.reshape(place.planes, rows, partial.shape[1]))
    return (yield from sum_plane(place, jnp.sum(arrived.astype(F32), axis=0).astype(BF16)))


def sum_devices(place, value):
    value, other = yield value, place.core(value)
    value = value + other
    value, others = yield value, [place.along_x(value), place.along_y(value), place.across(value)]
    value = functools.reduce(jnp.add, others, value)
    value, others = yield value, [place.along_z(value, step) for step in range(1, place.planes)]
    return functools.reduce(jnp.add, others, value)


def add_both_kernel(low, from_low, high, from_high, low_out, high_out):
    low_out[...] = (low[...].astype(F32) + from_low[...].astype(F32)).astype(BF16)
    high_out[...] = (high[...].astype(F32) + from_high[...].astype(F32)).astype(BF16)


def add_both(low, from_low, high, from_high):
    return pl.pallas_call(
        add_both_kernel,
        in_specs=[whole_spec()] * 4,
        out_specs=[whole_spec()] * 2,
        out_shape=[jax.ShapeDtypeStruct(low.shape, BF16), jax.ShapeDtypeStruct(high.shape, BF16)],
        compiler_params=vmem(16),
    )(low, from_low, high, from_high)


def norm_back_kernel(half, where, part, arrived, upstream, normed, inv_std, gain, low, own_columns, own_rows, sums):
    step = pl.program_id(0)
    e = part[...].astype(F32) + arrived[...].astype(F32)
    n = normed[...].astype(F32)
    scaled = e * gain[...]
    first_mean = jnp.mean(scaled, axis=-1, keepdims=True)
    second_mean = jnp.mean(scaled * n, axis=-1, keepdims=True)
    cot = upstream[...].astype(F32)
    d = cot + inv_std[...] * (scaled - first_mean - n * second_mean)
    d_low = d.astype(BF16)
    low[...] = d_low
    for core in range(2):

        @pl.when(where[0] == core)
        def _():
            own_columns[...] = d_low[:, core * half : (core + 1) * half]

    @pl.when(step < pl.num_programs(0) // 2)
    def _():
        own_rows[...] = d

    rows = jnp.concatenate([jnp.sum(v, axis=0, keepdims=True) for v in (e * n, e, d, cot)] + [jnp.zeros((4, e.shape[1]), F32)])

    @pl.when(step == 0)
    def _():
        sums[...] = rows

    @pl.when(step > 0)
    def _():
        sums[...] += rows


def norm_back_second(place, part, arrived, upstream, normed, inv_std, gain):
    tokens, width = part.shape
    size = tokens // 8
    by_row = pl.BlockSpec((size, width), lambda i: (i, 0))
    turned = pl.BlockSpec((size, width), lambda i: ((i + 4) % 8, 0))
    return pl.pallas_call(
        functools.partial(norm_back_kernel, width // 2),
        grid=(8,),
        in_specs=[
            scalar_spec(),
            by_row,
            turned,
            by_row,
            by_row,
            pl.BlockSpec((size, 1), lambda i: (i, 0)),
            pl.BlockSpec((1, width), lambda i: (0, 0)),
        ],
        out_specs=[
            by_row,
            pl.BlockSpec((size, width // 2), lambda i: (i, 0)),
            pl.BlockSpec((size, width), lambda i: (jnp.minimum(i, 3), 0)),
            pl.BlockSpec((8, width), lambda i: (0, 0)),
        ],
        out_shape=[
            jax.ShapeDtypeStruct((tokens, width), BF16),
            jax.ShapeDtypeStruct((tokens, width // 2), BF16),
            jax.ShapeDtypeStruct((tokens // 2, width), F32),
            jax.ShapeDtypeStruct((8, width), F32),
        ],
        compiler_params=vmem(24),
    )(place.spot, part, arrived, upstream, normed, inv_std, gain)


def norm_back_first_kernel(part, arrived, d_resid, normed, inv_std, gain, grad, sums):
    e = part[...].astype(F32) + arrived[...].astype(F32)
    n = normed[...].astype(F32)
    scaled = e * gain[...]
    first_mean = jnp.mean(scaled, axis=-1, keepdims=True)
    second_mean = jnp.mean(scaled * n, axis=-1, keepdims=True)
    grad[...] = (d_resid[...] + inv_std[...] * (scaled - first_mean - n * second_mean)).astype(BF16)
    rows = jnp.concatenate([jnp.sum(v, axis=0, keepdims=True) for v in (e * n, e)] + [jnp.zeros((6, e.shape[1]), F32)])

    @pl.when(pl.program_id(0) == 0)
    def _():
        sums[...] = rows

    @pl.when(pl.program_id(0) > 0)
    def _():
        sums[...] += rows


def norm_back_first(part, arrived, d_resid, normed, inv_std, gain):
    tokens, width = arrived.shape
    size = tokens // 4
    by_row = pl.BlockSpec((size, width), lambda i: (i, 0))
    return pl.pallas_call(
        norm_back_first_kernel,
        grid=(4,),
        in_specs=[by_row] * 4 + [pl.BlockSpec((size, 1), lambda i: (i, 0)), pl.BlockSpec((1, width), lambda i: (0, 0))],
        out_specs=[by_row, pl.BlockSpec((8, width), lambda i: (0, 0))],
        out_shape=[jax.ShapeDtypeStruct((tokens, width), BF16), jax.ShapeDtypeStruct((8, width), F32)],
        compiler_params=vmem(24),
    )(part, arrived, d_resid, normed, inv_std, gain)


def normalize(values):
    row_mean = jnp.mean(values, axis=-1, keepdims=True)
    centred = values - row_mean
    variance = jnp.mean(centred * centred, axis=-1, keepdims=True)
    inv_std = lax.rsqrt(variance + EPSILON)
    return centred * inv_std, inv_std


def layer_norm(values, gain_row, shift_row):
    row_mean = jnp.mean(values, axis=-1, keepdims=True)
    centred = values - row_mean
    variance = jnp.mean(centred * centred, axis=-1, keepdims=True)
    inv_std = lax.rsqrt(variance + EPSILON)
    normed = centred * inv_std
    return (normed * gain_row + shift_row, normed, inv_std)


def norm_back(upstream, normed, inv_std, gain_row):
    scaled = upstream * gain_row
    first_mean = jnp.mean(scaled, axis=-1, keepdims=True)
    second_mean = jnp.mean(scaled * normed, axis=-1, keepdims=True)
    return inv_std * (scaled - first_mean - normed * second_mean)


def gelu_and_slope(values):
    square = values * values
    tangent = jnp.tanh(GELU_SCALE * values * (1.0 + GELU_CUBE * square))
    half = 0.5 * (1.0 + tangent)
    slope = half + 0.5 * values * (1.0 - tangent * tangent) * GELU_SCALE * (1.0 + 3.0 * GELU_CUBE * square)
    return values * half, slope


def dot(a, b):
    return jnp.dot(a, b, preferred_element_type=F32)


def dot_t(a, b):
    return lax.dot_general(a, b, (((1,), (1,)), ((), ())), preferred_element_type=F32)


def t_dot(a, b):
    return lax.dot_general(a, b, (((0,), (0,)), ((), ())), preferred_element_type=F32)


def image_on_chip(inputs, key_mask, w_qkv, w_out, w_up, w_down, norm_gains, biases, up_bias, cotangent):
    place = Place()
    img_count, tok_count, width = inputs.shape
    shard = w_qkv.shape[0]
    fsdp = lax.axis_size("fsdp")
    half_width = width // 2
    hidden = w_up.shape[1]
    half_hidden = -(-hidden // 2 // LANES) * LANES
    up_shard = up_bias.shape[0]
    up_cols = -(-up_shard // shard)

    def halves_qkv(w):
        return jnp.moveaxis(w.reshape(w.shape[0], 3, 2, half_width), 2, 0).reshape(2, w.shape[0], 3 * half_width)

    def halves_hidden(w):
        padded = jnp.pad(w, ((0, 0), (0, 2 * half_hidden - hidden)))
        return jnp.stack([padded[:, :half_hidden], padded[:, half_hidden:]])

    small = jnp.concatenate(
        [
            norm_gains,
            biases,
            jnp.pad(up_bias, (0, up_cols * shard - up_shard)).reshape(up_cols, shard),
        ]
    )
    n_small = small.shape[0]
    spare = -(3 * half_width) % LANES
    extra = jnp.pad(small.T, ((0, 0), (0, spare - n_small)))
    c = place.c

    qkv_halves = halves_qkv(w_qkv)
    give = jnp.concatenate([pick(qkv_halves, 1 - c), extra], axis=1)
    keep = jnp.concatenate([pick(qkv_halves, c), extra], axis=1)
    qkv = Transfer(spread(place, give, keep))
    tokens_in = Transfer(to_image(place, pick(inputs, place.x), pick(inputs, 1 - place.x)))
    w_out, w_up, w_down, cotangent = close_round(qkv, hold=(w_out, w_up, w_down, cotangent))
    close_round(qkv)

    out_pad = -half_width % LANES
    out_cols = half_width + out_pad
    out_halves = jnp.pad(jnp.moveaxis(w_out.reshape(shard, 2, half_width), 1, 0), ((0, 0), (0, 0), (0, out_pad)))
    down_halves = halves_hidden(w_down.T)
    down = Transfer(spread(place, pick(down_halves, 1 - c), pick(down_halves, c)))
    rest = jnp.concatenate([out_halves, halves_hidden(w_up)], axis=2)
    out_up = Transfer(spread(place, pick(rest, 1 - c), pick(rest, c)))
    upstream_parts = pick(cotangent, place.x), pick(cotangent, 1 - place.x)
    close_round(out_up)
    key_mask, *upstream_parts = close_round(qkv, tokens_in, out_up, hold=(key_mask, *upstream_parts))

    other_mask = place.core(key_mask)
    close_round(qkv, tokens_in)

    live_keys = image_order(place, pick(jnp.where(c == place.y, key_mask, other_mask), place.x))
    mask_bias = jnp.where(live_keys > 0, 0.0, NEG_FILL).astype(F32)[:, None]
    (mask_bias,) = close_round(qkv, out_up, down, hold=(mask_bias,))

    full_first = assemble(place, qkv.result, 0, 3 * half_width + spare)
    full_qkv = full_first[:, : 3 * half_width]
    small_rows, qkv_shift = vectors(place, full_first, 3 * half_width, 16)
    gain_rows, bias_rows = small_rows[:2], small_rows[2:8]
    up_shift = (
        small_rows[8 : 8 + up_cols].reshape(up_cols, fsdp, shard).transpose(1, 0, 2).reshape(fsdp, up_cols * shard)[:, :up_shard]
    ).reshape(hidden)
    up_shift = pick(jnp.pad(up_shift, (0, 2 * half_hidden - hidden)).reshape(2, half_hidden), c)
    tokens, first_normed, first_inv, first_low = first_norm(*tokens_in.result, gain_rows[:1], bias_rows[:1])
    packed = (dot(first_low, full_qkv) + qkv_shift).astype(BF16)
    packed, *upstream_parts = close_round(out_up, down, hold=(packed, *upstream_parts))

    upstream_in = Transfer(to_image(place, *upstream_parts))
    attended_half, raised, inv_total = attention_forward(packed, mask_bias)
    (attended_half,) = close_round(out_up, down, upstream_in, hold=(attended_half,))

    half_out = assemble(place, out_up.result, 0, out_cols)
    full_out = join(place, half_out, place.core(half_out), half_width, False)
    attended = join(place, attended_half, place.core(attended_half), half_width, True)
    residual = tokens.astype(F32) + dot(attended, full_out) + bias_rows[4]
    second_normed, second_inv = normalize(residual)
    second_low = (second_normed * gain_rows[1] + bias_rows[1]).astype(BF16)
    second_normed = second_normed.astype(BF16)
    half = residual.shape[0] // 2
    residual_half = residual[:half]
    (second_low,) = close_round(down, upstream_in, hold=(second_low,))

    full_up = assemble(place, out_up.result, out_cols, half_hidden)
    active, slope = gelu_and_slope(dot(second_low, full_up) + up_shift)
    active, slope = active.astype(BF16), slope.astype(BF16)
    active, slope = close_round(down, hold=(active, slope))

    upstream = jnp.concatenate(upstream_in.result)
    dw_down = t_dot(upstream, active).astype(BF16)
    down_grad = Transfer(sum_lines(place, dw_down))
    full_down = assemble(place, down.result, 0, half_hidden)
    d_active = dot(upstream, full_down)
    d_upper = (d_active * slope.astype(F32)).astype(BF16)
    d_second_part = dot_t(d_upper, full_up).astype(BF16)
    (d_second_part,) = close_round(hold=(d_second_part,))

    d_second_other = place.core(d_second_part)
    *dw_up, d_upper_sums = weight_grad(place, [(second_low, d_upper)], with_sums=True)
    down_part = dot_t(active, full_down).astype(BF16)
    down_sum = down_part[:half].astype(F32) + place.core(down_part[half:]).astype(F32)
    layer_half = (residual_half + down_sum + bias_rows[5]).astype(BF16)
    *dw_up, d_second_other, layer_half = close_round(hold=(*dw_up, d_second_other, layer_half))

    up_grad = Transfer(collect(place, dw_up))
    layer_out = Transfer(from_image(place, layer_half))
    d_resid_low, d_resid_columns, d_resid_half, by_width = norm_back_second(
        place, d_second_part, d_second_other, upstream, second_normed, second_inv, gain_rows[1:]
    )
    d_attended = dot_t(d_resid_low, lax.dynamic_slice_in_dim(full_out, c * half_width, half_width)).astype(BF16)
    d_packed = attention_backward(packed, d_attended, attended_half, raised, inv_total)
    (d_packed,) = close_round(up_grad, layer_out, hold=(d_packed,))

    def own_part(row):
        size = row.shape[0]
        return jnp.where(c == 0, jnp.pad(row, (0, size)), jnp.pad(row, (size, 0)))

    by_hidden = own_part(d_upper_sums[0])[:hidden].reshape(fsdp, up_shard)
    by_hidden = jnp.pad(by_hidden, ((0, 0), (0, up_cols * shard - up_shard))).reshape(fsdp, up_cols, shard)
    by_hidden = by_hidden.transpose(1, 0, 2).reshape(up_cols, width)
    pack_sum = dot(jnp.ones((8, d_packed.shape[0]), BF16), d_packed)[0]
    riders = jnp.concatenate(
        [
            own_part(pack_sum[:half_width])[None],
            own_part(pack_sum[2 * half_width :])[None],
            jnp.where(c == 0, by_width[:4], 0.0),
            by_hidden,
        ]
    )
    riders = jnp.pad(riders, ((0, LANES - riders.shape[0]), (0, 0))).T
    dw_last = weight_grad(place, [(first_low, d_packed), (attended, d_resid_columns)], riders)
    *dw_last, d_packed = close_round(up_grad, down_grad, hold=(*dw_last, d_packed))

    last_grad = Transfer(collect(place, dw_last))
    d_first_part = dot_t(d_packed, full_qkv).astype(BF16)
    grad_half, first_sums = norm_back_first(
        d_first_part,
        place.core(d_first_part[half:]),
        d_resid_half,
        first_normed,
        first_inv,
        gain_rows[:1],
    )
    late = Transfer(sum_devices(place, first_sums[:2].reshape(-1, LANES)))
    (grad_half,) = close_round(up_grad, last_grad, hold=(grad_half,))

    def write_hidden(lower, higher, out):
        out[:, :half_hidden] = lower[:, :half_hidden]
        out[:, half_hidden:] = higher[:, : hidden - half_hidden]

    def write_last(lower, higher, qkv_out, proj, rest):
        for i in range(3):
            here = slice(i * half_width, (i + 1) * half_width)
            qkv_out[:, i * width : i * width + half_width] = lower[:, here]
            qkv_out[:, i * width + half_width : (i + 1) * width] = higher[:, here]
        here = slice(3 * half_width, 4 * half_width)
        proj[:, :half_width] = lower[:, here]
        proj[:, half_width:] = higher[:, here]
        rest[...] = lower[:, 4 * half_width :] + higher[:, 4 * half_width :]

    close_round(up_grad, last_grad, late, down_grad)
    grad_in = Transfer(from_image(place, grad_half))
    close_round(up_grad, last_grad, late, grad_in, down_grad)
    low, high = down_grad.result
    down_own, down_other = jnp.where(c == 0, low, high), place.core(jnp.where(c == 0, high, low))
    grad_in, layer_out, down_other = close_round(
        up_grad, last_grad, late, hold=(grad_in.result, layer_out.result, down_other)
    )
    (grad_down,) = lay(place, down_own, down_other, write_hidden, [(shard, hidden)])
    (grad_up,) = finish(place, up_grad.result, write_hidden, [(shard, hidden)])
    grad_up, grad_down = close_round(last_grad, hold=(grad_up, grad_down))
    close_round(last_grad)
    grad_qkv, grad_proj, rest_sums = finish(
        place, last_grad.result, write_last, [(shard, 3 * width), (shard, width), (shard, LANES)]
    )
    rows = rest_sums[:, : 6 + up_cols].T
    first_rows = lax.dynamic_slice_in_dim(late.result.reshape(2, width), lax.axis_index("fsdp") * shard, shard, axis=1)
    grad_upbias = rows[6:].reshape(up_cols * shard)[:up_shard]
    grad_gains = jnp.stack([first_rows[0], rows[2]])
    grad_biases = jnp.stack([first_rows[1], rows[3], rows[0], rows[1], rows[4], rows[5]])
    return (layer_out, grad_in, grad_qkv, grad_proj, grad_up, grad_down.T, grad_gains, grad_biases, grad_upbias)


def for_sending(array):
    return jax.tree.map(lambda a: a.astype(jnp.bfloat16) if a.dtype == jnp.float32 else a, array)


def gelu_tanh(values):
    return (
        0.5
        * values
        * (1.0 + jnp.tanh(GELU_SCALE * (values + GELU_CUBE * values * values * values)))
    )


def gelu_slope(values):
    tangent = jnp.tanh(GELU_SCALE * (values + GELU_CUBE * values * values * values))
    return 0.5 * (1.0 + tangent) + 0.5 * values * (1.0 - tangent * tangent) * GELU_SCALE * (
        1.0 + 3.0 * GELU_CUBE * values * values
    )


def block_scores(q_block, keys_full, live, score_scale):
    scores = (
        jnp.einsum("qhd,khd->hqk", q_block, keys_full, preferred_element_type=jnp.float32)
        * score_scale
    )
    return jnp.where(live[None, None, :] > 0, scores, NEG_FILL)


def forward_image(pieces, block_rows, score_scale):
    query, keys_full, values_full, live = pieces
    out_parts = []
    total_parts = []
    for start in range(0, query.shape[0], block_rows):
        masked = block_scores(query[start : start + block_rows], keys_full, live, score_scale)
        top_score = jnp.max(masked, axis=-1, keepdims=True)
        log_total = top_score + jnp.log(
            jnp.sum(jnp.exp(masked - top_score), axis=-1, keepdims=True)
        )
        probs_low = jnp.exp(masked - log_total).astype(jnp.bfloat16)
        out_parts.append(
            jnp.einsum(
                "hqk,khd->qhd", probs_low, values_full, preferred_element_type=jnp.float32
            ).astype(jnp.bfloat16)
        )
        total_parts.append(log_total)
    return (jnp.concatenate(out_parts, axis=0), jnp.concatenate(total_parts, axis=1))


def backward_image(pieces, block_rows, score_scale):
    query, keys_full, values_full, live, log_totals, d_heads = pieces
    dq_parts = []
    dk_total = jnp.zeros(keys_full.shape, jnp.float32)
    dv_total = jnp.zeros(values_full.shape, jnp.float32)
    for start in range(0, query.shape[0], block_rows):
        q_block = query[start : start + block_rows]
        d_block = d_heads[start : start + block_rows]
        masked = block_scores(q_block, keys_full, live, score_scale)
        probs = jnp.exp(masked - log_totals[:, start : start + block_rows])
        probs_low = probs.astype(jnp.bfloat16)
        d_probs = jnp.einsum(
            "qhd,khd->hqk", d_block, values_full, preferred_element_type=jnp.float32
        )
        row_dot = jnp.sum(probs * d_probs, axis=-1, keepdims=True)
        d_scores = (probs * (d_probs - row_dot)).astype(jnp.bfloat16)
        dq_block = (
            jnp.einsum("hqk,khd->qhd", d_scores, keys_full, preferred_element_type=jnp.float32)
            * score_scale
        )
        dq_parts.append(dq_block.astype(jnp.bfloat16))
        dk_total = dk_total + jnp.einsum(
            "hqk,qhd->khd", d_scores, q_block, preferred_element_type=jnp.float32
        )
        dv_total = dv_total + jnp.einsum(
            "hqk,qhd->khd", probs_low, d_block, preferred_element_type=jnp.float32
        )
    return (
        jnp.concatenate(dq_parts, axis=0),
        (dk_total * score_scale).astype(jnp.bfloat16),
        dv_total.astype(jnp.bfloat16),
    )


def heads_over_seq(inputs, key_mask, w_qkv, w_out, w_up, w_down, norm_gains, biases, up_bias, cotangent):
    img_count, tok_count, width = inputs.shape
    seq_len = key_mask.shape[1]
    row_count = img_count * tok_count
    head_cols = width // lax.axis_size("seq")
    local_heads = head_cols // HEAD_DIM
    block_rows = min(QBLOCK, seq_len)
    score_scale = 1.0 / math.sqrt(HEAD_DIM)
    gathered = (
        lax.all_gather(w_qkv, "fsdp", axis=0, tiled=True),
        lax.all_gather(w_out, "fsdp", axis=0, tiled=True),
        lax.all_gather(w_up, "fsdp", axis=0, tiled=True),
        lax.all_gather(w_down, "fsdp", axis=1, tiled=True),
        lax.all_gather(norm_gains, "fsdp", axis=1, tiled=True),
        lax.all_gather(biases, "fsdp", axis=1, tiled=True),
        lax.all_gather(up_bias, "fsdp", axis=0, tiled=True),
    )
    full_qkv, full_out, full_up, full_down, full_gains, full_biases, full_upbias = gathered
    gain_rows = full_gains.astype(jnp.float32)
    bias_rows = full_biases.astype(jnp.float32)
    up_shift = full_upbias.astype(jnp.float32)
    qkv_shift = jnp.concatenate([bias_rows[2], jnp.zeros((width,), jnp.float32), bias_rows[3]])
    tok_wide = inputs.reshape(row_count, width).astype(jnp.float32)
    first_out, first_normed, first_inv = layer_norm(tok_wide, gain_rows[0], bias_rows[0])
    first_low = first_out.astype(jnp.bfloat16)
    packed = (jnp.dot(first_low, full_qkv, preferred_element_type=jnp.float32) + qkv_shift).astype(
        jnp.bfloat16
    )
    by_heads = lax.all_to_all(
        packed.reshape(img_count, tok_count, 3, width),
        "seq",
        split_axis=3,
        concat_axis=1,
        tiled=True,
    )
    query = by_heads[:, :, 0].reshape(img_count, seq_len, local_heads, HEAD_DIM)
    keys_full = by_heads[:, :, 1].reshape(img_count, seq_len, local_heads, HEAD_DIM)
    values_full = by_heads[:, :, 2].reshape(img_count, seq_len, local_heads, HEAD_DIM)

    def run_forward(pieces):
        return forward_image(pieces, block_rows, score_scale)

    attended_heads, log_totals = lax.map(run_forward, (query, keys_full, values_full, key_mask))
    attended = lax.all_to_all(
        for_sending(attended_heads.reshape(img_count, seq_len, head_cols)),
        "seq",
        split_axis=1,
        concat_axis=2,
        tiled=True,
    ).reshape(row_count, width)
    residual = (
        tok_wide + jnp.dot(attended, full_out, preferred_element_type=jnp.float32) + bias_rows[4]
    )
    second_out, second_normed, second_inv = layer_norm(residual, gain_rows[1], bias_rows[1])
    second_low = second_out.astype(jnp.bfloat16)
    upper = jnp.dot(second_low, full_up, preferred_element_type=jnp.float32) + up_shift
    active = gelu_tanh(upper).astype(jnp.bfloat16)
    layer_out = (
        residual + jnp.dot(active, full_down, preferred_element_type=jnp.float32) + bias_rows[5]
    ).astype(jnp.bfloat16)
    back_qkv, back_out, back_up, back_down, back_gains, back_biases, back_upbias = gathered
    back_gain_rows = back_gains.astype(jnp.float32)
    upstream = cotangent.reshape(row_count, width)
    grad_wide = upstream.astype(jnp.float32)
    d_active = jnp.dot(upstream, back_down.T, preferred_element_type=jnp.float32)
    dw_down = jnp.dot(active.T, upstream, preferred_element_type=jnp.float32)
    d_upper = (d_active * gelu_slope(upper)).astype(jnp.bfloat16)
    dw_up = jnp.dot(second_low.T, d_upper, preferred_element_type=jnp.float32)
    d_second = jnp.dot(d_upper, back_up.T, preferred_element_type=jnp.float32)
    d_resid = grad_wide + norm_back(d_second, second_normed, second_inv, back_gain_rows[1])
    d_resid_low = d_resid.astype(jnp.bfloat16)
    dw_out = jnp.dot(attended.T, d_resid_low, preferred_element_type=jnp.float32)
    d_attended = jnp.dot(d_resid_low, back_out.T, preferred_element_type=jnp.float32).astype(
        jnp.bfloat16
    )
    d_heads = lax.all_to_all(
        d_attended.reshape(img_count, tok_count, width),
        "seq",
        split_axis=2,
        concat_axis=1,
        tiled=True,
    ).reshape(img_count, seq_len, local_heads, HEAD_DIM)

    def run_backward(pieces):
        return backward_image(pieces, block_rows, score_scale)

    dq_heads, dk_heads, dv_heads = lax.map(
        run_backward, (query, keys_full, values_full, key_mask, log_totals, d_heads)
    )
    stacked = jnp.stack(
        [
            dq_heads.reshape(img_count, seq_len, head_cols),
            dk_heads.reshape(img_count, seq_len, head_cols),
            dv_heads.reshape(img_count, seq_len, head_cols),
        ],
        axis=2,
    )
    d_packed = (
        lax.all_to_all(for_sending(stacked), "seq", split_axis=1, concat_axis=3, tiled=True)
        .astype(stacked.dtype)
        .reshape(row_count, 3 * width)
    )
    d_pack_wide = d_packed.astype(jnp.float32)
    dw_qkv = jnp.dot(first_low.T, d_packed, preferred_element_type=jnp.float32)
    d_first = jnp.dot(d_packed, back_qkv.T, preferred_element_type=jnp.float32)
    grad_in = (d_resid + norm_back(d_first, first_normed, first_inv, back_gain_rows[0])).astype(
        jnp.bfloat16
    )
    d_gains = jnp.stack(
        [jnp.sum(d_first * first_normed, axis=0), jnp.sum(d_second * second_normed, axis=0)]
    )
    d_biases = jnp.stack(
        [
            jnp.sum(d_first, axis=0),
            jnp.sum(d_second, axis=0),
            jnp.sum(d_pack_wide[:, :width], axis=0),
            jnp.sum(d_pack_wide[:, 2 * width :], axis=0),
            jnp.sum(d_resid, axis=0),
            jnp.sum(grad_wide, axis=0),
        ]
    )
    d_upbias = jnp.sum(d_upper.astype(jnp.float32), axis=0)
    owned = (
        lax.psum_scatter(dw_qkv, "fsdp", scatter_dimension=0, tiled=True),
        lax.psum_scatter(dw_out, "fsdp", scatter_dimension=0, tiled=True),
        lax.psum_scatter(dw_up, "fsdp", scatter_dimension=0, tiled=True),
        lax.psum_scatter(dw_down, "fsdp", scatter_dimension=1, tiled=True),
        lax.psum_scatter(d_gains, "fsdp", scatter_dimension=1, tiled=True),
        lax.psum_scatter(d_biases, "fsdp", scatter_dimension=1, tiled=True),
        lax.psum_scatter(d_upbias, "fsdp", scatter_dimension=0, tiled=True),
    )
    summed = lax.psum((owned[0], owned[1], owned[2], owned[3], owned[4], owned[5], owned[6]), "seq")
    grad_qkv, grad_proj, grad_up, grad_down, grad_gains, grad_biases, grad_upbias = summed
    return (
        layer_out.reshape(img_count, tok_count, width),
        grad_in.reshape(img_count, tok_count, width),
        grad_qkv,
        grad_proj,
        grad_up,
        grad_down,
        grad_gains,
        grad_biases,
        grad_upbias,
    )


def solution(mesh):
    in_specs = (
        P("fsdp", "seq", None),
        P("fsdp", None),
        P("fsdp", None),
        P("fsdp", None),
        P("fsdp", None),
        P(None, "fsdp"),
        P(None, "fsdp"),
        P(None, "fsdp"),
        P("fsdp"),
        P("fsdp", "seq", None),
    )
    out_specs = (
        P("fsdp", "seq", None),
        P("fsdp", "seq", None),
        P("fsdp", None),
        P("fsdp", None),
        P("fsdp", None),
        P(None, "fsdp"),
        P(None, "fsdp"),
        P(None, "fsdp"),
        P("fsdp"),
    )

    def layer(*args):
        images = args[0].shape[0] // mesh.shape["fsdp"]
        planes = mesh.shape["fsdp"] // 2
        fits = mesh.shape["seq"] == 4 and images == 2 and planes * 2 == mesh.shape["fsdp"] and planes & (planes - 1) == 0
        plan = image_on_chip if fits else heads_over_seq
        return jax.shard_map(plan, mesh=mesh, in_specs=in_specs, out_specs=out_specs, check_vma=False)(*args)

    return layer
```

```python
import functools
import math

import jax
import jax.numpy as jnp
from jax import lax
from jax.experimental import pallas as pl
from jax.experimental.pallas import tpu as pltpu
from jax.sharding import PartitionSpec as P

HEAD_DIM = 72
QBLOCK = 512
EPSILON = 1e-06
NEG_FILL = -1e30
GELU_CUBE = 0.044715
GELU_SCALE = math.sqrt(2.0 / math.pi)
LOG2E = math.log2(math.e)
LANES = 128
F32 = jnp.float32
BF16 = jnp.bfloat16
MIB = 2**20


def attention_forward_kernel(block, heads, qkv_ref, bias_ref, out_ref, probs_ref, inv_ref, by_row, out_rows):
    head = pl.program_id(0)
    width = heads * HEAD_DIM
    seq = qkv_ref.shape[0]

    @pl.when(head == 0)
    def _():
        by_row[...] = qkv_ref[...].astype(F32).T

    def rows(which):
        return pl.ds(pl.multiple_of(which * width + head * HEAD_DIM, 8), HEAD_DIM)

    query = by_row[rows(0), :].astype(BF16)
    keys = by_row[rows(1), :].T.astype(BF16)
    values = by_row[rows(2), :].astype(BF16)
    bias = bias_ref[...]
    for start in range(0, seq, block):
        part = slice(start, start + block)
        scores = jnp.dot(keys, query[:, part], preferred_element_type=F32) * (LOG2E / math.sqrt(HEAD_DIM)) + bias
        top = jnp.max(scores, axis=0, keepdims=True)
        raised = jnp.exp2(scores - top)
        inv = 1.0 / jnp.sum(raised, axis=0, keepdims=True)
        raised_low = raised.astype(BF16)
        probs_ref[0, :, part] = raised_low
        inv_ref[0, :, part] = inv
        out_rows[rows(0), part] = jnp.dot(values, raised_low, preferred_element_type=F32) * inv

    @pl.when(head == heads - 1)
    def _():
        out_ref[:, :width] = out_rows[...].T.astype(BF16)


def attention_forward(qkv, bias, block=QBLOCK):
    seq, triple = qkv.shape
    width = triple // 3
    heads = width // HEAD_DIM
    whole_tiles = -(-width // LANES) * LANES
    return pl.pallas_call(
        functools.partial(attention_forward_kernel, block, heads),
        grid=(heads,),
        in_specs=[pl.BlockSpec((seq, triple), lambda h: (0, 0)), pl.BlockSpec((seq, 1), lambda h: (0, 0))],
        out_specs=[
            pl.BlockSpec((seq, whole_tiles), lambda h: (0, 0)),
            pl.BlockSpec((1, seq, seq), lambda h: (h, 0, 0)),
            pl.BlockSpec((1, 1, seq), lambda h: (h, 0, 0)),
        ],
        out_shape=[
            jax.ShapeDtypeStruct((seq, whole_tiles), BF16),
            jax.ShapeDtypeStruct((heads, seq, seq), BF16),
            jax.ShapeDtypeStruct((heads, 1, seq), F32),
        ],
        scratch_shapes=[pltpu.VMEM((triple, seq), F32), pltpu.VMEM((width, seq), F32)],
        compiler_params=pltpu.CompilerParams(vmem_limit_bytes=48 * MIB),
        cost_estimate=pl.CostEstimate(
            flops=heads * seq * seq, bytes_accessed=seq * triple, transcendentals=0
        ),
    )(qkv, bias)


def attention_backward_kernel(
    block, heads, qkv_ref, d_out_ref, out_ref, probs_ref, inv_ref, grad_ref, by_row, d_rows, o_rows, grad_rows
):
    head = pl.program_id(0)
    width = heads * HEAD_DIM
    seq = qkv_ref.shape[0]
    scale = 1.0 / math.sqrt(HEAD_DIM)

    @pl.when(head == 0)
    def _():
        by_row[...] = qkv_ref[...].astype(F32).T
        d_rows[...] = d_out_ref[...].astype(F32).T
        o_rows[...] = out_ref[:, :width].astype(F32).T

    def rows(which):
        return pl.ds(pl.multiple_of(which * width + head * HEAD_DIM, 8), HEAD_DIM)

    query = by_row[rows(0), :].T.astype(BF16)
    keys = by_row[rows(1), :].astype(BF16)
    values = by_row[rows(2), :].T.astype(BF16)
    d_out = d_rows[rows(0), :]
    inv = inv_ref[0]
    row_dot = jnp.sum(d_out * o_rows[rows(0), :], axis=0, keepdims=True) * inv
    d_scaled = d_out * inv
    d_tokens = d_scaled.T.astype(BF16)
    d_scaled = d_scaled.astype(BF16)
    d_keys = jnp.zeros((seq, HEAD_DIM), F32)
    d_values = jnp.zeros((seq, HEAD_DIM), F32)
    for start in range(0, seq, block):
        part = slice(start, start + block)
        raised = probs_ref[0, :, part]
        d_probs = jnp.dot(values, d_scaled[:, part], preferred_element_type=F32)
        d_scores = (raised.astype(F32) * (d_probs - row_dot[:, part])).astype(BF16)
        d_values += jnp.dot(raised, d_tokens[part, :], preferred_element_type=F32)
        d_keys += jnp.dot(d_scores, query[part, :], preferred_element_type=F32)
        grad_rows[rows(0), part] = jnp.dot(keys, d_scores, preferred_element_type=F32) * scale
    grad_rows[rows(1), :] = d_keys.T * scale
    grad_rows[rows(2), :] = d_values.T

    @pl.when(head == heads - 1)
    def _():
        grad_ref[...] = grad_rows[...].T.astype(BF16)


def attention_backward(qkv, d_out, out, probs, inv, block=QBLOCK):
    seq, triple = qkv.shape
    width = triple // 3
    heads = width // HEAD_DIM
    whole = lambda h: (0, 0)
    return pl.pallas_call(
        functools.partial(attention_backward_kernel, block, heads),
        grid=(heads,),
        in_specs=[
            pl.BlockSpec((seq, triple), whole),
            pl.BlockSpec((seq, width), whole),
            pl.BlockSpec(out.shape, whole),
            pl.BlockSpec((1, seq, seq), lambda h: (h, 0, 0)),
            pl.BlockSpec((1, 1, seq), lambda h: (h, 0, 0)),
        ],
        out_specs=pl.BlockSpec((seq, triple), whole),
        out_shape=jax.ShapeDtypeStruct((seq, triple), BF16),
        scratch_shapes=[
            pltpu.VMEM((triple, seq), F32),
            pltpu.VMEM((width, seq), F32),
            pltpu.VMEM((width, seq), F32),
            pltpu.VMEM((triple, seq), F32),
        ],
        compiler_params=pltpu.CompilerParams(vmem_limit_bytes=56 * MIB),
        cost_estimate=pl.CostEstimate(
            flops=heads * seq * seq, bytes_accessed=seq * triple, transcendentals=0
        ),
    )(qkv, d_out, out, probs, inv)


class Place:
    def __init__(self):
        self.planes = lax.axis_size("fsdp") // 2
        f = lax.axis_index("fsdp")
        k = lax.axis_index("seq")
        self.z, self.c = f // 2, f % 2
        self.k, self.y, self.x = k, k // 2, k % 2
        self.z_lines = [[2 * z + c for z in range(self.planes)] for c in range(2)]
        self.spot = jnp.stack([self.c, self.z, self.y, self.x, self.k]).astype(jnp.int32)

    def send(self, value, to):
        pairs = []
        for z in range(self.planes):
            for c in range(2):
                for y in range(2):
                    for x in range(2):
                        tz, tc, ty, tx = to(z, c, y, x)
                        here, there = ((z * 2 + c) * 2 + y) * 2 + x, ((tz * 2 + tc) * 2 + ty) * 2 + tx
                        if here != there:
                            pairs.append((here, there))
        return lax.ppermute(value, ("fsdp", "seq"), pairs)

    def core(self, value):
        return self.send(value, lambda z, c, y, x: (z, 1 - c, y, x))

    def along_x(self, value):
        return self.send(value, lambda z, c, y, x: (z, c, y, 1 - x))

    def along_y(self, value):
        return self.send(value, lambda z, c, y, x: (z, c, 1 - y, x))

    def across(self, value):
        return self.send(value, lambda z, c, y, x: (z, c, 1 - y, 1 - x))

    def along_z(self, value, step):
        return self.send(value, lambda z, c, y, x: (z ^ step, c, y, x))

    def over_z(self, value):
        return lax.all_to_all(value, "fsdp", 0, 0, axis_index_groups=self.z_lines, tiled=True)

    def turn(self, value, step):
        return self.send(value, lambda z, c, y, x: (z, y, c, x ^ step))


def pick(stack, index):
    return lax.dynamic_index_in_dim(stack, index, 0, keepdims=False)


def in_order(flag, mine, other):
    return jnp.where(flag == 0, jnp.concatenate([mine, other]), jnp.concatenate([other, mine]))


def to_image(place, here, there):
    near, far = place.turn(here, 0), place.turn(there, 1)
    here, near, far = yield here, near, far
    half = jnp.concatenate([jnp.where(place.c == place.y, here, near), far])
    half, other = yield half, place.core(half)
    return half, other


def image_order(place, row):
    blocks = row.reshape(4, -1)
    first = 2 * place.c + place.x
    return jnp.concatenate([pick(blocks, first ^ i) for i in range(4)])


def from_image(place, half):
    size = half.shape[0] // 2
    here = half[:size]
    near, far = place.turn(here, 0), place.turn(half[size:], 1)
    here, near, far = yield here, near, far
    return in_order(place.x, jnp.where(place.c == place.y, here, near)[None], far[None])


def other_order(value):
    size = value.shape[0] // 2
    return jnp.concatenate([value[size:], value[:size]])


def lane_cut(columns):
    return columns // 2 // LANES * LANES


class Transfer:
    def __init__(self, steps):
        self.steps = steps
        self.arrays = next(steps)
        self.result = None


def close_round(*transfers, rest=(), hold=()):
    every = (*transfers, *rest)
    arrays, held = lax.optimization_barrier(([transfer.arrays for transfer in every], list(hold)))
    for transfer, arrived in zip(every, arrays):
        if transfer in rest:
            transfer.arrays = arrived
            continue
        try:
            transfer.arrays = transfer.steps.send(arrived)
        except StopIteration as end:
            transfer.result = end.value
    return held


def spread(place, give, keep, corner=False):
    arrived = place.core(give)
    keep, arrived = yield keep, arrived
    block = in_order(place.c, keep, arrived)
    rows, columns = block.shape[0] // 4, block.shape[1]
    quarters = block.reshape(4, rows, columns)
    wide = jnp.broadcast_to(pick(quarters, place.k)[None], (place.planes, rows, columns))
    quarters, wide = yield quarters, wide
    quarters, planes = yield quarters, place.over_z(wide)
    own = jnp.stack([pick(planes, place.z ^ step) for step in range(1, place.planes)])
    x_part, y_part = place.along_x(own), place.along_y(own)
    quarters, own, x_part, y_part = yield quarters, own, x_part, y_part
    cut = lane_cut(columns)
    if corner:
        far = [place.across(own)]
    else:
        far = [place.along_x(y_part[:, :, :cut]), place.along_y(x_part[:, :, cut:])]
    pieces = yield quarters, own, x_part, y_part, *far
    return pieces


def assemble_kernel(planes, start, size, where, block, own, x_part, y_part, *refs):
    *far, out, sems = refs
    z, k = where[1], where[4]
    here = pl.ds(start, size)
    copies = [(block.at[:, :, here], out.at[pl.ds(z * 4, 4)])]
    for step in range(1, planes):
        at = (z ^ step) * 4
        for turn, part in enumerate((own, x_part, y_part)):
            copies.append((part.at[step - 1, :, here], out.at[at + (k ^ turn)]))
        first = 0
        for part in far:
            low, high = max(start, first), min(start + size, first + part.shape[2])
            if low < high:
                source = part.at[step - 1, :, pl.ds(low - first, high - low)]
                copies.append((source, out.at[at + (k ^ 3), :, pl.ds(low - start, high - low)]))
            first += part.shape[2]
    started = [pltpu.make_async_copy(source, target, sems.at[i]) for i, (source, target) in enumerate(copies)]
    for copy in started:
        copy.start()
    for copy in started:
        copy.wait()


def assemble(place, pieces, start, size):
    planes = place.planes
    rows = pieces[0].shape[1]
    out = pl.pallas_call(
        functools.partial(assemble_kernel, planes, start, size),
        in_specs=[scalar_spec()] + [pl.BlockSpec(memory_space=pltpu.HBM)] * len(pieces),
        out_specs=whole_spec(),
        out_shape=jax.ShapeDtypeStruct((planes * 4, rows, size), BF16),
        scratch_shapes=[pltpu.SemaphoreType.DMA((1 + 5 * (planes - 1),))],
        compiler_params=vmem(12),
        cost_estimate=pl.CostEstimate(flops=0, bytes_accessed=planes * 4 * rows * size, transcendentals=0),
    )(place.spot, *pieces)
    return out.reshape(planes * 4 * rows, size)


def whole_spec():
    return pl.BlockSpec(memory_space=pltpu.VMEM)


def scalar_spec():
    return pl.BlockSpec(memory_space=pltpu.SMEM)


def vmem(mib):
    return pltpu.CompilerParams(vmem_limit_bytes=mib * MIB)


def weight_grad_kernel(cut, group, rows, pair_count, with_riders, with_sums, where, *refs):
    lefts, rights, refs = refs[:pair_count], refs[pair_count : 2 * pair_count], refs[2 * pair_count :]
    riders, refs = (refs[0], refs[1:]) if with_riders else (None, refs)
    low_keep, low_send, high_keep, high_send, *refs = refs
    sums, refs = (refs[0], refs[1:]) if with_sums else (None, refs)
    total, *turned = refs
    step = pl.program_id(0)
    y, x = where[2], where[3]
    block = group * 4 * rows

    @pl.when(step == 0)
    def _():
        for left, by_row in zip(lefts, turned):
            by_row[...] = left[...].astype(F32).T.astype(BF16)
        if with_sums:
            sums[...] = jnp.broadcast_to(jnp.sum(rights[0][...].astype(F32), axis=0, keepdims=True), sums.shape)

    at = 0
    for right, by_row in zip(rights, turned):
        left = by_row[pl.ds(pl.multiple_of(step * block, 16), block), :]
        columns = right.shape[1]
        for start in range(0, columns, 4 * LANES):
            end = min(start + 4 * LANES, columns)
            total[:, at + start : at + end] = jnp.dot(left, right[:, start:end], preferred_element_type=F32)
        at += columns
    if with_riders:
        total[:, at:] = riders[...]
    for plane in range(group):
        for dy in range(2):
            for dx in range(2):
                row = (plane * 4 + (y ^ dy) * 2 + (x ^ dx)) * rows
                part = total[pl.ds(pl.multiple_of(row, 8), rows), :].astype(BF16)
                (low_send if dx else low_keep)[dy, plane] = part[:, :cut]
                (high_send if dy else high_keep)[dx, plane] = part[:, cut:]


def weight_grad(place, pairs, riders=None, with_sums=False):
    planes = place.planes
    tokens, width = pairs[0][0].shape
    rows = width // planes // 4
    group = planes
    columns = sum(right.shape[1] for _, right in pairs) + (0 if riders is None else riders.shape[1])
    rider_list = [] if riders is None else [riders]
    cut = lane_cut(columns)
    still = lambda shape: pl.BlockSpec(shape, lambda i: (0, 0), pipeline_mode=pl.Buffered(1))
    low = jax.ShapeDtypeStruct((2, planes, rows, cut), BF16)
    high = jax.ShapeDtypeStruct((2, planes, rows, columns - cut), BF16)
    low_spec = pl.BlockSpec((2, group, rows, cut), lambda i: (0, i, 0, 0))
    high_spec = pl.BlockSpec((2, group, rows, columns - cut), lambda i: (0, i, 0, 0))
    sum_shapes = [jax.ShapeDtypeStruct((8, pairs[0][1].shape[1]), F32)] if with_sums else []
    return pl.pallas_call(
        functools.partial(weight_grad_kernel, cut, group, rows, len(pairs), riders is not None, with_sums),
        grid=(planes // group,),
        in_specs=[scalar_spec()]
        + [still(left.shape) for left, _ in pairs]
        + [still(right.shape) for _, right in pairs]
        + [pl.BlockSpec((group * 4 * rows, extra.shape[1]), lambda i: (i, 0)) for extra in rider_list],
        out_specs=[low_spec, low_spec, high_spec, high_spec] + [pl.BlockSpec(s.shape, lambda i: (0, 0)) for s in sum_shapes],
        out_shape=[low, low, high, high] + sum_shapes,
        scratch_shapes=[pltpu.VMEM((group * 4 * rows, columns), F32)] + [pltpu.VMEM((width, tokens), BF16) for _ in pairs],
        compiler_params=vmem(56),
        cost_estimate=pl.CostEstimate(flops=tokens * width, bytes_accessed=width * columns, transcendentals=0),
    )(place.spot, *[left for left, _ in pairs], *[right for _, right in pairs], *rider_list)


def add_first_kernel(low, from_x, high, from_y, low_keep, low_send, high_keep, high_send):
    for kept, arrived, outs in ((low, from_x, (low_keep, low_send)), (high, from_y, (high_keep, high_send))):
        for i, out in enumerate(outs):
            out[...] = (kept[i].astype(F32) + arrived[i].astype(F32)).astype(BF16)


def add_first(low, from_x, high, from_y):
    planes = low.shape[1]
    ins = lambda a: pl.BlockSpec((2, 1, *a.shape[2:]), lambda i: (0, i, 0, 0))
    out = lambda a: pl.BlockSpec((1, *a.shape[2:]), lambda i: (i, 0, 0))
    shape = lambda a: jax.ShapeDtypeStruct(a.shape[1:], BF16)
    return pl.pallas_call(
        add_first_kernel,
        grid=(planes,),
        in_specs=[ins(low), ins(from_x), ins(high), ins(from_y)],
        out_specs=[out(low), out(low), out(high), out(high)],
        out_shape=[shape(low), shape(low), shape(high), shape(high)],
        compiler_params=vmem(24),
    )(low, from_x, high, from_y)


def add_second_kernel(low, from_y, high, from_x, out):
    cut = low.shape[2]
    out[:, :, :cut] = (low[...].astype(F32) + from_y[...].astype(F32)).astype(BF16)
    out[:, :, cut:] = (high[...].astype(F32) + from_x[...].astype(F32)).astype(BF16)


def add_second(low, from_y, high, from_x):
    planes, rows, cut = low.shape
    spec = lambda columns: pl.BlockSpec((1, rows, columns), lambda i: (i, 0, 0))
    rest = high.shape[2]
    return pl.pallas_call(
        add_second_kernel,
        grid=(planes,),
        in_specs=[spec(cut), spec(cut), spec(rest), spec(rest)],
        out_specs=spec(cut + rest),
        out_shape=jax.ShapeDtypeStruct((planes, rows, cut + rest), BF16),
        compiler_params=vmem(24),
    )(low, from_y, high, from_x)


def quarter_of(where, parts, core, side, store):
    mine, x_part, y_part, far_low, far_high = parts
    near, same = where[2] == core, where[3] == side

    @pl.when(near & same)
    def _():
        store(mine[...])

    @pl.when(near & ~same)
    def _():
        store(x_part[...])

    @pl.when(~near & same)
    def _():
        store(y_part[...])

    @pl.when(~near & ~same)
    def _():
        store(jnp.concatenate([far_low[...], far_high[...]], axis=1))


def give_kernel(where, *refs):
    out = refs[-1]
    for core in range(2):

        @pl.when(where[0] != core)
        def _():
            for side in range(2):

                def store(value):
                    out[side] = value

                quarter_of(where, refs[:-1], core, side, store)


def give_rows(place, parts):
    rows, columns = parts[0].shape
    return pl.pallas_call(
        give_kernel,
        in_specs=[scalar_spec()] + [whole_spec()] * 5,
        out_specs=whole_spec(),
        out_shape=jax.ShapeDtypeStruct((2, rows, columns), BF16),
        compiler_params=vmem(24),
    )(place.spot, *parts)


def finish_kernel(write, where, *refs):
    parts, arrived = refs[:5], refs[5]
    outs, kept = refs[6:-1], refs[-1]
    for core in range(2):

        @pl.when(where[0] == core)
        def _():
            for side in range(2):

                def store(value):
                    kept[side] = value

                quarter_of(where, parts, core, side, store)
            halves = [kept[...], arrived[...]]
            if core:
                halves = halves[::-1]
            lower, higher = (half.astype(F32).reshape(-1, half.shape[2]) for half in halves)
            write(lower, higher, *outs)


def finish(place, pieces, write, shapes):
    *parts, arrived = pieces
    return pl.pallas_call(
        functools.partial(finish_kernel, write),
        in_specs=[scalar_spec()] + [whole_spec()] * 6,
        out_specs=[whole_spec()] * len(shapes),
        out_shape=[jax.ShapeDtypeStruct(shape, F32) for shape in shapes],
        scratch_shapes=[pltpu.VMEM(arrived.shape, BF16)],
        compiler_params=vmem(40),
    )(place.spot, *parts, arrived)


def split_rows_kernel(where, arrived, low_keep, low_send, high_keep, high_send, total):
    planes = arrived.shape[0]
    rows, cut = low_keep.shape[2:]
    total[...] = functools.reduce(jnp.add, (arrived[plane].astype(F32) for plane in range(planes)))
    for dy in range(2):
        for dx in range(2):
            row = ((where[2] ^ dy) * 2 + (where[3] ^ dx)) * rows
            part = total[pl.ds(pl.multiple_of(row, 8), rows), :].astype(BF16)
            (low_send if dx else low_keep)[dy, 0] = part[:, :cut]
            (high_send if dy else high_keep)[dx, 0] = part[:, cut:]


def split_rows(place, arrived):
    _, rows, columns = arrived.shape
    cut = lane_cut(columns)
    low = jax.ShapeDtypeStruct((2, 1, rows // 4, cut), BF16)
    high = jax.ShapeDtypeStruct((2, 1, rows // 4, columns - cut), BF16)
    return pl.pallas_call(
        split_rows_kernel,
        in_specs=[scalar_spec(), whole_spec()],
        out_specs=[whole_spec()] * 4,
        out_shape=[low, low, high, high],
        scratch_shapes=[pltpu.VMEM((rows, columns), F32)],
        compiler_params=vmem(24),
    )(place.spot, arrived)


def collect_lines(place, partial):
    arrived = yield place.over_z(partial.reshape(place.planes, -1, partial.shape[1]))
    return (yield from collect(place, split_rows(place, arrived), along_z=False))


def collect(place, pieces, along_z=True):
    low, low_send, high, high_send = pieces
    low, high, from_x, from_y = yield low, high, place.along_x(low_send), place.along_y(high_send)
    low, low_send, high, high_send = add_first(low, from_x, high, from_y)
    low, high, from_y, from_x = yield low, high, place.along_y(low_send), place.along_x(high_send)
    cut = low.shape[2]
    plane = add_second(low, from_y, high, from_x)
    if along_z:
        arrived = yield place.over_z(plane)
        mine = jnp.sum(arrived.astype(F32), axis=0).astype(BF16)
    else:
        mine = plane[0]
    mine, x_part, y_part = yield mine, place.along_x(mine), place.along_y(mine)
    far_low, far_high = place.along_x(y_part[:, :cut]), place.along_y(x_part[:, cut:])
    parts = yield mine, x_part, y_part, far_low, far_high
    parts, arrived = yield parts, place.core(give_rows(place, parts))
    return (*parts, arrived)


def vectors_kernel(first, half, where, block, rows, shift):
    turned = block[...].astype(F32).T
    rows[...] = turned[first : first + rows.shape[0]]
    shift[...] = jnp.zeros_like(shift)
    for core in range(2):

        @pl.when(where[0] == core)
        def _():
            for row, at in ((4, 0), (5, 2 * half)):
                shift[:, at : at + half] = turned[first + row : first + row + 1, core * half : (core + 1) * half]


def vectors(place, full, at, count):
    width = full.shape[0]
    tile = at // LANES
    return pl.pallas_call(
        functools.partial(vectors_kernel, at - tile * LANES, width // 2),
        grid=(1,),
        in_specs=[scalar_spec(), pl.BlockSpec((width, LANES), lambda i: (0, tile))],
        out_specs=[pl.BlockSpec((count, width), lambda i: (0, 0)), pl.BlockSpec((1, 3 * width // 2), lambda i: (0, 0))],
        out_shape=[jax.ShapeDtypeStruct((count, width), F32), jax.ShapeDtypeStruct((1, 3 * width // 2), F32)],
        compiler_params=vmem(24),
    )(place.spot, full)


def norm_and_project_kernel(half, other, weights, shift, rows, tokens, normed, inv_std, low, packed):
    step = pl.program_id(0)
    blocks = pl.num_programs(0) // 2

    @pl.when(step < blocks)
    def _():
        tokens[...] = half[...]

    @pl.when(step >= blocks)
    def _():
        tokens[...] = other[...]

    n, inv_std[...] = normalize(tokens[...].astype(F32))
    normed[...] = n.astype(BF16)
    low[...] = (n * rows[0:1, :] + rows[2:3, :]).astype(BF16)
    columns = packed.shape[1]
    packed[...] = (
        jnp.dot(low[...], weights[:, :columns], preferred_element_type=F32) + shift[...]
    ).astype(BF16)


def norm_and_project(half, other, weights, shift, rows, columns):
    size, width = half.shape
    blocks = 2
    block = size // blocks
    own = lambda shape: pl.BlockSpec(shape, lambda i: (i, 0))
    still = lambda array: pl.BlockSpec(array.shape, lambda i: (0, 0), pipeline_mode=pl.Buffered(1))
    wide = jax.ShapeDtypeStruct((2 * size, width), BF16)
    return pl.pallas_call(
        norm_and_project_kernel,
        grid=(2 * blocks,),
        in_specs=[
            pl.BlockSpec((block, width), lambda i: (jnp.minimum(i, blocks - 1), 0)),
            pl.BlockSpec((block, width), lambda i: (jnp.maximum(i - blocks, 0), 0)),
            still(weights),
            still(shift),
            still(rows),
        ],
        out_specs=[own((block, width)), own((block, width)), own((block, 1)), own((block, width)), own((block, columns))],
        out_shape=[
            wide,
            wide,
            jax.ShapeDtypeStruct((2 * size, 1), F32),
            wide,
            jax.ShapeDtypeStruct((2 * size, columns), BF16),
        ],
        compiler_params=vmem(32),
        cost_estimate=pl.CostEstimate(flops=size * width, bytes_accessed=size * width, transcendentals=0),
    )(half, other, weights, shift, rows)


def project_and_norm_kernel(
    half, where, tokens, mine, other, w_mine, w_other, rows, attended, full_out, residual, normed, inv_std, low
):
    step = pl.program_id(0)
    for core in range(2):
        here, there = slice(core * half, (core + 1) * half), slice((1 - core) * half, (2 - core) * half)

        @pl.when((where[0] == core) & (step == 0))
        def _():
            full_out[:, here] = w_mine[:, :half]
            full_out[:, there] = w_other[:, :half]

        @pl.when(where[0] == core)
        def _():
            attended[:, here] = mine[:, :half]
            attended[:, there] = other[:, :half]

    value = tokens[...].astype(F32) + jnp.dot(attended[...], full_out[...], preferred_element_type=F32) + rows[6:7, :]

    @pl.when(step < pl.num_programs(0) // 2)
    def _():
        residual[...] = value

    n, inv_std[...] = normalize(value)
    normed[...] = n.astype(BF16)
    low[...] = (n * rows[1:2, :] + rows[3:4, :]).astype(BF16)


def project_and_norm(place, tokens, mine, other, w_mine, w_other, rows):
    count, width = tokens.shape
    blocks = 4
    block = count // blocks
    own = lambda columns: pl.BlockSpec((block, columns), lambda i: (i, 0))
    still = lambda shape: pl.BlockSpec(shape, lambda i: (0, 0), pipeline_mode=pl.Buffered(1))
    wide = jax.ShapeDtypeStruct((count, width), BF16)
    return pl.pallas_call(
        functools.partial(project_and_norm_kernel, width // 2),
        grid=(blocks,),
        in_specs=[
            scalar_spec(),
            own(width),
            own(mine.shape[1]),
            pl.BlockSpec((block, other.shape[1]), lambda i: ((i + blocks // 2) % blocks, 0)),
            still(w_mine.shape),
            still(w_other.shape),
            still(rows.shape),
        ],
        out_specs=[
            own(width),
            pl.BlockSpec((width, width), lambda i: (0, 0)),
            pl.BlockSpec((block, width), lambda i: (jnp.minimum(i, blocks // 2 - 1), 0)),
            own(width),
            own(1),
            own(width),
        ],
        out_shape=[
            wide,
            jax.ShapeDtypeStruct((width, width), BF16),
            jax.ShapeDtypeStruct((count // 2, width), F32),
            wide,
            jax.ShapeDtypeStruct((count, 1), F32),
            wide,
        ],
        compiler_params=vmem(32),
        cost_estimate=pl.CostEstimate(flops=count * width, bytes_accessed=count * width, transcendentals=0),
    )(place.spot, tokens, mine, other, w_mine, w_other, rows)


def sum_devices(place, value):
    ways = [place.core, place.along_x, place.along_y]
    step = 1
    while step < place.planes:
        ways.append(functools.partial(place.along_z, step=step))
        step *= 2
    for way in ways:
        value, other = yield value, way(value)
        value = value + other
    return value


def norm_back_kernel(half, where, part, arrived, upstream, normed, inv_std, gain, low, own_columns, own_rows, sums):
    step = pl.program_id(0)
    e = part[...].astype(F32) + arrived[...].astype(F32)
    n = normed[...].astype(F32)
    scaled = e * gain[...]
    first_mean = jnp.mean(scaled, axis=-1, keepdims=True)
    second_mean = jnp.mean(scaled * n, axis=-1, keepdims=True)
    cot = upstream[...].astype(F32)
    d = cot + inv_std[...] * (scaled - first_mean - n * second_mean)
    d_low = d.astype(BF16)
    low[...] = d_low
    for core in range(2):

        @pl.when(where[0] == core)
        def _():
            own_columns[...] = d_low[:, core * half : (core + 1) * half]

    @pl.when(step < pl.num_programs(0) // 2)
    def _():
        own_rows[...] = d

    rows = jnp.concatenate([jnp.sum(v, axis=0, keepdims=True) for v in (e * n, e, d, cot)] + [jnp.zeros((4, e.shape[1]), F32)])

    @pl.when(step == 0)
    def _():
        sums[...] = rows

    @pl.when(step > 0)
    def _():
        sums[...] += rows


def norm_back_second(place, part, arrived, upstream, normed, inv_std, gain):
    tokens, width = part.shape
    size = tokens // 8
    by_row = pl.BlockSpec((size, width), lambda i: (i, 0))
    turned = pl.BlockSpec((size, width), lambda i: ((i + 4) % 8, 0))
    return pl.pallas_call(
        functools.partial(norm_back_kernel, width // 2),
        grid=(8,),
        in_specs=[
            scalar_spec(),
            by_row,
            turned,
            by_row,
            by_row,
            pl.BlockSpec((size, 1), lambda i: (i, 0)),
            pl.BlockSpec((1, width), lambda i: (0, 0)),
        ],
        out_specs=[
            by_row,
            pl.BlockSpec((size, width // 2), lambda i: (i, 0)),
            pl.BlockSpec((size, width), lambda i: (jnp.minimum(i, 3), 0)),
            pl.BlockSpec((8, width), lambda i: (0, 0)),
        ],
        out_shape=[
            jax.ShapeDtypeStruct((tokens, width), BF16),
            jax.ShapeDtypeStruct((tokens, width // 2), BF16),
            jax.ShapeDtypeStruct((tokens // 2, width), F32),
            jax.ShapeDtypeStruct((8, width), F32),
        ],
        compiler_params=vmem(24),
    )(place.spot, part, arrived, upstream, normed, inv_std, gain)


def norm_back_first_kernel(part, arrived, d_resid, normed, inv_std, gain, grad, sums):
    e = part[...].astype(F32) + arrived[...].astype(F32)
    n = normed[...].astype(F32)
    scaled = e * gain[...]
    first_mean = jnp.mean(scaled, axis=-1, keepdims=True)
    second_mean = jnp.mean(scaled * n, axis=-1, keepdims=True)
    grad[...] = (d_resid[...] + inv_std[...] * (scaled - first_mean - n * second_mean)).astype(BF16)
    rows = jnp.concatenate([jnp.sum(v, axis=0, keepdims=True) for v in (e * n, e)] + [jnp.zeros((6, e.shape[1]), F32)])

    @pl.when(pl.program_id(0) == 0)
    def _():
        sums[...] = rows

    @pl.when(pl.program_id(0) > 0)
    def _():
        sums[...] += rows


def norm_back_first(part, arrived, d_resid, normed, inv_std, gain):
    tokens, width = arrived.shape
    size = tokens // 4
    by_row = pl.BlockSpec((size, width), lambda i: (i, 0))
    return pl.pallas_call(
        norm_back_first_kernel,
        grid=(4,),
        in_specs=[by_row] * 4 + [pl.BlockSpec((size, 1), lambda i: (i, 0)), pl.BlockSpec((1, width), lambda i: (0, 0))],
        out_specs=[by_row, pl.BlockSpec((8, width), lambda i: (0, 0))],
        out_shape=[jax.ShapeDtypeStruct((tokens, width), BF16), jax.ShapeDtypeStruct((8, width), F32)],
        compiler_params=vmem(24),
    )(part, arrived, d_resid, normed, inv_std, gain)


def normalize(values):
    row_mean = jnp.mean(values, axis=-1, keepdims=True)
    centred = values - row_mean
    variance = jnp.mean(centred * centred, axis=-1, keepdims=True)
    inv_std = lax.rsqrt(variance + EPSILON)
    return centred * inv_std, inv_std


def layer_norm(values, gain_row, shift_row):
    row_mean = jnp.mean(values, axis=-1, keepdims=True)
    centred = values - row_mean
    variance = jnp.mean(centred * centred, axis=-1, keepdims=True)
    inv_std = lax.rsqrt(variance + EPSILON)
    normed = centred * inv_std
    return (normed * gain_row + shift_row, normed, inv_std)


def norm_back(upstream, normed, inv_std, gain_row):
    scaled = upstream * gain_row
    first_mean = jnp.mean(scaled, axis=-1, keepdims=True)
    second_mean = jnp.mean(scaled * normed, axis=-1, keepdims=True)
    return inv_std * (scaled - first_mean - normed * second_mean)


def gelu_and_slope(values):
    square = values * values
    tangent = jnp.tanh(GELU_SCALE * values * (1.0 + GELU_CUBE * square))
    half = 0.5 * (1.0 + tangent)
    slope = half + 0.5 * values * (1.0 - tangent * tangent) * GELU_SCALE * (1.0 + 3.0 * GELU_CUBE * square)
    return values * half, slope


def dot(a, b):
    return jnp.dot(a, b, preferred_element_type=F32)


def dot_t(a, b):
    return lax.dot_general(a, b, (((1,), (1,)), ((), ())), preferred_element_type=F32)


def t_dot(a, b):
    return lax.dot_general(a, b, (((0,), (0,)), ((), ())), preferred_element_type=F32)


def image_on_chip(inputs, key_mask, w_qkv, w_out, w_up, w_down, norm_gains, biases, up_bias, cotangent):
    place = Place()
    img_count, tok_count, width = inputs.shape
    shard = w_qkv.shape[0]
    fsdp = lax.axis_size("fsdp")
    half_width = width // 2
    hidden = w_up.shape[1]
    half_hidden = -(-hidden // 2 // LANES) * LANES
    up_shard = up_bias.shape[0]
    up_cols = -(-up_shard // shard)

    def halves_qkv(w):
        return jnp.moveaxis(w.reshape(w.shape[0], 3, 2, half_width), 2, 0).reshape(2, w.shape[0], 3 * half_width)

    def halves_hidden(w):
        padded = jnp.pad(w, ((0, 0), (0, 2 * half_hidden - hidden)))
        return jnp.stack([padded[:, :half_hidden], padded[:, half_hidden:]])

    small = jnp.concatenate(
        [
            norm_gains,
            biases,
            jnp.pad(up_bias, (0, up_cols * shard - up_shard)).reshape(up_cols, shard),
        ]
    )
    n_small = small.shape[0]
    spare = -(3 * half_width) % LANES
    extra = jnp.pad(small.T, ((0, 0), (0, spare - n_small)))
    c = place.c

    qkv_halves = halves_qkv(w_qkv)
    give = jnp.concatenate([pick(qkv_halves, 1 - c), extra], axis=1)
    keep = jnp.concatenate([pick(qkv_halves, c), extra], axis=1)
    qkv = Transfer(spread(place, give, keep))
    tokens_in = Transfer(to_image(place, pick(inputs, place.x), pick(inputs, 1 - place.x)))
    w_out, w_up, w_down, cotangent = close_round(qkv, hold=(w_out, w_up, w_down, cotangent))
    close_round(qkv)

    out_pad = -half_width % LANES
    out_cols = half_width + out_pad
    out_halves = jnp.pad(jnp.moveaxis(w_out.reshape(shard, 2, half_width), 1, 0), ((0, 0), (0, 0), (0, out_pad)))
    down_halves = halves_hidden(w_down.T)
    down = Transfer(spread(place, pick(down_halves, 1 - c), pick(down_halves, c)))
    rest = jnp.concatenate([out_halves, halves_hidden(w_up)], axis=2)
    out_up = Transfer(spread(place, pick(rest, 1 - c), pick(rest, c), corner=True))
    upstream_parts = pick(cotangent, place.x), pick(cotangent, 1 - place.x)
    close_round(out_up)
    key_mask, *upstream_parts = close_round(qkv, tokens_in, out_up, hold=(key_mask, *upstream_parts))

    upstream_in = Transfer(to_image(place, *upstream_parts))
    other_mask = place.core(key_mask)
    close_round(qkv, tokens_in)

    live_keys = image_order(place, pick(jnp.where(c == place.y, key_mask, other_mask), place.x))
    mask_bias = jnp.where(live_keys > 0, 0.0, NEG_FILL).astype(F32)[:, None]
    (mask_bias,) = close_round(qkv, out_up, down, upstream_in, hold=(mask_bias,))

    full_first = assemble(place, qkv.result, 0, 3 * half_width + spare)
    full_qkv = full_first[:, : 3 * half_width]
    small_rows, qkv_shift = vectors(place, full_first, 3 * half_width, 16)
    gain_rows, bias_rows = small_rows[:2], small_rows[2:8]
    up_shift = (
        small_rows[8 : 8 + up_cols].reshape(up_cols, fsdp, shard).transpose(1, 0, 2).reshape(fsdp, up_cols * shard)[:, :up_shard]
    ).reshape(hidden)
    up_shift = pick(jnp.pad(up_shift, (0, 2 * half_hidden - hidden)).reshape(2, half_hidden), c)
    tokens, first_normed, first_inv, first_low, packed = norm_and_project(
        *tokens_in.result, full_first, qkv_shift, small_rows, 3 * half_width
    )
    (packed,) = close_round(out_up, down, upstream_in, hold=(packed,))

    attended_half, raised, inv_total = attention_forward(packed, mask_bias)
    (attended_half,) = close_round(out_up, down, hold=(attended_half,))

    half_out = assemble(place, out_up.result, 0, out_cols)
    attended, full_out, residual_half, second_normed, second_inv, second_low = project_and_norm(
        place, tokens, attended_half, place.core(attended_half), half_out, place.core(half_out), small_rows
    )
    half = residual_half.shape[0]
    (second_low,) = close_round(down, hold=(second_low,))

    full_up = assemble(place, out_up.result, out_cols, half_hidden)
    active, slope = gelu_and_slope(dot(second_low, full_up) + up_shift)
    active, slope = active.astype(BF16), slope.astype(BF16)
    active, slope = close_round(down, hold=(active, slope))

    upstream = jnp.concatenate(upstream_in.result)
    dw_down = t_dot(upstream, active).astype(BF16)
    down_grad = Transfer(collect_lines(place, dw_down))
    full_down = assemble(place, down.result, 0, half_hidden)
    d_active = dot(upstream, full_down)
    d_upper = (d_active * slope.astype(F32)).astype(BF16)
    d_second_part = dot_t(d_upper, full_up).astype(BF16)
    (d_second_part,) = close_round(hold=(d_second_part,))

    d_second_other = place.core(d_second_part)
    *dw_up, d_upper_sums = weight_grad(place, [(second_low, d_upper)], with_sums=True)
    down_part = dot_t(active, full_down).astype(BF16)
    down_sum = down_part[:half].astype(F32) + place.core(down_part[half:]).astype(F32)
    layer_half = (residual_half + down_sum + bias_rows[5]).astype(BF16)
    *dw_up, d_second_other, layer_half = close_round(hold=(*dw_up, d_second_other, layer_half))

    up_grad = Transfer(collect(place, dw_up))
    layer_out = Transfer(from_image(place, layer_half))
    d_resid_low, d_resid_columns, d_resid_half, by_width = norm_back_second(
        place, d_second_part, d_second_other, upstream, second_normed, second_inv, gain_rows[1:]
    )
    d_attended = dot_t(d_resid_low, lax.dynamic_slice_in_dim(full_out, c * half_width, half_width)).astype(BF16)
    d_packed = attention_backward(packed, d_attended, attended_half, raised, inv_total)
    (d_packed,) = close_round(up_grad, layer_out, hold=(d_packed,))

    def own_part(row):
        size = row.shape[0]
        return jnp.where(c == 0, jnp.pad(row, (0, size)), jnp.pad(row, (size, 0)))

    by_hidden = own_part(d_upper_sums[0])[:hidden].reshape(fsdp, up_shard)
    by_hidden = jnp.pad(by_hidden, ((0, 0), (0, up_cols * shard - up_shard))).reshape(fsdp, up_cols, shard)
    by_hidden = by_hidden.transpose(1, 0, 2).reshape(up_cols, width)
    pack_sum = dot(jnp.ones((8, d_packed.shape[0]), BF16), d_packed)[0]
    riders = jnp.concatenate(
        [
            own_part(pack_sum[:half_width])[None],
            own_part(pack_sum[2 * half_width :])[None],
            jnp.where(c == 0, by_width[:4], 0.0),
            by_hidden,
        ]
    )
    riders = jnp.pad(riders, ((0, LANES - riders.shape[0]), (0, 0))).T
    dw_last = weight_grad(place, [(first_low, d_packed), (attended, d_resid_columns)], riders)
    *dw_last, d_packed = close_round(up_grad, down_grad, hold=(*dw_last, d_packed))

    last_grad = Transfer(collect(place, dw_last))
    d_first_part = dot_t(d_packed, full_qkv).astype(BF16)
    grad_half, first_sums = norm_back_first(
        d_first_part,
        place.core(d_first_part[half:]),
        d_resid_half,
        first_normed,
        first_inv,
        gain_rows[:1],
    )
    late = Transfer(sum_devices(place, first_sums[:2].reshape(-1, LANES)))
    (grad_half,) = close_round(last_grad, down_grad, hold=(grad_half,))

    def write_hidden(lower, higher, out):
        out[:, :half_hidden] = lower[:, :half_hidden]
        out[:, half_hidden:] = higher[:, : hidden - half_hidden]

    def write_last(lower, higher, qkv_out, proj, rest):
        for i in range(3):
            here = slice(i * half_width, (i + 1) * half_width)
            qkv_out[:, i * width : i * width + half_width] = lower[:, here]
            qkv_out[:, i * width + half_width : (i + 1) * width] = higher[:, here]
        here = slice(3 * half_width, 4 * half_width)
        proj[:, :half_width] = lower[:, here]
        proj[:, half_width:] = higher[:, here]
        rest[...] = lower[:, 4 * half_width :] + higher[:, 4 * half_width :]

    close_round(up_grad, last_grad, down_grad, late)
    grad_in = Transfer(from_image(place, grad_half))
    close_round(up_grad, last_grad, down_grad, late, grad_in)
    grad_in, layer_out = close_round(
        up_grad, last_grad, down_grad, late, hold=(grad_in.result, layer_out.result)
    )
    close_round(up_grad, last_grad, down_grad, late)
    (grad_up,) = finish(place, up_grad.result, write_hidden, [(shard, hidden)])
    (grad_down,) = finish(place, down_grad.result, write_hidden, [(shard, hidden)])
    grad_up, grad_down = close_round(last_grad, late, hold=(grad_up, grad_down))
    grad_qkv, grad_proj, rest_sums = finish(
        place, last_grad.result, write_last, [(shard, 3 * width), (shard, width), (shard, LANES)]
    )
    rows = rest_sums[:, : 6 + up_cols].T
    first_rows = lax.dynamic_slice_in_dim(late.result.reshape(2, width), lax.axis_index("fsdp") * shard, shard, axis=1)
    grad_upbias = rows[6:].reshape(up_cols * shard)[:up_shard]
    grad_gains = jnp.stack([first_rows[0], rows[2]])
    grad_biases = jnp.stack([first_rows[1], rows[3], rows[0], rows[1], rows[4], rows[5]])
    return (layer_out, grad_in, grad_qkv, grad_proj, grad_up, grad_down.T, grad_gains, grad_biases, grad_upbias)


def for_sending(array):
    return jax.tree.map(lambda a: a.astype(jnp.bfloat16) if a.dtype == jnp.float32 else a, array)


def gelu_tanh(values):
    return (
        0.5
        * values
        * (1.0 + jnp.tanh(GELU_SCALE * (values + GELU_CUBE * values * values * values)))
    )


def gelu_slope(values):
    tangent = jnp.tanh(GELU_SCALE * (values + GELU_CUBE * values * values * values))
    return 0.5 * (1.0 + tangent) + 0.5 * values * (1.0 - tangent * tangent) * GELU_SCALE * (
        1.0 + 3.0 * GELU_CUBE * values * values
    )


def block_scores(q_block, keys_full, live, score_scale):
    scores = (
        jnp.einsum("qhd,khd->hqk", q_block, keys_full, preferred_element_type=jnp.float32)
        * score_scale
    )
    return jnp.where(live[None, None, :] > 0, scores, NEG_FILL)


def forward_image(pieces, block_rows, score_scale):
    query, keys_full, values_full, live = pieces
    out_parts = []
    total_parts = []
    for start in range(0, query.shape[0], block_rows):
        masked = block_scores(query[start : start + block_rows], keys_full, live, score_scale)
        top_score = jnp.max(masked, axis=-1, keepdims=True)
        log_total = top_score + jnp.log(
            jnp.sum(jnp.exp(masked - top_score), axis=-1, keepdims=True)
        )
        probs_low = jnp.exp(masked - log_total).astype(jnp.bfloat16)
        out_parts.append(
            jnp.einsum(
                "hqk,khd->qhd", probs_low, values_full, preferred_element_type=jnp.float32
            ).astype(jnp.bfloat16)
        )
        total_parts.append(log_total)
    return (jnp.concatenate(out_parts, axis=0), jnp.concatenate(total_parts, axis=1))


def backward_image(pieces, block_rows, score_scale):
    query, keys_full, values_full, live, log_totals, d_heads = pieces
    dq_parts = []
    dk_total = jnp.zeros(keys_full.shape, jnp.float32)
    dv_total = jnp.zeros(values_full.shape, jnp.float32)
    for start in range(0, query.shape[0], block_rows):
        q_block = query[start : start + block_rows]
        d_block = d_heads[start : start + block_rows]
        masked = block_scores(q_block, keys_full, live, score_scale)
        probs = jnp.exp(masked - log_totals[:, start : start + block_rows])
        probs_low = probs.astype(jnp.bfloat16)
        d_probs = jnp.einsum(
            "qhd,khd->hqk", d_block, values_full, preferred_element_type=jnp.float32
        )
        row_dot = jnp.sum(probs * d_probs, axis=-1, keepdims=True)
        d_scores = (probs * (d_probs - row_dot)).astype(jnp.bfloat16)
        dq_block = (
            jnp.einsum("hqk,khd->qhd", d_scores, keys_full, preferred_element_type=jnp.float32)
            * score_scale
        )
        dq_parts.append(dq_block.astype(jnp.bfloat16))
        dk_total = dk_total + jnp.einsum(
            "hqk,qhd->khd", d_scores, q_block, preferred_element_type=jnp.float32
        )
        dv_total = dv_total + jnp.einsum(
            "hqk,qhd->khd", probs_low, d_block, preferred_element_type=jnp.float32
        )
    return (
        jnp.concatenate(dq_parts, axis=0),
        (dk_total * score_scale).astype(jnp.bfloat16),
        dv_total.astype(jnp.bfloat16),
    )


def heads_over_seq(inputs, key_mask, w_qkv, w_out, w_up, w_down, norm_gains, biases, up_bias, cotangent):
    img_count, tok_count, width = inputs.shape
    seq_len = key_mask.shape[1]
    row_count = img_count * tok_count
    head_cols = width // lax.axis_size("seq")
    local_heads = head_cols // HEAD_DIM
    block_rows = min(QBLOCK, seq_len)
    score_scale = 1.0 / math.sqrt(HEAD_DIM)
    gathered = (
        lax.all_gather(w_qkv, "fsdp", axis=0, tiled=True),
        lax.all_gather(w_out, "fsdp", axis=0, tiled=True),
        lax.all_gather(w_up, "fsdp", axis=0, tiled=True),
        lax.all_gather(w_down, "fsdp", axis=1, tiled=True),
        lax.all_gather(norm_gains, "fsdp", axis=1, tiled=True),
        lax.all_gather(biases, "fsdp", axis=1, tiled=True),
        lax.all_gather(up_bias, "fsdp", axis=0, tiled=True),
    )
    full_qkv, full_out, full_up, full_down, full_gains, full_biases, full_upbias = gathered
    gain_rows = full_gains.astype(jnp.float32)
    bias_rows = full_biases.astype(jnp.float32)
    up_shift = full_upbias.astype(jnp.float32)
    qkv_shift = jnp.concatenate([bias_rows[2], jnp.zeros((width,), jnp.float32), bias_rows[3]])
    tok_wide = inputs.reshape(row_count, width).astype(jnp.float32)
    first_out, first_normed, first_inv = layer_norm(tok_wide, gain_rows[0], bias_rows[0])
    first_low = first_out.astype(jnp.bfloat16)
    packed = (jnp.dot(first_low, full_qkv, preferred_element_type=jnp.float32) + qkv_shift).astype(
        jnp.bfloat16
    )
    by_heads = lax.all_to_all(
        packed.reshape(img_count, tok_count, 3, width),
        "seq",
        split_axis=3,
        concat_axis=1,
        tiled=True,
    )
    query = by_heads[:, :, 0].reshape(img_count, seq_len, local_heads, HEAD_DIM)
    keys_full = by_heads[:, :, 1].reshape(img_count, seq_len, local_heads, HEAD_DIM)
    values_full = by_heads[:, :, 2].reshape(img_count, seq_len, local_heads, HEAD_DIM)

    def run_forward(pieces):
        return forward_image(pieces, block_rows, score_scale)

    attended_heads, log_totals = lax.map(run_forward, (query, keys_full, values_full, key_mask))
    attended = lax.all_to_all(
        for_sending(attended_heads.reshape(img_count, seq_len, head_cols)),
        "seq",
        split_axis=1,
        concat_axis=2,
        tiled=True,
    ).reshape(row_count, width)
    residual = (
        tok_wide + jnp.dot(attended, full_out, preferred_element_type=jnp.float32) + bias_rows[4]
    )
    second_out, second_normed, second_inv = layer_norm(residual, gain_rows[1], bias_rows[1])
    second_low = second_out.astype(jnp.bfloat16)
    upper = jnp.dot(second_low, full_up, preferred_element_type=jnp.float32) + up_shift
    active = gelu_tanh(upper).astype(jnp.bfloat16)
    layer_out = (
        residual + jnp.dot(active, full_down, preferred_element_type=jnp.float32) + bias_rows[5]
    ).astype(jnp.bfloat16)
    back_qkv, back_out, back_up, back_down, back_gains, back_biases, back_upbias = gathered
    back_gain_rows = back_gains.astype(jnp.float32)
    upstream = cotangent.reshape(row_count, width)
    grad_wide = upstream.astype(jnp.float32)
    d_active = jnp.dot(upstream, back_down.T, preferred_element_type=jnp.float32)
    dw_down = jnp.dot(active.T, upstream, preferred_element_type=jnp.float32)
    d_upper = (d_active * gelu_slope(upper)).astype(jnp.bfloat16)
    dw_up = jnp.dot(second_low.T, d_upper, preferred_element_type=jnp.float32)
    d_second = jnp.dot(d_upper, back_up.T, preferred_element_type=jnp.float32)
    d_resid = grad_wide + norm_back(d_second, second_normed, second_inv, back_gain_rows[1])
    d_resid_low = d_resid.astype(jnp.bfloat16)
    dw_out = jnp.dot(attended.T, d_resid_low, preferred_element_type=jnp.float32)
    d_attended = jnp.dot(d_resid_low, back_out.T, preferred_element_type=jnp.float32).astype(
        jnp.bfloat16
    )
    d_heads = lax.all_to_all(
        d_attended.reshape(img_count, tok_count, width),
        "seq",
        split_axis=2,
        concat_axis=1,
        tiled=True,
    ).reshape(img_count, seq_len, local_heads, HEAD_DIM)

    def run_backward(pieces):
        return backward_image(pieces, block_rows, score_scale)

    dq_heads, dk_heads, dv_heads = lax.map(
        run_backward, (query, keys_full, values_full, key_mask, log_totals, d_heads)
    )
    stacked = jnp.stack(
        [
            dq_heads.reshape(img_count, seq_len, head_cols),
            dk_heads.reshape(img_count, seq_len, head_cols),
            dv_heads.reshape(img_count, seq_len, head_cols),
        ],
        axis=2,
    )
    d_packed = (
        lax.all_to_all(for_sending(stacked), "seq", split_axis=1, concat_axis=3, tiled=True)
        .astype(stacked.dtype)
        .reshape(row_count, 3 * width)
    )
    d_pack_wide = d_packed.astype(jnp.float32)
    dw_qkv = jnp.dot(first_low.T, d_packed, preferred_element_type=jnp.float32)
    d_first = jnp.dot(d_packed, back_qkv.T, preferred_element_type=jnp.float32)
    grad_in = (d_resid + norm_back(d_first, first_normed, first_inv, back_gain_rows[0])).astype(
        jnp.bfloat16
    )
    d_gains = jnp.stack(
        [jnp.sum(d_first * first_normed, axis=0), jnp.sum(d_second * second_normed, axis=0)]
    )
    d_biases = jnp.stack(
        [
            jnp.sum(d_first, axis=0),
            jnp.sum(d_second, axis=0),
            jnp.sum(d_pack_wide[:, :width], axis=0),
            jnp.sum(d_pack_wide[:, 2 * width :], axis=0),
            jnp.sum(d_resid, axis=0),
            jnp.sum(grad_wide, axis=0),
        ]
    )
    d_upbias = jnp.sum(d_upper.astype(jnp.float32), axis=0)
    owned = (
        lax.psum_scatter(dw_qkv, "fsdp", scatter_dimension=0, tiled=True),
        lax.psum_scatter(dw_out, "fsdp", scatter_dimension=0, tiled=True),
        lax.psum_scatter(dw_up, "fsdp", scatter_dimension=0, tiled=True),
        lax.psum_scatter(dw_down, "fsdp", scatter_dimension=1, tiled=True),
        lax.psum_scatter(d_gains, "fsdp", scatter_dimension=1, tiled=True),
        lax.psum_scatter(d_biases, "fsdp", scatter_dimension=1, tiled=True),
        lax.psum_scatter(d_upbias, "fsdp", scatter_dimension=0, tiled=True),
    )
    summed = lax.psum((owned[0], owned[1], owned[2], owned[3], owned[4], owned[5], owned[6]), "seq")
    grad_qkv, grad_proj, grad_up, grad_down, grad_gains, grad_biases, grad_upbias = summed
    return (
        layer_out.reshape(img_count, tok_count, width),
        grad_in.reshape(img_count, tok_count, width),
        grad_qkv,
        grad_proj,
        grad_up,
        grad_down,
        grad_gains,
        grad_biases,
        grad_upbias,
    )


def solution(mesh):
    in_specs = (
        P("fsdp", "seq", None),
        P("fsdp", None),
        P("fsdp", None),
        P("fsdp", None),
        P("fsdp", None),
        P(None, "fsdp"),
        P(None, "fsdp"),
        P(None, "fsdp"),
        P("fsdp"),
        P("fsdp", "seq", None),
    )
    out_specs = (
        P("fsdp", "seq", None),
        P("fsdp", "seq", None),
        P("fsdp", None),
        P("fsdp", None),
        P("fsdp", None),
        P(None, "fsdp"),
        P(None, "fsdp"),
        P(None, "fsdp"),
        P("fsdp"),
    )

    def layer(*args):
        images = args[0].shape[0] // mesh.shape["fsdp"]
        planes = mesh.shape["fsdp"] // 2
        fits = mesh.shape["seq"] == 4 and images == 2 and planes * 2 == mesh.shape["fsdp"] and planes & (planes - 1) == 0
        plan = image_on_chip if fits else heads_over_seq
        return jax.shard_map(plan, mesh=mesh, in_specs=in_specs, out_specs=out_specs, check_vma=False)(*args)

    return layer
```

```python
import functools
import math

import jax
import jax.numpy as jnp
from jax import lax
from jax.experimental import pallas as pl
from jax.experimental.pallas import tpu as pltpu
from jax.sharding import PartitionSpec as P

HEAD_DIM = 72
QBLOCK = 512
EPSILON = 1e-06
NEG_FILL = -1e30
GELU_CUBE = 0.044715
GELU_SCALE = math.sqrt(2.0 / math.pi)
LOG2E = math.log2(math.e)
LANES = 128
F32 = jnp.float32
BF16 = jnp.bfloat16
MIB = 2**20


def attention_forward_kernel(block, heads, qkv_ref, bias_ref, out_ref, probs_ref, inv_ref, by_row, out_rows):
    head = pl.program_id(0)
    width = heads * HEAD_DIM
    seq = qkv_ref.shape[0]

    @pl.when(head == 0)
    def _():
        by_row[...] = qkv_ref[...].astype(F32).T

    def rows(which):
        return pl.ds(pl.multiple_of(which * width + head * HEAD_DIM, 8), HEAD_DIM)

    query = by_row[rows(0), :].astype(BF16)
    keys = by_row[rows(1), :].T.astype(BF16)
    values = by_row[rows(2), :].astype(BF16)
    bias = bias_ref[...]
    for start in range(0, seq, block):
        part = slice(start, start + block)
        scores = jnp.dot(keys, query[:, part], preferred_element_type=F32) * (LOG2E / math.sqrt(HEAD_DIM)) + bias
        top = jnp.max(scores, axis=0, keepdims=True)
        raised = jnp.exp2(scores - top)
        inv = 1.0 / jnp.sum(raised, axis=0, keepdims=True)
        raised_low = raised.astype(BF16)
        probs_ref[0, :, part] = raised_low
        inv_ref[0, :, part] = inv
        out_rows[rows(0), part] = jnp.dot(values, raised_low, preferred_element_type=F32) * inv

    @pl.when(head == heads - 1)
    def _():
        out_ref[:, :width] = out_rows[...].T.astype(BF16)


def attention_forward(qkv, bias, block=QBLOCK):
    seq, triple = qkv.shape
    width = triple // 3
    heads = width // HEAD_DIM
    whole_tiles = -(-width // LANES) * LANES
    return pl.pallas_call(
        functools.partial(attention_forward_kernel, block, heads),
        grid=(heads,),
        in_specs=[pl.BlockSpec((seq, triple), lambda h: (0, 0)), pl.BlockSpec((seq, 1), lambda h: (0, 0))],
        out_specs=[
            pl.BlockSpec((seq, whole_tiles), lambda h: (0, 0)),
            pl.BlockSpec((1, seq, seq), lambda h: (h, 0, 0)),
            pl.BlockSpec((1, 1, seq), lambda h: (h, 0, 0)),
        ],
        out_shape=[
            jax.ShapeDtypeStruct((seq, whole_tiles), BF16),
            jax.ShapeDtypeStruct((heads, seq, seq), BF16),
            jax.ShapeDtypeStruct((heads, 1, seq), F32),
        ],
        scratch_shapes=[pltpu.VMEM((triple, seq), F32), pltpu.VMEM((width, seq), F32)],
        compiler_params=pltpu.CompilerParams(vmem_limit_bytes=48 * MIB),
        cost_estimate=pl.CostEstimate(
            flops=heads * seq * seq, bytes_accessed=seq * triple, transcendentals=0
        ),
    )(qkv, bias)


def attention_backward_kernel(
    block, heads, qkv_ref, d_out_ref, out_ref, probs_ref, inv_ref, grad_ref, by_row, d_rows, o_rows, grad_rows
):
    head = pl.program_id(0)
    width = heads * HEAD_DIM
    seq = qkv_ref.shape[0]
    scale = 1.0 / math.sqrt(HEAD_DIM)

    @pl.when(head == 0)
    def _():
        by_row[...] = qkv_ref[...].astype(F32).T
        d_rows[...] = d_out_ref[...].astype(F32).T
        o_rows[...] = out_ref[:, :width].astype(F32).T

    def rows(which):
        return pl.ds(pl.multiple_of(which * width + head * HEAD_DIM, 8), HEAD_DIM)

    query = by_row[rows(0), :].T.astype(BF16)
    keys = by_row[rows(1), :].astype(BF16)
    values = by_row[rows(2), :].T.astype(BF16)
    d_out = d_rows[rows(0), :]
    inv = inv_ref[0]
    row_dot = jnp.sum(d_out * o_rows[rows(0), :], axis=0, keepdims=True) * inv
    d_scaled = d_out * inv
    d_tokens = d_scaled.T.astype(BF16)
    d_scaled = d_scaled.astype(BF16)
    d_keys = jnp.zeros((seq, HEAD_DIM), F32)
    d_values = jnp.zeros((seq, HEAD_DIM), F32)
    for start in range(0, seq, block):
        part = slice(start, start + block)
        raised = probs_ref[0, :, part]
        d_probs = jnp.dot(values, d_scaled[:, part], preferred_element_type=F32)
        d_scores = (raised.astype(F32) * (d_probs - row_dot[:, part])).astype(BF16)
        d_values += jnp.dot(raised, d_tokens[part, :], preferred_element_type=F32)
        d_keys += jnp.dot(d_scores, query[part, :], preferred_element_type=F32)
        grad_rows[rows(0), part] = jnp.dot(keys, d_scores, preferred_element_type=F32) * scale
    grad_rows[rows(1), :] = d_keys.T * scale
    grad_rows[rows(2), :] = d_values.T

    @pl.when(head == heads - 1)
    def _():
        grad_ref[...] = grad_rows[...].T.astype(BF16)


def attention_backward(qkv, d_out, out, probs, inv, block=QBLOCK):
    seq, triple = qkv.shape
    width = triple // 3
    heads = width // HEAD_DIM
    whole = lambda h: (0, 0)
    return pl.pallas_call(
        functools.partial(attention_backward_kernel, block, heads),
        grid=(heads,),
        in_specs=[
            pl.BlockSpec((seq, triple), whole),
            pl.BlockSpec((seq, width), whole),
            pl.BlockSpec(out.shape, whole),
            pl.BlockSpec((1, seq, seq), lambda h: (h, 0, 0)),
            pl.BlockSpec((1, 1, seq), lambda h: (h, 0, 0)),
        ],
        out_specs=pl.BlockSpec((seq, triple), whole),
        out_shape=jax.ShapeDtypeStruct((seq, triple), BF16),
        scratch_shapes=[
            pltpu.VMEM((triple, seq), F32),
            pltpu.VMEM((width, seq), F32),
            pltpu.VMEM((width, seq), F32),
            pltpu.VMEM((triple, seq), F32),
        ],
        compiler_params=pltpu.CompilerParams(vmem_limit_bytes=56 * MIB),
        cost_estimate=pl.CostEstimate(
            flops=heads * seq * seq, bytes_accessed=seq * triple, transcendentals=0
        ),
    )(qkv, d_out, out, probs, inv)


class Place:
    def __init__(self):
        self.planes = lax.axis_size("fsdp") // 2
        f = lax.axis_index("fsdp")
        k = lax.axis_index("seq")
        self.z, self.c = f // 2, f % 2
        self.k, self.y, self.x = k, k // 2, k % 2
        self.z_lines = [[2 * z + c for z in range(self.planes)] for c in range(2)]
        self.spot = jnp.stack([self.c, self.z, self.y, self.x, self.k]).astype(jnp.int32)

    def send(self, value, to):
        pairs = []
        for z in range(self.planes):
            for c in range(2):
                for y in range(2):
                    for x in range(2):
                        tz, tc, ty, tx = to(z, c, y, x)
                        here, there = ((z * 2 + c) * 2 + y) * 2 + x, ((tz * 2 + tc) * 2 + ty) * 2 + tx
                        if here != there:
                            pairs.append((here, there))
        return lax.ppermute(value, ("fsdp", "seq"), pairs)

    def core(self, value):
        return self.send(value, lambda z, c, y, x: (z, 1 - c, y, x))

    def along_x(self, value):
        return self.send(value, lambda z, c, y, x: (z, c, y, 1 - x))

    def along_y(self, value):
        return self.send(value, lambda z, c, y, x: (z, c, 1 - y, x))

    def across(self, value):
        return self.send(value, lambda z, c, y, x: (z, c, 1 - y, 1 - x))

    def along_z(self, value, step):
        return self.send(value, lambda z, c, y, x: (z ^ step, c, y, x))

    def over_z(self, value):
        return lax.all_to_all(value, "fsdp", 0, 0, axis_index_groups=self.z_lines, tiled=True)

    def turn(self, value, step):
        return self.send(value, lambda z, c, y, x: (z, y, c, x ^ step))


def pick(stack, index):
    return lax.dynamic_index_in_dim(stack, index, 0, keepdims=False)


def in_order(flag, mine, other):
    return jnp.where(flag == 0, jnp.concatenate([mine, other]), jnp.concatenate([other, mine]))


def to_image(place, here, there):
    near, far = place.turn(here, 0), place.turn(there, 1)
    here, near, far = yield here, near, far
    half = jnp.concatenate([jnp.where(place.c == place.y, here, near), far])
    half, other = yield half, place.core(half)
    return half, other


def image_order(place, row):
    blocks = row.reshape(4, -1)
    first = 2 * place.c + place.x
    return jnp.concatenate([pick(blocks, first ^ i) for i in range(4)])


def from_image(place, half):
    size = half.shape[0] // 2
    here = half[:size]
    near, far = place.turn(here, 0), place.turn(half[size:], 1)
    here, near, far = yield here, near, far
    return in_order(place.x, jnp.where(place.c == place.y, here, near)[None], far[None])


def other_order(value):
    size = value.shape[0] // 2
    return jnp.concatenate([value[size:], value[:size]])


def lane_cut(columns):
    return columns // 2 // LANES * LANES


class Transfer:
    def __init__(self, steps):
        self.steps = steps
        self.arrays = next(steps)
        self.result = None


def close_round(*transfers, rest=(), hold=()):
    every = (*transfers, *rest)
    arrays, held = lax.optimization_barrier(([transfer.arrays for transfer in every], list(hold)))
    for transfer, arrived in zip(every, arrays):
        if transfer in rest:
            transfer.arrays = arrived
            continue
        try:
            transfer.arrays = transfer.steps.send(arrived)
        except StopIteration as end:
            transfer.result = end.value
    return held


def spread(place, give, keep, corner=False):
    arrived = place.core(give)
    keep, arrived = yield keep, arrived
    block = in_order(place.c, keep, arrived)
    rows, columns = block.shape[0] // 4, block.shape[1]
    quarters = block.reshape(4, rows, columns)
    wide = jnp.broadcast_to(pick(quarters, place.k)[None], (place.planes, rows, columns))
    quarters, wide = yield quarters, wide
    quarters, planes = yield quarters, place.over_z(wide)
    own = jnp.stack([pick(planes, place.z ^ step) for step in range(1, place.planes)])
    x_part, y_part = place.along_x(own), place.along_y(own)
    quarters, own, x_part, y_part = yield quarters, own, x_part, y_part
    cut = lane_cut(columns)
    if corner:
        far = [place.across(own)]
    else:
        far = [place.along_x(y_part[:, :, :cut]), place.along_y(x_part[:, :, cut:])]
    pieces = yield quarters, own, x_part, y_part, *far
    return pieces


def halve_kernel(where, weights, extra, give, keep):
    half = weights.shape[1] // 6
    for core in range(2):

        @pl.when(where[0] == core)
        def _():
            for i in range(3):
                at = slice(i * half, (i + 1) * half)
                for out, side in ((keep, core), (give, 1 - core)):
                    start = (2 * i + side) * half
                    out[:, at] = weights[:, start : start + half]

    for out in (give, keep):
        out[:, 3 * half :] = extra[...]


def halve(place, weights, extra):
    rows = weights.shape[0]
    shape = jax.ShapeDtypeStruct((rows, weights.shape[1] // 2 + extra.shape[1]), BF16)
    return pl.pallas_call(
        halve_kernel,
        in_specs=[scalar_spec()] + [whole_spec()] * 2,
        out_specs=[whole_spec()] * 2,
        out_shape=[shape, shape],
        compiler_params=vmem(16),
    )(place.spot, weights, extra)


def assemble_kernel(planes, start, size, where, block, own, x_part, y_part, *refs):
    *far, out, sems = refs
    z, k = where[1], where[4]
    here = pl.ds(start, size)
    copies = [(block.at[:, :, here], out.at[pl.ds(z * 4, 4)])]
    for step in range(1, planes):
        at = (z ^ step) * 4
        for turn, part in enumerate((own, x_part, y_part)):
            copies.append((part.at[step - 1, :, here], out.at[at + (k ^ turn)]))
        first = 0
        for part in far:
            low, high = max(start, first), min(start + size, first + part.shape[2])
            if low < high:
                source = part.at[step - 1, :, pl.ds(low - first, high - low)]
                copies.append((source, out.at[at + (k ^ 3), :, pl.ds(low - start, high - low)]))
            first += part.shape[2]
    started = [pltpu.make_async_copy(source, target, sems.at[i]) for i, (source, target) in enumerate(copies)]
    for copy in started:
        copy.start()
    for copy in started:
        copy.wait()


def assemble(place, pieces, start, size):
    planes = place.planes
    rows = pieces[0].shape[1]
    out = pl.pallas_call(
        functools.partial(assemble_kernel, planes, start, size),
        in_specs=[scalar_spec()] + [pl.BlockSpec(memory_space=pltpu.HBM)] * len(pieces),
        out_specs=whole_spec(),
        out_shape=jax.ShapeDtypeStruct((planes * 4, rows, size), BF16),
        scratch_shapes=[pltpu.SemaphoreType.DMA((1 + 5 * (planes - 1),))],
        compiler_params=vmem(12),
        cost_estimate=pl.CostEstimate(flops=0, bytes_accessed=planes * 4 * rows * size, transcendentals=0),
    )(place.spot, *pieces)
    return out.reshape(planes * 4 * rows, size)


def whole_spec():
    return pl.BlockSpec(memory_space=pltpu.VMEM)


def scalar_spec():
    return pl.BlockSpec(memory_space=pltpu.SMEM)


def vmem(mib):
    return pltpu.CompilerParams(vmem_limit_bytes=mib * MIB)


def weight_grad_kernel(cut, group, rows, pair_count, with_riders, with_sums, where, *refs):
    lefts, rights, refs = refs[:pair_count], refs[pair_count : 2 * pair_count], refs[2 * pair_count :]
    riders, refs = (refs[0], refs[1:]) if with_riders else (None, refs)
    low_keep, low_send, high_keep, high_send, *refs = refs
    sums, refs = (refs[0], refs[1:]) if with_sums else (None, refs)
    total, *turned = refs
    step = pl.program_id(0)
    y, x = where[2], where[3]
    block = group * 4 * rows

    @pl.when(step == 0)
    def _():
        for left, by_row in zip(lefts, turned):
            by_row[...] = left[...].astype(F32).T.astype(BF16)
        if with_sums:
            sums[...] = jnp.broadcast_to(jnp.sum(rights[0][...].astype(F32), axis=0, keepdims=True), sums.shape)

    at = 0
    for right, by_row in zip(rights, turned):
        left = by_row[pl.ds(pl.multiple_of(step * block, 16), block), :]
        columns = right.shape[1]
        for start in range(0, columns, 4 * LANES):
            end = min(start + 4 * LANES, columns)
            total[:, at + start : at + end] = jnp.dot(left, right[:, start:end], preferred_element_type=F32)
        at += columns
    if with_riders:
        rows_of = riders[...]
        rest = jnp.zeros((total.shape[1] - at - rows_of.shape[0], rows_of.shape[1]), F32)
        total[:, at:] = jnp.concatenate([rows_of, rest], axis=0).T
    for plane in range(group):
        for dy in range(2):
            for dx in range(2):
                row = (plane * 4 + (y ^ dy) * 2 + (x ^ dx)) * rows
                part = total[pl.ds(pl.multiple_of(row, 8), rows), :].astype(BF16)
                (low_send if dx else low_keep)[dy, plane] = part[:, :cut]
                (high_send if dy else high_keep)[dx, plane] = part[:, cut:]


def weight_grad(place, pairs, riders=None, with_sums=False):
    planes = place.planes
    tokens, width = pairs[0][0].shape
    rows = width // planes // 4
    group = planes
    columns = sum(right.shape[1] for _, right in pairs) + (0 if riders is None else LANES)
    rider_list = [] if riders is None else [riders]
    cut = lane_cut(columns)
    still = lambda shape: pl.BlockSpec(shape, lambda i: (0, 0), pipeline_mode=pl.Buffered(1))
    low = jax.ShapeDtypeStruct((2, planes, rows, cut), BF16)
    high = jax.ShapeDtypeStruct((2, planes, rows, columns - cut), BF16)
    low_spec = pl.BlockSpec((2, group, rows, cut), lambda i: (0, i, 0, 0))
    high_spec = pl.BlockSpec((2, group, rows, columns - cut), lambda i: (0, i, 0, 0))
    sum_shapes = [jax.ShapeDtypeStruct((8, pairs[0][1].shape[1]), F32)] if with_sums else []
    return pl.pallas_call(
        functools.partial(weight_grad_kernel, cut, group, rows, len(pairs), riders is not None, with_sums),
        grid=(planes // group,),
        in_specs=[scalar_spec()]
        + [still(left.shape) for left, _ in pairs]
        + [still(right.shape) for _, right in pairs]
        + [pl.BlockSpec((extra.shape[0], group * 4 * rows), lambda i: (0, i)) for extra in rider_list],
        out_specs=[low_spec, low_spec, high_spec, high_spec] + [pl.BlockSpec(s.shape, lambda i: (0, 0)) for s in sum_shapes],
        out_shape=[low, low, high, high] + sum_shapes,
        scratch_shapes=[pltpu.VMEM((group * 4 * rows, columns), F32)] + [pltpu.VMEM((width, tokens), BF16) for _ in pairs],
        compiler_params=vmem(56),
        cost_estimate=pl.CostEstimate(flops=tokens * width, bytes_accessed=width * columns, transcendentals=0),
    )(place.spot, *[left for left, _ in pairs], *[right for _, right in pairs], *rider_list)


def add_first_kernel(low, from_x, high, from_y, low_keep, low_send, high_keep, high_send):
    for kept, arrived, outs in ((low, from_x, (low_keep, low_send)), (high, from_y, (high_keep, high_send))):
        for i, out in enumerate(outs):
            out[...] = (kept[i].astype(F32) + arrived[i].astype(F32)).astype(BF16)


def add_first(low, from_x, high, from_y):
    planes = low.shape[1]
    ins = lambda a: pl.BlockSpec((2, 1, *a.shape[2:]), lambda i: (0, i, 0, 0))
    out = lambda a: pl.BlockSpec((1, *a.shape[2:]), lambda i: (i, 0, 0))
    shape = lambda a: jax.ShapeDtypeStruct(a.shape[1:], BF16)
    return pl.pallas_call(
        add_first_kernel,
        grid=(planes,),
        in_specs=[ins(low), ins(from_x), ins(high), ins(from_y)],
        out_specs=[out(low), out(low), out(high), out(high)],
        out_shape=[shape(low), shape(low), shape(high), shape(high)],
        compiler_params=vmem(24),
    )(low, from_x, high, from_y)


def add_second_kernel(low, from_y, high, from_x, out):
    cut = low.shape[2]
    out[:, :, :cut] = (low[...].astype(F32) + from_y[...].astype(F32)).astype(BF16)
    out[:, :, cut:] = (high[...].astype(F32) + from_x[...].astype(F32)).astype(BF16)


def add_second(low, from_y, high, from_x):
    planes, rows, cut = low.shape
    spec = lambda columns: pl.BlockSpec((1, rows, columns), lambda i: (i, 0, 0))
    rest = high.shape[2]
    return pl.pallas_call(
        add_second_kernel,
        grid=(planes,),
        in_specs=[spec(cut), spec(cut), spec(rest), spec(rest)],
        out_specs=spec(cut + rest),
        out_shape=jax.ShapeDtypeStruct((planes, rows, cut + rest), BF16),
        compiler_params=vmem(24),
    )(low, from_y, high, from_x)


def quarter_of(where, parts, core, side, store):
    mine, x_part, y_part, far_low, far_high = parts
    near, same = where[2] == core, where[3] == side

    @pl.when(near & same)
    def _():
        store(mine[...])

    @pl.when(near & ~same)
    def _():
        store(x_part[...])

    @pl.when(~near & same)
    def _():
        store(y_part[...])

    @pl.when(~near & ~same)
    def _():
        store(jnp.concatenate([far_low[...], far_high[...]], axis=1))


def give_kernel(where, *refs):
    out = refs[-1]
    for core in range(2):

        @pl.when(where[0] != core)
        def _():
            for side in range(2):

                def store(value):
                    out[side] = value

                quarter_of(where, refs[:-1], core, side, store)


def give_rows(place, parts):
    rows, columns = parts[0].shape
    return pl.pallas_call(
        give_kernel,
        in_specs=[scalar_spec()] + [whole_spec()] * 5,
        out_specs=whole_spec(),
        out_shape=jax.ShapeDtypeStruct((2, rows, columns), BF16),
        compiler_params=vmem(24),
    )(place.spot, *parts)


def finish_kernel(write, where, *refs):
    parts, arrived = refs[:5], refs[5]
    outs, kept = refs[6:-1], refs[-1]
    for core in range(2):

        @pl.when(where[0] == core)
        def _():
            for side in range(2):

                def store(value):
                    kept[side] = value

                quarter_of(where, parts, core, side, store)
            halves = [kept[...], arrived[...]]
            if core:
                halves = halves[::-1]
            lower, higher = (half.astype(F32).reshape(-1, half.shape[2]) for half in halves)
            write(lower, higher, *outs)


def finish(place, pieces, write, shapes):
    *parts, arrived = pieces
    return pl.pallas_call(
        functools.partial(finish_kernel, write),
        in_specs=[scalar_spec()] + [whole_spec()] * 6,
        out_specs=[whole_spec()] * len(shapes),
        out_shape=[jax.ShapeDtypeStruct(shape, F32) for shape in shapes],
        scratch_shapes=[pltpu.VMEM(arrived.shape, BF16)],
        compiler_params=vmem(40),
    )(place.spot, *parts, arrived)


def split_rows_kernel(where, arrived, low_keep, low_send, high_keep, high_send, total):
    planes = arrived.shape[0]
    rows, cut = low_keep.shape[2:]
    total[...] = functools.reduce(jnp.add, (arrived[plane].astype(F32) for plane in range(planes)))
    for dy in range(2):
        for dx in range(2):
            row = ((where[2] ^ dy) * 2 + (where[3] ^ dx)) * rows
            part = total[pl.ds(pl.multiple_of(row, 8), rows), :].astype(BF16)
            (low_send if dx else low_keep)[dy, 0] = part[:, :cut]
            (high_send if dy else high_keep)[dx, 0] = part[:, cut:]


def split_rows(place, arrived):
    _, rows, columns = arrived.shape
    cut = lane_cut(columns)
    low = jax.ShapeDtypeStruct((2, 1, rows // 4, cut), BF16)
    high = jax.ShapeDtypeStruct((2, 1, rows // 4, columns - cut), BF16)
    return pl.pallas_call(
        split_rows_kernel,
        in_specs=[scalar_spec(), whole_spec()],
        out_specs=[whole_spec()] * 4,
        out_shape=[low, low, high, high],
        scratch_shapes=[pltpu.VMEM((rows, columns), F32)],
        compiler_params=vmem(24),
    )(place.spot, arrived)


def collect_lines(place, partial):
    arrived = yield place.over_z(partial.reshape(place.planes, -1, partial.shape[1]))
    return (yield from collect(place, split_rows(place, arrived), along_z=False))


def collect(place, pieces, along_z=True):
    low, low_send, high, high_send = pieces
    low, high, from_x, from_y = yield low, high, place.along_x(low_send), place.along_y(high_send)
    low, low_send, high, high_send = add_first(low, from_x, high, from_y)
    low, high, from_y, from_x = yield low, high, place.along_y(low_send), place.along_x(high_send)
    cut = low.shape[2]
    plane = add_second(low, from_y, high, from_x)
    if along_z:
        arrived = yield place.over_z(plane)
        mine = jnp.sum(arrived.astype(F32), axis=0).astype(BF16)
    else:
        mine = plane[0]
    mine, x_part, y_part = yield mine, place.along_x(mine), place.along_y(mine)
    far_low, far_high = place.along_x(y_part[:, :cut]), place.along_y(x_part[:, cut:])
    parts = yield mine, x_part, y_part, far_low, far_high
    parts, arrived = yield parts, place.core(give_rows(place, parts))
    return (*parts, arrived)


def vectors_kernel(first, half, where, block, rows, shift):
    turned = block[...].astype(F32).T
    rows[...] = turned[first : first + rows.shape[0]]
    shift[...] = jnp.zeros_like(shift)
    for core in range(2):

        @pl.when(where[0] == core)
        def _():
            for row, at in ((4, 0), (5, 2 * half)):
                shift[:, at : at + half] = turned[first + row : first + row + 1, core * half : (core + 1) * half]


def vectors(place, full, at, count):
    width = full.shape[0]
    tile = at // LANES
    return pl.pallas_call(
        functools.partial(vectors_kernel, at - tile * LANES, width // 2),
        grid=(1,),
        in_specs=[scalar_spec(), pl.BlockSpec((width, LANES), lambda i: (0, tile))],
        out_specs=[pl.BlockSpec((count, width), lambda i: (0, 0)), pl.BlockSpec((1, 3 * width // 2), lambda i: (0, 0))],
        out_shape=[jax.ShapeDtypeStruct((count, width), F32), jax.ShapeDtypeStruct((1, 3 * width // 2), F32)],
        compiler_params=vmem(24),
    )(place.spot, full)


def norm_and_project_kernel(half, other, weights, shift, rows, tokens, normed, inv_std, low, packed):
    step = pl.program_id(0)
    blocks = pl.num_programs(0) // 2

    @pl.when(step < blocks)
    def _():
        tokens[...] = half[...]

    @pl.when(step >= blocks)
    def _():
        tokens[...] = other[...]

    n, inv_std[...] = normalize(tokens[...].astype(F32))
    normed[...] = n.astype(BF16)
    low[...] = (n * rows[0:1, :] + rows[2:3, :]).astype(BF16)
    columns = packed.shape[1]
    packed[...] = (
        jnp.dot(low[...], weights[:, :columns], preferred_element_type=F32) + shift[...]
    ).astype(BF16)


def norm_and_project(half, other, weights, shift, rows, columns):
    size, width = half.shape
    blocks = 2
    block = size // blocks
    own = lambda shape: pl.BlockSpec(shape, lambda i: (i, 0))
    still = lambda array: pl.BlockSpec(array.shape, lambda i: (0, 0), pipeline_mode=pl.Buffered(1))
    wide = jax.ShapeDtypeStruct((2 * size, width), BF16)
    return pl.pallas_call(
        norm_and_project_kernel,
        grid=(2 * blocks,),
        in_specs=[
            pl.BlockSpec((block, width), lambda i: (jnp.minimum(i, blocks - 1), 0)),
            pl.BlockSpec((block, width), lambda i: (jnp.maximum(i - blocks, 0), 0)),
            still(weights),
            still(shift),
            still(rows),
        ],
        out_specs=[own((block, width)), own((block, width)), own((block, 1)), own((block, width)), own((block, columns))],
        out_shape=[
            wide,
            wide,
            jax.ShapeDtypeStruct((2 * size, 1), F32),
            wide,
            jax.ShapeDtypeStruct((2 * size, columns), BF16),
        ],
        compiler_params=vmem(32),
        cost_estimate=pl.CostEstimate(flops=size * width, bytes_accessed=size * width, transcendentals=0),
    )(half, other, weights, shift, rows)


def project_and_norm_kernel(
    half, where, tokens, mine, other, w_mine, w_other, rows, attended, full_out, residual, normed, inv_std, low
):
    step = pl.program_id(0)
    for core in range(2):
        here, there = slice(core * half, (core + 1) * half), slice((1 - core) * half, (2 - core) * half)

        @pl.when((where[0] == core) & (step == 0))
        def _():
            full_out[:, here] = w_mine[:, :half]
            full_out[:, there] = w_other[:, :half]

        @pl.when(where[0] == core)
        def _():
            attended[:, here] = mine[:, :half]
            attended[:, there] = other[:, :half]

    value = tokens[...].astype(F32) + jnp.dot(attended[...], full_out[...], preferred_element_type=F32) + rows[6:7, :]

    @pl.when(step < pl.num_programs(0) // 2)
    def _():
        residual[...] = value

    n, inv_std[...] = normalize(value)
    normed[...] = n.astype(BF16)
    low[...] = (n * rows[1:2, :] + rows[3:4, :]).astype(BF16)


def project_and_norm(place, tokens, mine, other, w_mine, w_other, rows):
    count, width = tokens.shape
    blocks = 4
    block = count // blocks
    own = lambda columns: pl.BlockSpec((block, columns), lambda i: (i, 0))
    still = lambda shape: pl.BlockSpec(shape, lambda i: (0, 0), pipeline_mode=pl.Buffered(1))
    wide = jax.ShapeDtypeStruct((count, width), BF16)
    return pl.pallas_call(
        functools.partial(project_and_norm_kernel, width // 2),
        grid=(blocks,),
        in_specs=[
            scalar_spec(),
            own(width),
            own(mine.shape[1]),
            pl.BlockSpec((block, other.shape[1]), lambda i: ((i + blocks // 2) % blocks, 0)),
            still(w_mine.shape),
            still(w_other.shape),
            still(rows.shape),
        ],
        out_specs=[
            own(width),
            pl.BlockSpec((width, width), lambda i: (0, 0)),
            pl.BlockSpec((block, width), lambda i: (jnp.minimum(i, blocks // 2 - 1), 0)),
            own(width),
            own(1),
            own(width),
        ],
        out_shape=[
            wide,
            jax.ShapeDtypeStruct((width, width), BF16),
            jax.ShapeDtypeStruct((count // 2, width), F32),
            wide,
            jax.ShapeDtypeStruct((count, 1), F32),
            wide,
        ],
        compiler_params=vmem(32),
        cost_estimate=pl.CostEstimate(flops=count * width, bytes_accessed=count * width, transcendentals=0),
    )(place.spot, tokens, mine, other, w_mine, w_other, rows)


def sum_devices(place, value):
    ways = [place.core, place.along_x, place.along_y]
    step = 1
    while step < place.planes:
        ways.append(functools.partial(place.along_z, step=step))
        step *= 2
    for way in ways:
        value, other = yield value, way(value)
        value = value + other
    return value


def norm_back_kernel(
    half, where, part, arrived, upstream, normed, inv_std, gain, weights, own_columns, d_attended, own_rows, sums
):
    step = pl.program_id(0)
    e = part[...].astype(F32) + arrived[...].astype(F32)
    n = normed[...].astype(F32)
    scaled = e * gain[...]
    first_mean = jnp.mean(scaled, axis=-1, keepdims=True)
    second_mean = jnp.mean(scaled * n, axis=-1, keepdims=True)
    cot = upstream[...].astype(F32)
    d = cot + inv_std[...] * (scaled - first_mean - n * second_mean)
    d_low = d.astype(BF16)
    rows_here = weights[pl.ds(pl.multiple_of(where[0] * half, 16), half), :]
    d_attended[...] = lax.dot_general(
        d_low, rows_here, (((1,), (1,)), ((), ())), preferred_element_type=F32
    ).astype(BF16)
    for core in range(2):

        @pl.when(where[0] == core)
        def _():
            own_columns[...] = d_low[:, core * half : (core + 1) * half]

    @pl.when(step < pl.num_programs(0) // 2)
    def _():
        own_rows[...] = d

    rows = jnp.concatenate([jnp.sum(v, axis=0, keepdims=True) for v in (e * n, e, d, cot)] + [jnp.zeros((4, e.shape[1]), F32)])

    @pl.when(step == 0)
    def _():
        sums[...] = rows

    @pl.when(step > 0)
    def _():
        sums[...] += rows


def norm_back_second(place, part, arrived, upstream, normed, inv_std, gain, weights):
    tokens, width = part.shape
    size = tokens // 4
    by_row = pl.BlockSpec((size, width), lambda i: (i, 0))
    turned = pl.BlockSpec((size, width), lambda i: ((i + 2) % 4, 0))
    return pl.pallas_call(
        functools.partial(norm_back_kernel, width // 2),
        grid=(4,),
        in_specs=[
            scalar_spec(),
            by_row,
            turned,
            by_row,
            by_row,
            pl.BlockSpec((size, 1), lambda i: (i, 0)),
            pl.BlockSpec((1, width), lambda i: (0, 0)),
            pl.BlockSpec((width, width), lambda i: (0, 0), pipeline_mode=pl.Buffered(1)),
        ],
        out_specs=[
            pl.BlockSpec((size, width // 2), lambda i: (i, 0)),
            pl.BlockSpec((size, width // 2), lambda i: (i, 0)),
            pl.BlockSpec((size, width), lambda i: (jnp.minimum(i, 1), 0)),
            pl.BlockSpec((8, width), lambda i: (0, 0)),
        ],
        out_shape=[
            jax.ShapeDtypeStruct((tokens, width // 2), BF16),
            jax.ShapeDtypeStruct((tokens, width // 2), BF16),
            jax.ShapeDtypeStruct((tokens // 2, width), F32),
            jax.ShapeDtypeStruct((8, width), F32),
        ],
        compiler_params=vmem(58),
    )(place.spot, part, arrived, upstream, normed, inv_std, gain, weights)


def rider_rows_kernel(hidden, up_shard, up_cols, where, pack, by_width, by_hidden, out):
    width = out.shape[1]
    half, half_hidden = width // 2, by_hidden.shape[1]
    shard = width // (hidden // up_shard)
    out[...] = jnp.zeros_like(out)
    for core in range(2):

        @pl.when(where[0] == core)
        def _():
            here = slice(core * half, (core + 1) * half)
            out[0:1, here] = pack[0:1, :half]
            out[1:2, here] = pack[0:1, 2 * half :]
            if core == 0:
                out[2:6, :] = by_width[:4, :]
            for owner in range(hidden // up_shard):
                for row in range(up_cols):
                    start = owner * up_shard + row * shard
                    first = max(start, core * half_hidden)
                    last = min(start + shard, (owner + 1) * up_shard, (core + 1) * half_hidden, hidden)
                    if first < last:
                        at = owner * shard + first - start
                        out[6 + row : 7 + row, at : at + last - first] = by_hidden[
                            0:1, first - core * half_hidden : last - core * half_hidden
                        ]


def rider_rows(place, pack, by_width, by_hidden, hidden, up_shard, up_cols):
    return pl.pallas_call(
        functools.partial(rider_rows_kernel, hidden, up_shard, up_cols),
        in_specs=[scalar_spec()] + [whole_spec()] * 3,
        out_specs=whole_spec(),
        out_shape=jax.ShapeDtypeStruct((-(-(6 + up_cols) // 8) * 8, by_width.shape[1]), F32),
        compiler_params=vmem(16),
    )(place.spot, pack, by_width, by_hidden)


def norm_back_first_kernel(part, arrived, d_resid, normed, inv_std, gain, grad, sums):
    e = part[...].astype(F32) + arrived[...].astype(F32)
    n = normed[...].astype(F32)
    scaled = e * gain[...]
    first_mean = jnp.mean(scaled, axis=-1, keepdims=True)
    second_mean = jnp.mean(scaled * n, axis=-1, keepdims=True)
    grad[...] = (d_resid[...] + inv_std[...] * (scaled - first_mean - n * second_mean)).astype(BF16)
    rows = jnp.concatenate([jnp.sum(v, axis=0, keepdims=True) for v in (e * n, e)] + [jnp.zeros((6, e.shape[1]), F32)])

    @pl.when(pl.program_id(0) == 0)
    def _():
        sums[...] = rows

    @pl.when(pl.program_id(0) > 0)
    def _():
        sums[...] += rows


def norm_back_first(part, arrived, d_resid, normed, inv_std, gain):
    tokens, width = arrived.shape
    size = tokens // 4
    by_row = pl.BlockSpec((size, width), lambda i: (i, 0))
    return pl.pallas_call(
        norm_back_first_kernel,
        grid=(4,),
        in_specs=[by_row] * 4 + [pl.BlockSpec((size, 1), lambda i: (i, 0)), pl.BlockSpec((1, width), lambda i: (0, 0))],
        out_specs=[by_row, pl.BlockSpec((8, width), lambda i: (0, 0))],
        out_shape=[jax.ShapeDtypeStruct((tokens, width), BF16), jax.ShapeDtypeStruct((8, width), F32)],
        compiler_params=vmem(24),
    )(part, arrived, d_resid, normed, inv_std, gain)


def normalize(values):
    row_mean = jnp.mean(values, axis=-1, keepdims=True)
    centred = values - row_mean
    variance = jnp.mean(centred * centred, axis=-1, keepdims=True)
    inv_std = lax.rsqrt(variance + EPSILON)
    return centred * inv_std, inv_std


def layer_norm(values, gain_row, shift_row):
    row_mean = jnp.mean(values, axis=-1, keepdims=True)
    centred = values - row_mean
    variance = jnp.mean(centred * centred, axis=-1, keepdims=True)
    inv_std = lax.rsqrt(variance + EPSILON)
    normed = centred * inv_std
    return (normed * gain_row + shift_row, normed, inv_std)


def norm_back(upstream, normed, inv_std, gain_row):
    scaled = upstream * gain_row
    first_mean = jnp.mean(scaled, axis=-1, keepdims=True)
    second_mean = jnp.mean(scaled * normed, axis=-1, keepdims=True)
    return inv_std * (scaled - first_mean - normed * second_mean)


def gelu_and_slope(values):
    square = values * values
    tangent = jnp.tanh(GELU_SCALE * values * (1.0 + GELU_CUBE * square))
    half = 0.5 * (1.0 + tangent)
    slope = half + 0.5 * values * (1.0 - tangent * tangent) * GELU_SCALE * (1.0 + 3.0 * GELU_CUBE * square)
    return values * half, slope


def dot(a, b):
    return jnp.dot(a, b, preferred_element_type=F32)


def dot_t(a, b):
    return lax.dot_general(a, b, (((1,), (1,)), ((), ())), preferred_element_type=F32)


def t_dot(a, b):
    return lax.dot_general(a, b, (((0,), (0,)), ((), ())), preferred_element_type=F32)


def image_on_chip(inputs, key_mask, w_qkv, w_out, w_up, w_down, norm_gains, biases, up_bias, cotangent):
    place = Place()
    img_count, tok_count, width = inputs.shape
    shard = w_qkv.shape[0]
    fsdp = lax.axis_size("fsdp")
    half_width = width // 2
    hidden = w_up.shape[1]
    half_hidden = -(-hidden // 2 // LANES) * LANES
    up_shard = up_bias.shape[0]
    up_cols = -(-up_shard // shard)

    def halves_hidden(w):
        padded = jnp.pad(w, ((0, 0), (0, 2 * half_hidden - hidden)))
        return jnp.stack([padded[:, :half_hidden], padded[:, half_hidden:]])

    small = jnp.concatenate(
        [
            norm_gains,
            biases,
            jnp.pad(up_bias, (0, up_cols * shard - up_shard)).reshape(up_cols, shard),
        ]
    )
    n_small = small.shape[0]
    spare = -(3 * half_width) % LANES
    extra = jnp.pad(small.T, ((0, 0), (0, spare - n_small)))
    c = place.c

    give, keep = halve(place, w_qkv, extra)
    qkv = Transfer(spread(place, give, keep))
    tokens_in = Transfer(to_image(place, pick(inputs, place.x), pick(inputs, 1 - place.x)))
    w_out, w_up, w_down, cotangent = close_round(qkv, hold=(w_out, w_up, w_down, cotangent))
    close_round(qkv)

    out_pad = -half_width % LANES
    out_cols = half_width + out_pad
    out_halves = jnp.pad(jnp.moveaxis(w_out.reshape(shard, 2, half_width), 1, 0), ((0, 0), (0, 0), (0, out_pad)))
    down_halves = halves_hidden(w_down.T)
    down = Transfer(spread(place, pick(down_halves, 1 - c), pick(down_halves, c)))
    rest = jnp.concatenate([out_halves, halves_hidden(w_up)], axis=2)
    out_up = Transfer(spread(place, pick(rest, 1 - c), pick(rest, c), corner=True))
    upstream_parts = pick(cotangent, place.x), pick(cotangent, 1 - place.x)
    close_round(out_up)
    key_mask, *upstream_parts = close_round(qkv, tokens_in, out_up, hold=(key_mask, *upstream_parts))

    upstream_in = Transfer(to_image(place, *upstream_parts))
    other_mask = place.core(key_mask)
    close_round(qkv, tokens_in)

    live_keys = image_order(place, pick(jnp.where(c == place.y, key_mask, other_mask), place.x))
    mask_bias = jnp.where(live_keys > 0, 0.0, NEG_FILL).astype(F32)[:, None]
    (mask_bias,) = close_round(qkv, out_up, down, upstream_in, hold=(mask_bias,))

    full_first = assemble(place, qkv.result, 0, 3 * half_width + spare)
    full_qkv = full_first[:, : 3 * half_width]
    small_rows, qkv_shift = vectors(place, full_first, 3 * half_width, 16)
    gain_rows, bias_rows = small_rows[:2], small_rows[2:8]
    up_shift = (
        small_rows[8 : 8 + up_cols].reshape(up_cols, fsdp, shard).transpose(1, 0, 2).reshape(fsdp, up_cols * shard)[:, :up_shard]
    ).reshape(hidden)
    up_shift = pick(jnp.pad(up_shift, (0, 2 * half_hidden - hidden)).reshape(2, half_hidden), c)
    tokens, first_normed, first_inv, first_low, packed = norm_and_project(
        *tokens_in.result, full_first, qkv_shift, small_rows, 3 * half_width
    )
    (packed,) = close_round(out_up, down, upstream_in, hold=(packed,))

    attended_half, raised, inv_total = attention_forward(packed, mask_bias)
    (attended_half,) = close_round(out_up, down, hold=(attended_half,))

    half_out = assemble(place, out_up.result, 0, out_cols)
    attended, full_out, residual_half, second_normed, second_inv, second_low = project_and_norm(
        place, tokens, attended_half, place.core(attended_half), half_out, place.core(half_out), small_rows
    )
    half = residual_half.shape[0]
    (second_low,) = close_round(down, hold=(second_low,))

    full_up = assemble(place, out_up.result, out_cols, half_hidden)
    active, slope = gelu_and_slope(dot(second_low, full_up) + up_shift)
    active, slope = active.astype(BF16), slope.astype(BF16)
    active, slope = close_round(down, hold=(active, slope))

    upstream = jnp.concatenate(upstream_in.result)
    dw_down = t_dot(upstream, active).astype(BF16)
    down_grad = Transfer(collect_lines(place, dw_down))
    full_down = assemble(place, down.result, 0, half_hidden)
    d_active = dot(upstream, full_down)
    d_upper = (d_active * slope.astype(F32)).astype(BF16)
    d_second_part = dot_t(d_upper, full_up).astype(BF16)
    (d_second_part,) = close_round(hold=(d_second_part,))

    d_second_other = place.core(d_second_part)
    *dw_up, d_upper_sums = weight_grad(place, [(second_low, d_upper)], with_sums=True)
    down_part = dot_t(active, full_down).astype(BF16)
    down_sum = down_part[:half].astype(F32) + place.core(down_part[half:]).astype(F32)
    layer_half = (residual_half + down_sum + bias_rows[5]).astype(BF16)
    *dw_up, d_second_other, layer_half = close_round(hold=(*dw_up, d_second_other, layer_half))

    up_grad = Transfer(collect(place, dw_up))
    layer_out = Transfer(from_image(place, layer_half))
    d_resid_columns, d_attended, d_resid_half, by_width = norm_back_second(
        place, d_second_part, d_second_other, upstream, second_normed, second_inv, gain_rows[1:], full_out
    )
    d_packed = attention_backward(packed, d_attended, attended_half, raised, inv_total)
    (d_packed,) = close_round(up_grad, layer_out, hold=(d_packed,))

    pack_sum = dot(jnp.ones((8, d_packed.shape[0]), BF16), d_packed)
    riders = rider_rows(place, pack_sum, by_width, d_upper_sums, hidden, up_shard, up_cols)
    dw_last = weight_grad(place, [(first_low, d_packed), (attended, d_resid_columns)], riders)
    *dw_last, d_packed = close_round(up_grad, down_grad, hold=(*dw_last, d_packed))

    last_grad = Transfer(collect(place, dw_last))
    d_first_part = dot_t(d_packed, full_qkv).astype(BF16)
    grad_half, first_sums = norm_back_first(
        d_first_part,
        place.core(d_first_part[half:]),
        d_resid_half,
        first_normed,
        first_inv,
        gain_rows[:1],
    )
    late = Transfer(sum_devices(place, first_sums[:2].reshape(-1, LANES)))
    (grad_half,) = close_round(last_grad, down_grad, late, hold=(grad_half,))

    def write_hidden(lower, higher, out):
        out[:, :half_hidden] = lower[:, :half_hidden]
        out[:, half_hidden:] = higher[:, : hidden - half_hidden]

    def write_last(lower, higher, qkv_out, proj, rest):
        for i in range(3):
            here = slice(i * half_width, (i + 1) * half_width)
            qkv_out[:, i * width : i * width + half_width] = lower[:, here]
            qkv_out[:, i * width + half_width : (i + 1) * width] = higher[:, here]
        here = slice(3 * half_width, 4 * half_width)
        proj[:, :half_width] = lower[:, here]
        proj[:, half_width:] = higher[:, here]
        rest[...] = lower[:, 4 * half_width :] + higher[:, 4 * half_width :]

    close_round(up_grad, last_grad, down_grad, late)
    grad_in = Transfer(from_image(place, grad_half))
    close_round(up_grad, last_grad, down_grad, late, grad_in)
    grad_in, layer_out = close_round(
        up_grad, last_grad, down_grad, late, hold=(grad_in.result, layer_out.result)
    )
    close_round(up_grad, last_grad, down_grad, late)
    (grad_up,) = finish(place, up_grad.result, write_hidden, [(shard, hidden)])
    (grad_down,) = finish(place, down_grad.result, write_hidden, [(shard, hidden)])
    grad_up, grad_down = close_round(last_grad, hold=(grad_up, grad_down))
    grad_qkv, grad_proj, rest_sums = finish(
        place, last_grad.result, write_last, [(shard, 3 * width), (shard, width), (shard, LANES)]
    )
    rows = rest_sums[:, : 6 + up_cols].T
    first_rows = lax.dynamic_slice_in_dim(late.result.reshape(2, width), lax.axis_index("fsdp") * shard, shard, axis=1)
    grad_upbias = rows[6:].reshape(up_cols * shard)[:up_shard]
    grad_gains = jnp.stack([first_rows[0], rows[2]])
    grad_biases = jnp.stack([first_rows[1], rows[3], rows[0], rows[1], rows[4], rows[5]])
    return (layer_out, grad_in, grad_qkv, grad_proj, grad_up, grad_down.T, grad_gains, grad_biases, grad_upbias)


def for_sending(array):
    return jax.tree.map(lambda a: a.astype(jnp.bfloat16) if a.dtype == jnp.float32 else a, array)


def gelu_tanh(values):
    return (
        0.5
        * values
        * (1.0 + jnp.tanh(GELU_SCALE * (values + GELU_CUBE * values * values * values)))
    )


def gelu_slope(values):
    tangent = jnp.tanh(GELU_SCALE * (values + GELU_CUBE * values * values * values))
    return 0.5 * (1.0 + tangent) + 0.5 * values * (1.0 - tangent * tangent) * GELU_SCALE * (
        1.0 + 3.0 * GELU_CUBE * values * values
    )


def block_scores(q_block, keys_full, live, score_scale):
    scores = (
        jnp.einsum("qhd,khd->hqk", q_block, keys_full, preferred_element_type=jnp.float32)
        * score_scale
    )
    return jnp.where(live[None, None, :] > 0, scores, NEG_FILL)


def forward_image(pieces, block_rows, score_scale):
    query, keys_full, values_full, live = pieces
    out_parts = []
    total_parts = []
    for start in range(0, query.shape[0], block_rows):
        masked = block_scores(query[start : start + block_rows], keys_full, live, score_scale)
        top_score = jnp.max(masked, axis=-1, keepdims=True)
        log_total = top_score + jnp.log(
            jnp.sum(jnp.exp(masked - top_score), axis=-1, keepdims=True)
        )
        probs_low = jnp.exp(masked - log_total).astype(jnp.bfloat16)
        out_parts.append(
            jnp.einsum(
                "hqk,khd->qhd", probs_low, values_full, preferred_element_type=jnp.float32
            ).astype(jnp.bfloat16)
        )
        total_parts.append(log_total)
    return (jnp.concatenate(out_parts, axis=0), jnp.concatenate(total_parts, axis=1))


def backward_image(pieces, block_rows, score_scale):
    query, keys_full, values_full, live, log_totals, d_heads = pieces
    dq_parts = []
    dk_total = jnp.zeros(keys_full.shape, jnp.float32)
    dv_total = jnp.zeros(values_full.shape, jnp.float32)
    for start in range(0, query.shape[0], block_rows):
        q_block = query[start : start + block_rows]
        d_block = d_heads[start : start + block_rows]
        masked = block_scores(q_block, keys_full, live, score_scale)
        probs = jnp.exp(masked - log_totals[:, start : start + block_rows])
        probs_low = probs.astype(jnp.bfloat16)
        d_probs = jnp.einsum(
            "qhd,khd->hqk", d_block, values_full, preferred_element_type=jnp.float32
        )
        row_dot = jnp.sum(probs * d_probs, axis=-1, keepdims=True)
        d_scores = (probs * (d_probs - row_dot)).astype(jnp.bfloat16)
        dq_block = (
            jnp.einsum("hqk,khd->qhd", d_scores, keys_full, preferred_element_type=jnp.float32)
            * score_scale
        )
        dq_parts.append(dq_block.astype(jnp.bfloat16))
        dk_total = dk_total + jnp.einsum(
            "hqk,qhd->khd", d_scores, q_block, preferred_element_type=jnp.float32
        )
        dv_total = dv_total + jnp.einsum(
            "hqk,qhd->khd", probs_low, d_block, preferred_element_type=jnp.float32
        )
    return (
        jnp.concatenate(dq_parts, axis=0),
        (dk_total * score_scale).astype(jnp.bfloat16),
        dv_total.astype(jnp.bfloat16),
    )


def heads_over_seq(inputs, key_mask, w_qkv, w_out, w_up, w_down, norm_gains, biases, up_bias, cotangent):
    img_count, tok_count, width = inputs.shape
    seq_len = key_mask.shape[1]
    row_count = img_count * tok_count
    head_cols = width // lax.axis_size("seq")
    local_heads = head_cols // HEAD_DIM
    block_rows = min(QBLOCK, seq_len)
    score_scale = 1.0 / math.sqrt(HEAD_DIM)
    gathered = (
        lax.all_gather(w_qkv, "fsdp", axis=0, tiled=True),
        lax.all_gather(w_out, "fsdp", axis=0, tiled=True),
        lax.all_gather(w_up, "fsdp", axis=0, tiled=True),
        lax.all_gather(w_down, "fsdp", axis=1, tiled=True),
        lax.all_gather(norm_gains, "fsdp", axis=1, tiled=True),
        lax.all_gather(biases, "fsdp", axis=1, tiled=True),
        lax.all_gather(up_bias, "fsdp", axis=0, tiled=True),
    )
    full_qkv, full_out, full_up, full_down, full_gains, full_biases, full_upbias = gathered
    gain_rows = full_gains.astype(jnp.float32)
    bias_rows = full_biases.astype(jnp.float32)
    up_shift = full_upbias.astype(jnp.float32)
    qkv_shift = jnp.concatenate([bias_rows[2], jnp.zeros((width,), jnp.float32), bias_rows[3]])
    tok_wide = inputs.reshape(row_count, width).astype(jnp.float32)
    first_out, first_normed, first_inv = layer_norm(tok_wide, gain_rows[0], bias_rows[0])
    first_low = first_out.astype(jnp.bfloat16)
    packed = (jnp.dot(first_low, full_qkv, preferred_element_type=jnp.float32) + qkv_shift).astype(
        jnp.bfloat16
    )
    by_heads = lax.all_to_all(
        packed.reshape(img_count, tok_count, 3, width),
        "seq",
        split_axis=3,
        concat_axis=1,
        tiled=True,
    )
    query = by_heads[:, :, 0].reshape(img_count, seq_len, local_heads, HEAD_DIM)
    keys_full = by_heads[:, :, 1].reshape(img_count, seq_len, local_heads, HEAD_DIM)
    values_full = by_heads[:, :, 2].reshape(img_count, seq_len, local_heads, HEAD_DIM)

    def run_forward(pieces):
        return forward_image(pieces, block_rows, score_scale)

    attended_heads, log_totals = lax.map(run_forward, (query, keys_full, values_full, key_mask))
    attended = lax.all_to_all(
        for_sending(attended_heads.reshape(img_count, seq_len, head_cols)),
        "seq",
        split_axis=1,
        concat_axis=2,
        tiled=True,
    ).reshape(row_count, width)
    residual = (
        tok_wide + jnp.dot(attended, full_out, preferred_element_type=jnp.float32) + bias_rows[4]
    )
    second_out, second_normed, second_inv = layer_norm(residual, gain_rows[1], bias_rows[1])
    second_low = second_out.astype(jnp.bfloat16)
    upper = jnp.dot(second_low, full_up, preferred_element_type=jnp.float32) + up_shift
    active = gelu_tanh(upper).astype(jnp.bfloat16)
    layer_out = (
        residual + jnp.dot(active, full_down, preferred_element_type=jnp.float32) + bias_rows[5]
    ).astype(jnp.bfloat16)
    back_qkv, back_out, back_up, back_down, back_gains, back_biases, back_upbias = gathered
    back_gain_rows = back_gains.astype(jnp.float32)
    upstream = cotangent.reshape(row_count, width)
    grad_wide = upstream.astype(jnp.float32)
    d_active = jnp.dot(upstream, back_down.T, preferred_element_type=jnp.float32)
    dw_down = jnp.dot(active.T, upstream, preferred_element_type=jnp.float32)
    d_upper = (d_active * gelu_slope(upper)).astype(jnp.bfloat16)
    dw_up = jnp.dot(second_low.T, d_upper, preferred_element_type=jnp.float32)
    d_second = jnp.dot(d_upper, back_up.T, preferred_element_type=jnp.float32)
    d_resid = grad_wide + norm_back(d_second, second_normed, second_inv, back_gain_rows[1])
    d_resid_low = d_resid.astype(jnp.bfloat16)
    dw_out = jnp.dot(attended.T, d_resid_low, preferred_element_type=jnp.float32)
    d_attended = jnp.dot(d_resid_low, back_out.T, preferred_element_type=jnp.float32).astype(
        jnp.bfloat16
    )
    d_heads = lax.all_to_all(
        d_attended.reshape(img_count, tok_count, width),
        "seq",
        split_axis=2,
        concat_axis=1,
        tiled=True,
    ).reshape(img_count, seq_len, local_heads, HEAD_DIM)

    def run_backward(pieces):
        return backward_image(pieces, block_rows, score_scale)

    dq_heads, dk_heads, dv_heads = lax.map(
        run_backward, (query, keys_full, values_full, key_mask, log_totals, d_heads)
    )
    stacked = jnp.stack(
        [
            dq_heads.reshape(img_count, seq_len, head_cols),
            dk_heads.reshape(img_count, seq_len, head_cols),
            dv_heads.reshape(img_count, seq_len, head_cols),
        ],
        axis=2,
    )
    d_packed = (
        lax.all_to_all(for_sending(stacked), "seq", split_axis=1, concat_axis=3, tiled=True)
        .astype(stacked.dtype)
        .reshape(row_count, 3 * width)
    )
    d_pack_wide = d_packed.astype(jnp.float32)
    dw_qkv = jnp.dot(first_low.T, d_packed, preferred_element_type=jnp.float32)
    d_first = jnp.dot(d_packed, back_qkv.T, preferred_element_type=jnp.float32)
    grad_in = (d_resid + norm_back(d_first, first_normed, first_inv, back_gain_rows[0])).astype(
        jnp.bfloat16
    )
    d_gains = jnp.stack(
        [jnp.sum(d_first * first_normed, axis=0), jnp.sum(d_second * second_normed, axis=0)]
    )
    d_biases = jnp.stack(
        [
            jnp.sum(d_first, axis=0),
            jnp.sum(d_second, axis=0),
            jnp.sum(d_pack_wide[:, :width], axis=0),
            jnp.sum(d_pack_wide[:, 2 * width :], axis=0),
            jnp.sum(d_resid, axis=0),
            jnp.sum(grad_wide, axis=0),
        ]
    )
    d_upbias = jnp.sum(d_upper.astype(jnp.float32), axis=0)
    owned = (
        lax.psum_scatter(dw_qkv, "fsdp", scatter_dimension=0, tiled=True),
        lax.psum_scatter(dw_out, "fsdp", scatter_dimension=0, tiled=True),
        lax.psum_scatter(dw_up, "fsdp", scatter_dimension=0, tiled=True),
        lax.psum_scatter(dw_down, "fsdp", scatter_dimension=1, tiled=True),
        lax.psum_scatter(d_gains, "fsdp", scatter_dimension=1, tiled=True),
        lax.psum_scatter(d_biases, "fsdp", scatter_dimension=1, tiled=True),
        lax.psum_scatter(d_upbias, "fsdp", scatter_dimension=0, tiled=True),
    )
    summed = lax.psum((owned[0], owned[1], owned[2], owned[3], owned[4], owned[5], owned[6]), "seq")
    grad_qkv, grad_proj, grad_up, grad_down, grad_gains, grad_biases, grad_upbias = summed
    return (
        layer_out.reshape(img_count, tok_count, width),
        grad_in.reshape(img_count, tok_count, width),
        grad_qkv,
        grad_proj,
        grad_up,
        grad_down,
        grad_gains,
        grad_biases,
        grad_upbias,
    )


def solution(mesh):
    in_specs = (
        P("fsdp", "seq", None),
        P("fsdp", None),
        P("fsdp", None),
        P("fsdp", None),
        P("fsdp", None),
        P(None, "fsdp"),
        P(None, "fsdp"),
        P(None, "fsdp"),
        P("fsdp"),
        P("fsdp", "seq", None),
    )
    out_specs = (
        P("fsdp", "seq", None),
        P("fsdp", "seq", None),
        P("fsdp", None),
        P("fsdp", None),
        P("fsdp", None),
        P(None, "fsdp"),
        P(None, "fsdp"),
        P(None, "fsdp"),
        P("fsdp"),
    )

    def layer(*args):
        images = args[0].shape[0] // mesh.shape["fsdp"]
        planes = mesh.shape["fsdp"] // 2
        fits = mesh.shape["seq"] == 4 and images == 2 and planes * 2 == mesh.shape["fsdp"] and planes & (planes - 1) == 0
        plan = image_on_chip if fits else heads_over_seq
        return jax.shard_map(plan, mesh=mesh, in_specs=in_specs, out_specs=out_specs, check_vma=False)(*args)

    return layer
```

```python
import functools
import math

import jax
import jax.numpy as jnp
from jax import lax
from jax.experimental import pallas as pl
from jax.experimental.pallas import tpu as pltpu
from jax.sharding import PartitionSpec as P

HEAD_DIM = 72
QBLOCK = 512
EPSILON = 1e-06
NEG_FILL = -1e30
GELU_CUBE = 0.044715
GELU_SCALE = math.sqrt(2.0 / math.pi)
LOG2E = math.log2(math.e)
LANES = 128
F32 = jnp.float32
BF16 = jnp.bfloat16
MIB = 2**20


def attention_forward_kernel(block, heads, qkv_ref, bias_ref, out_ref, probs_ref, inv_ref, by_row, out_rows):
    head = pl.program_id(0)
    width = heads * HEAD_DIM
    seq = qkv_ref.shape[0]

    @pl.when(head == 0)
    def _():
        by_row[...] = qkv_ref[...].astype(F32).T

    def rows(which):
        return pl.ds(pl.multiple_of(which * width + head * HEAD_DIM, 8), HEAD_DIM)

    query = by_row[rows(0), :].astype(BF16)
    keys = by_row[rows(1), :].T.astype(BF16)
    values = by_row[rows(2), :].astype(BF16)
    bias = bias_ref[...]
    for start in range(0, seq, block):
        part = slice(start, start + block)
        scores = jnp.dot(keys, query[:, part], preferred_element_type=F32) * (LOG2E / math.sqrt(HEAD_DIM)) + bias
        top = jnp.max(scores, axis=0, keepdims=True)
        raised = jnp.exp2(scores - top)
        inv = 1.0 / jnp.sum(raised, axis=0, keepdims=True)
        raised_low = raised.astype(BF16)
        probs_ref[0, :, part] = raised_low
        inv_ref[0, :, part] = inv
        out_rows[rows(0), part] = jnp.dot(values, raised_low, preferred_element_type=F32) * inv

    @pl.when(head == heads - 1)
    def _():
        out_ref[:, :width] = out_rows[...].T.astype(BF16)


def attention_forward(qkv, bias, block=QBLOCK):
    seq, triple = qkv.shape
    width = triple // 3
    heads = width // HEAD_DIM
    whole_tiles = -(-width // LANES) * LANES
    return pl.pallas_call(
        functools.partial(attention_forward_kernel, block, heads),
        grid=(heads,),
        in_specs=[pl.BlockSpec((seq, triple), lambda h: (0, 0)), pl.BlockSpec((seq, 1), lambda h: (0, 0))],
        out_specs=[
            pl.BlockSpec((seq, whole_tiles), lambda h: (0, 0)),
            pl.BlockSpec((1, seq, seq), lambda h: (h, 0, 0)),
            pl.BlockSpec((1, 1, seq), lambda h: (h, 0, 0)),
        ],
        out_shape=[
            jax.ShapeDtypeStruct((seq, whole_tiles), BF16),
            jax.ShapeDtypeStruct((heads, seq, seq), BF16),
            jax.ShapeDtypeStruct((heads, 1, seq), F32),
        ],
        scratch_shapes=[pltpu.VMEM((triple, seq), F32), pltpu.VMEM((width, seq), F32)],
        compiler_params=pltpu.CompilerParams(vmem_limit_bytes=48 * MIB),
        cost_estimate=pl.CostEstimate(
            flops=heads * seq * seq, bytes_accessed=seq * triple, transcendentals=0
        ),
    )(qkv, bias)


def attention_backward_kernel(
    block, heads, qkv_ref, d_out_ref, out_ref, probs_ref, inv_ref, grad_ref, by_row, d_rows, o_rows, grad_rows
):
    head = pl.program_id(0)
    width = heads * HEAD_DIM
    seq = qkv_ref.shape[0]
    scale = 1.0 / math.sqrt(HEAD_DIM)

    @pl.when(head == 0)
    def _():
        by_row[...] = qkv_ref[...].astype(F32).T
        d_rows[...] = d_out_ref[...].astype(F32).T
        o_rows[...] = out_ref[:, :width].astype(F32).T

    def rows(which):
        return pl.ds(pl.multiple_of(which * width + head * HEAD_DIM, 8), HEAD_DIM)

    query = by_row[rows(0), :].T.astype(BF16)
    keys = by_row[rows(1), :].astype(BF16)
    values = by_row[rows(2), :].T.astype(BF16)
    d_out = d_rows[rows(0), :]
    inv = inv_ref[0]
    row_dot = jnp.sum(d_out * o_rows[rows(0), :], axis=0, keepdims=True) * inv
    d_scaled = d_out * inv
    d_tokens = d_scaled.T.astype(BF16)
    d_scaled = d_scaled.astype(BF16)
    d_keys = jnp.zeros((seq, HEAD_DIM), F32)
    d_values = jnp.zeros((seq, HEAD_DIM), F32)
    for start in range(0, seq, block):
        part = slice(start, start + block)
        raised = probs_ref[0, :, part]
        d_probs = jnp.dot(values, d_scaled[:, part], preferred_element_type=F32)
        d_scores = (raised.astype(F32) * (d_probs - row_dot[:, part])).astype(BF16)
        d_values += jnp.dot(raised, d_tokens[part, :], preferred_element_type=F32)
        d_keys += jnp.dot(d_scores, query[part, :], preferred_element_type=F32)
        grad_rows[rows(0), part] = jnp.dot(keys, d_scores, preferred_element_type=F32) * scale
    grad_rows[rows(1), :] = d_keys.T * scale
    grad_rows[rows(2), :] = d_values.T

    @pl.when(head == heads - 1)
    def _():
        grad_ref[...] = grad_rows[...].T.astype(BF16)


def attention_backward(qkv, d_out, out, probs, inv, block=QBLOCK):
    seq, triple = qkv.shape
    width = triple // 3
    heads = width // HEAD_DIM
    whole = lambda h: (0, 0)
    return pl.pallas_call(
        functools.partial(attention_backward_kernel, block, heads),
        grid=(heads,),
        in_specs=[
            pl.BlockSpec((seq, triple), whole),
            pl.BlockSpec((seq, width), whole),
            pl.BlockSpec(out.shape, whole),
            pl.BlockSpec((1, seq, seq), lambda h: (h, 0, 0)),
            pl.BlockSpec((1, 1, seq), lambda h: (h, 0, 0)),
        ],
        out_specs=pl.BlockSpec((seq, triple), whole),
        out_shape=jax.ShapeDtypeStruct((seq, triple), BF16),
        scratch_shapes=[
            pltpu.VMEM((triple, seq), F32),
            pltpu.VMEM((width, seq), F32),
            pltpu.VMEM((width, seq), F32),
            pltpu.VMEM((triple, seq), F32),
        ],
        compiler_params=pltpu.CompilerParams(vmem_limit_bytes=56 * MIB),
        cost_estimate=pl.CostEstimate(
            flops=heads * seq * seq, bytes_accessed=seq * triple, transcendentals=0
        ),
    )(qkv, d_out, out, probs, inv)


class Place:
    def __init__(self):
        self.planes = lax.axis_size("fsdp") // 2
        f = lax.axis_index("fsdp")
        k = lax.axis_index("seq")
        self.z, self.c = f // 2, f % 2
        self.k, self.y, self.x = k, k // 2, k % 2
        self.z_lines = [[2 * z + c for z in range(self.planes)] for c in range(2)]
        self.spot = jnp.stack([self.c, self.z, self.y, self.x, self.k]).astype(jnp.int32)

    def send(self, value, to):
        pairs = []
        for z in range(self.planes):
            for c in range(2):
                for y in range(2):
                    for x in range(2):
                        tz, tc, ty, tx = to(z, c, y, x)
                        here, there = ((z * 2 + c) * 2 + y) * 2 + x, ((tz * 2 + tc) * 2 + ty) * 2 + tx
                        if here != there:
                            pairs.append((here, there))
        return lax.ppermute(value, ("fsdp", "seq"), pairs)

    def core(self, value):
        return self.send(value, lambda z, c, y, x: (z, 1 - c, y, x))

    def along_x(self, value):
        return self.send(value, lambda z, c, y, x: (z, c, y, 1 - x))

    def along_y(self, value):
        return self.send(value, lambda z, c, y, x: (z, c, 1 - y, x))

    def across(self, value):
        return self.send(value, lambda z, c, y, x: (z, c, 1 - y, 1 - x))

    def along_z(self, value, step):
        return self.send(value, lambda z, c, y, x: (z ^ step, c, y, x))

    def over_z(self, value):
        return lax.all_to_all(value, "fsdp", 0, 0, axis_index_groups=self.z_lines, tiled=True)

    def turn(self, value, step):
        return self.send(value, lambda z, c, y, x: (z, y, c, x ^ step))


def pick(stack, index):
    return lax.dynamic_index_in_dim(stack, index, 0, keepdims=False)


def in_order(flag, mine, other):
    return jnp.where(flag == 0, jnp.concatenate([mine, other]), jnp.concatenate([other, mine]))


def to_image(place, here, there):
    near, far = place.turn(here, 0), place.turn(there, 1)
    here, near, far = yield here, near, far
    half = jnp.concatenate([jnp.where(place.c == place.y, here, near), far])
    half, other = yield half, place.core(half)
    return half, other


def image_order(place, row):
    blocks = row.reshape(4, -1)
    first = 2 * place.c + place.x
    return jnp.concatenate([pick(blocks, first ^ i) for i in range(4)])


def from_image(place, half):
    size = half.shape[0] // 2
    here = half[:size]
    near, far = place.turn(here, 0), place.turn(half[size:], 1)
    here, near, far = yield here, near, far
    return in_order(place.x, jnp.where(place.c == place.y, here, near)[None], far[None])


def other_order(value):
    size = value.shape[0] // 2
    return jnp.concatenate([value[size:], value[:size]])


def lane_cut(columns):
    return columns // 2 // LANES * LANES


class Transfer:
    def __init__(self, steps):
        self.steps = steps
        self.arrays = next(steps)
        self.result = None


def close_round(*transfers, rest=(), hold=()):
    every = (*transfers, *rest)
    arrays, held = lax.optimization_barrier(([transfer.arrays for transfer in every], list(hold)))
    for transfer, arrived in zip(every, arrays):
        if transfer in rest:
            transfer.arrays = arrived
            continue
        try:
            transfer.arrays = transfer.steps.send(arrived)
        except StopIteration as end:
            transfer.result = end.value
    return held


def spread(place, give, keep, corner=False):
    arrived = place.core(give)
    keep, arrived = yield keep, arrived
    block = in_order(place.c, keep, arrived)
    rows, columns = block.shape[0] // 4, block.shape[1]
    quarters = block.reshape(4, rows, columns)
    wide = jnp.broadcast_to(pick(quarters, place.k)[None], (place.planes, rows, columns))
    quarters, wide = yield quarters, wide
    quarters, planes = yield quarters, place.over_z(wide)
    own = jnp.stack([pick(planes, place.z ^ step) for step in range(1, place.planes)])
    x_part, y_part = place.along_x(own), place.along_y(own)
    quarters, own, x_part, y_part = yield quarters, own, x_part, y_part
    cut = lane_cut(columns)
    if corner:
        far = [place.across(own)]
    else:
        far = [place.along_x(y_part[:, :, :cut]), place.along_y(x_part[:, :, cut:])]
    pieces = yield quarters, own, x_part, y_part, *far
    return pieces


def halve_kernel(where, weights, extra, give, keep):
    half = weights.shape[1] // 6
    for core in range(2):

        @pl.when(where[0] == core)
        def _():
            for i in range(3):
                at = slice(i * half, (i + 1) * half)
                for out, side in ((keep, core), (give, 1 - core)):
                    start = (2 * i + side) * half
                    out[:, at] = weights[:, start : start + half]

    for out in (give, keep):
        out[:, 3 * half :] = extra[...]


def halve(place, weights, extra):
    rows = weights.shape[0]
    shape = jax.ShapeDtypeStruct((rows, weights.shape[1] // 2 + extra.shape[1]), BF16)
    return pl.pallas_call(
        halve_kernel,
        in_specs=[scalar_spec()] + [whole_spec()] * 2,
        out_specs=[whole_spec()] * 2,
        out_shape=[shape, shape],
        compiler_params=vmem(16),
    )(place.spot, weights, extra)


def assemble_kernel(planes, start, size, where, block, own, x_part, y_part, *refs):
    *far, out, sems = refs
    z, k = where[1], where[4]
    here = pl.ds(start, size)
    copies = [(block.at[:, :, here], out.at[pl.ds(z * 4, 4)])]
    for step in range(1, planes):
        at = (z ^ step) * 4
        for turn, part in enumerate((own, x_part, y_part)):
            copies.append((part.at[step - 1, :, here], out.at[at + (k ^ turn)]))
        first = 0
        for part in far:
            low, high = max(start, first), min(start + size, first + part.shape[2])
            if low < high:
                source = part.at[step - 1, :, pl.ds(low - first, high - low)]
                copies.append((source, out.at[at + (k ^ 3), :, pl.ds(low - start, high - low)]))
            first += part.shape[2]
    started = [pltpu.make_async_copy(source, target, sems.at[i]) for i, (source, target) in enumerate(copies)]
    for copy in started:
        copy.start()
    for copy in started:
        copy.wait()


def assemble(place, pieces, start, size):
    planes = place.planes
    rows = pieces[0].shape[1]
    out = pl.pallas_call(
        functools.partial(assemble_kernel, planes, start, size),
        in_specs=[scalar_spec()] + [pl.BlockSpec(memory_space=pltpu.HBM)] * len(pieces),
        out_specs=whole_spec(),
        out_shape=jax.ShapeDtypeStruct((planes * 4, rows, size), BF16),
        scratch_shapes=[pltpu.SemaphoreType.DMA((1 + 5 * (planes - 1),))],
        compiler_params=vmem(12),
        cost_estimate=pl.CostEstimate(flops=0, bytes_accessed=planes * 4 * rows * size, transcendentals=0),
    )(place.spot, *pieces)
    return out.reshape(planes * 4 * rows, size)


def whole_spec():
    return pl.BlockSpec(memory_space=pltpu.VMEM)


def scalar_spec():
    return pl.BlockSpec(memory_space=pltpu.SMEM)


def vmem(mib):
    return pltpu.CompilerParams(vmem_limit_bytes=mib * MIB)


def weight_grad_kernel(cut, group, rows, pair_count, with_riders, with_sums, where, *refs):
    lefts, rights, refs = refs[:pair_count], refs[pair_count : 2 * pair_count], refs[2 * pair_count :]
    riders, refs = (refs[0], refs[1:]) if with_riders else (None, refs)
    low_keep, low_send, high_keep, high_send, *refs = refs
    sums, refs = (refs[0], refs[1:]) if with_sums else (None, refs)
    total, *turned = refs
    step = pl.program_id(0)
    y, x = where[2], where[3]
    block = group * 4 * rows

    @pl.when(step == 0)
    def _():
        for left, by_row in zip(lefts, turned):
            by_row[...] = left[...].astype(F32).T.astype(BF16)
        if with_sums:
            sums[...] = jnp.broadcast_to(jnp.sum(rights[0][...].astype(F32), axis=0, keepdims=True), sums.shape)

    at = 0
    for right, by_row in zip(rights, turned):
        left = by_row[pl.ds(pl.multiple_of(step * block, 16), block), :]
        columns = right.shape[1]
        for start in range(0, columns, 4 * LANES):
            end = min(start + 4 * LANES, columns)
            total[:, at + start : at + end] = jnp.dot(left, right[:, start:end], preferred_element_type=F32)
        at += columns
    if with_riders:
        rows_of = riders[...]
        rest = jnp.zeros((total.shape[1] - at - rows_of.shape[0], rows_of.shape[1]), F32)
        total[:, at:] = jnp.concatenate([rows_of, rest], axis=0).T
    for plane in range(group):
        for dy in range(2):
            for dx in range(2):
                row = (plane * 4 + (y ^ dy) * 2 + (x ^ dx)) * rows
                part = total[pl.ds(pl.multiple_of(row, 8), rows), :].astype(BF16)
                (low_send if dx else low_keep)[dy, plane] = part[:, :cut]
                (high_send if dy else high_keep)[dx, plane] = part[:, cut:]


def weight_grad(place, pairs, riders=None, with_sums=False):
    planes = place.planes
    tokens, width = pairs[0][0].shape
    rows = width // planes // 4
    group = planes
    columns = sum(right.shape[1] for _, right in pairs) + (0 if riders is None else LANES)
    rider_list = [] if riders is None else [riders]
    cut = lane_cut(columns)
    still = lambda shape: pl.BlockSpec(shape, lambda i: (0, 0), pipeline_mode=pl.Buffered(1))
    low = jax.ShapeDtypeStruct((2, planes, rows, cut), BF16)
    high = jax.ShapeDtypeStruct((2, planes, rows, columns - cut), BF16)
    low_spec = pl.BlockSpec((2, group, rows, cut), lambda i: (0, i, 0, 0))
    high_spec = pl.BlockSpec((2, group, rows, columns - cut), lambda i: (0, i, 0, 0))
    sum_shapes = [jax.ShapeDtypeStruct((8, pairs[0][1].shape[1]), F32)] if with_sums else []
    return pl.pallas_call(
        functools.partial(weight_grad_kernel, cut, group, rows, len(pairs), riders is not None, with_sums),
        grid=(planes // group,),
        in_specs=[scalar_spec()]
        + [still(left.shape) for left, _ in pairs]
        + [still(right.shape) for _, right in pairs]
        + [pl.BlockSpec((extra.shape[0], group * 4 * rows), lambda i: (0, i)) for extra in rider_list],
        out_specs=[low_spec, low_spec, high_spec, high_spec] + [pl.BlockSpec(s.shape, lambda i: (0, 0)) for s in sum_shapes],
        out_shape=[low, low, high, high] + sum_shapes,
        scratch_shapes=[pltpu.VMEM((group * 4 * rows, columns), F32)] + [pltpu.VMEM((width, tokens), BF16) for _ in pairs],
        compiler_params=vmem(56),
        cost_estimate=pl.CostEstimate(flops=tokens * width, bytes_accessed=width * columns, transcendentals=0),
    )(place.spot, *[left for left, _ in pairs], *[right for _, right in pairs], *rider_list)


def add_first_kernel(low, from_x, high, from_y, low_keep, low_send, high_keep, high_send):
    for kept, arrived, outs in ((low, from_x, (low_keep, low_send)), (high, from_y, (high_keep, high_send))):
        for i, out in enumerate(outs):
            out[...] = (kept[i].astype(F32) + arrived[i].astype(F32)).astype(BF16)


def add_first(low, from_x, high, from_y):
    planes = low.shape[1]
    ins = lambda a: pl.BlockSpec((2, 1, *a.shape[2:]), lambda i: (0, i, 0, 0))
    out = lambda a: pl.BlockSpec((1, *a.shape[2:]), lambda i: (i, 0, 0))
    shape = lambda a: jax.ShapeDtypeStruct(a.shape[1:], BF16)
    return pl.pallas_call(
        add_first_kernel,
        grid=(planes,),
        in_specs=[ins(low), ins(from_x), ins(high), ins(from_y)],
        out_specs=[out(low), out(low), out(high), out(high)],
        out_shape=[shape(low), shape(low), shape(high), shape(high)],
        compiler_params=vmem(24),
    )(low, from_x, high, from_y)


def add_second_kernel(low, from_y, high, from_x, out):
    cut = low.shape[2]
    out[:, :, :cut] = (low[...].astype(F32) + from_y[...].astype(F32)).astype(BF16)
    out[:, :, cut:] = (high[...].astype(F32) + from_x[...].astype(F32)).astype(BF16)


def add_second(low, from_y, high, from_x):
    planes, rows, cut = low.shape
    spec = lambda columns: pl.BlockSpec((1, rows, columns), lambda i: (i, 0, 0))
    rest = high.shape[2]
    return pl.pallas_call(
        add_second_kernel,
        grid=(planes,),
        in_specs=[spec(cut), spec(cut), spec(rest), spec(rest)],
        out_specs=spec(cut + rest),
        out_shape=jax.ShapeDtypeStruct((planes, rows, cut + rest), BF16),
        compiler_params=vmem(24),
    )(low, from_y, high, from_x)


def quarter_of(where, parts, core, side, store):
    mine, x_part, y_part, far_low, far_high = parts
    near, same = where[2] == core, where[3] == side

    @pl.when(near & same)
    def _():
        store(mine[...])

    @pl.when(near & ~same)
    def _():
        store(x_part[...])

    @pl.when(~near & same)
    def _():
        store(y_part[...])

    @pl.when(~near & ~same)
    def _():
        store(jnp.concatenate([far_low[...], far_high[...]], axis=1))


def give_kernel(where, *refs):
    out = refs[-1]
    for core in range(2):

        @pl.when(where[0] != core)
        def _():
            for side in range(2):

                def store(value):
                    out[side] = value

                quarter_of(where, refs[:-1], core, side, store)


def give_rows(place, parts):
    rows, columns = parts[0].shape
    return pl.pallas_call(
        give_kernel,
        in_specs=[scalar_spec()] + [whole_spec()] * 5,
        out_specs=whole_spec(),
        out_shape=jax.ShapeDtypeStruct((2, rows, columns), BF16),
        compiler_params=vmem(24),
    )(place.spot, *parts)


def finish_kernel(write, where, *refs):
    parts, arrived = refs[:5], refs[5]
    outs, kept = refs[6:-1], refs[-1]
    for core in range(2):

        @pl.when(where[0] == core)
        def _():
            for side in range(2):

                def store(value):
                    kept[side] = value

                quarter_of(where, parts, core, side, store)
            halves = [kept[...], arrived[...]]
            if core:
                halves = halves[::-1]
            lower, higher = (half.astype(F32).reshape(-1, half.shape[2]) for half in halves)
            write(lower, higher, *outs)


def finish(place, pieces, write, shapes):
    *parts, arrived = pieces
    return pl.pallas_call(
        functools.partial(finish_kernel, write),
        in_specs=[scalar_spec()] + [whole_spec()] * 6,
        out_specs=[whole_spec()] * len(shapes),
        out_shape=[jax.ShapeDtypeStruct(shape, F32) for shape in shapes],
        scratch_shapes=[pltpu.VMEM(arrived.shape, BF16)],
        compiler_params=vmem(40),
    )(place.spot, *parts, arrived)


def split_rows_kernel(where, arrived, low_keep, low_send, high_keep, high_send, total):
    planes = arrived.shape[0]
    rows, cut = low_keep.shape[2:]
    total[...] = functools.reduce(jnp.add, (arrived[plane].astype(F32) for plane in range(planes)))
    for dy in range(2):
        for dx in range(2):
            row = ((where[2] ^ dy) * 2 + (where[3] ^ dx)) * rows
            part = total[pl.ds(pl.multiple_of(row, 8), rows), :].astype(BF16)
            (low_send if dx else low_keep)[dy, 0] = part[:, :cut]
            (high_send if dy else high_keep)[dx, 0] = part[:, cut:]


def split_rows(place, arrived):
    _, rows, columns = arrived.shape
    cut = lane_cut(columns)
    low = jax.ShapeDtypeStruct((2, 1, rows // 4, cut), BF16)
    high = jax.ShapeDtypeStruct((2, 1, rows // 4, columns - cut), BF16)
    return pl.pallas_call(
        split_rows_kernel,
        in_specs=[scalar_spec(), whole_spec()],
        out_specs=[whole_spec()] * 4,
        out_shape=[low, low, high, high],
        scratch_shapes=[pltpu.VMEM((rows, columns), F32)],
        compiler_params=vmem(24),
    )(place.spot, arrived)


def collect_lines(place, partial):
    arrived = yield place.over_z(partial.reshape(place.planes, -1, partial.shape[1]))
    return (yield from collect(place, split_rows(place, arrived), along_z=False))


def collect(place, pieces, along_z=True):
    low, low_send, high, high_send = pieces
    low, high, from_x, from_y = yield low, high, place.along_x(low_send), place.along_y(high_send)
    low, low_send, high, high_send = add_first(low, from_x, high, from_y)
    low, high, from_y, from_x = yield low, high, place.along_y(low_send), place.along_x(high_send)
    cut = low.shape[2]
    plane = add_second(low, from_y, high, from_x)
    if along_z:
        arrived = yield place.over_z(plane)
        mine = jnp.sum(arrived.astype(F32), axis=0).astype(BF16)
    else:
        mine = plane[0]
    mine, x_part, y_part = yield mine, place.along_x(mine), place.along_y(mine)
    far_low, far_high = place.along_x(y_part[:, :cut]), place.along_y(x_part[:, cut:])
    parts = yield mine, x_part, y_part, far_low, far_high
    parts, arrived = yield parts, place.core(give_rows(place, parts))
    return (*parts, arrived)


def vectors_kernel(first, half, where, block, rows, shift):
    turned = block[...].astype(F32).T
    rows[...] = turned[first : first + rows.shape[0]]
    shift[...] = jnp.zeros_like(shift)
    for core in range(2):

        @pl.when(where[0] == core)
        def _():
            for row, at in ((4, 0), (5, 2 * half)):
                shift[:, at : at + half] = turned[first + row : first + row + 1, core * half : (core + 1) * half]


def vectors(place, full, at, count):
    width = full.shape[0]
    tile = at // LANES
    return pl.pallas_call(
        functools.partial(vectors_kernel, at - tile * LANES, width // 2),
        grid=(1,),
        in_specs=[scalar_spec(), pl.BlockSpec((width, LANES), lambda i: (0, tile))],
        out_specs=[pl.BlockSpec((count, width), lambda i: (0, 0)), pl.BlockSpec((1, 3 * width // 2), lambda i: (0, 0))],
        out_shape=[jax.ShapeDtypeStruct((count, width), F32), jax.ShapeDtypeStruct((1, 3 * width // 2), F32)],
        compiler_params=vmem(24),
    )(place.spot, full)


def norm_and_project_kernel(half, other, weights, shift, rows, tokens, normed, inv_std, low, packed):
    step = pl.program_id(0)
    blocks = pl.num_programs(0) // 2

    @pl.when(step < blocks)
    def _():
        tokens[...] = half[...]

    @pl.when(step >= blocks)
    def _():
        tokens[...] = other[...]

    n, inv_std[...] = normalize(tokens[...].astype(F32))
    normed[...] = n.astype(BF16)
    low[...] = (n * rows[0:1, :] + rows[2:3, :]).astype(BF16)
    columns = packed.shape[1]
    packed[...] = (
        jnp.dot(low[...], weights[:, :columns], preferred_element_type=F32) + shift[...]
    ).astype(BF16)


def norm_and_project(half, other, weights, shift, rows, columns):
    size, width = half.shape
    blocks = 2
    block = size // blocks
    own = lambda shape: pl.BlockSpec(shape, lambda i: (i, 0))
    still = lambda array: pl.BlockSpec(array.shape, lambda i: (0, 0), pipeline_mode=pl.Buffered(1))
    wide = jax.ShapeDtypeStruct((2 * size, width), BF16)
    return pl.pallas_call(
        norm_and_project_kernel,
        grid=(2 * blocks,),
        in_specs=[
            pl.BlockSpec((block, width), lambda i: (jnp.minimum(i, blocks - 1), 0)),
            pl.BlockSpec((block, width), lambda i: (jnp.maximum(i - blocks, 0), 0)),
            still(weights),
            still(shift),
            still(rows),
        ],
        out_specs=[own((block, width)), own((block, width)), own((block, 1)), own((block, width)), own((block, columns))],
        out_shape=[
            wide,
            wide,
            jax.ShapeDtypeStruct((2 * size, 1), F32),
            wide,
            jax.ShapeDtypeStruct((2 * size, columns), BF16),
        ],
        compiler_params=vmem(32),
        cost_estimate=pl.CostEstimate(flops=size * width, bytes_accessed=size * width, transcendentals=0),
    )(half, other, weights, shift, rows)


def project_and_norm_kernel(
    half, where, tokens, mine, other, w_mine, w_other, rows, attended, full_out, residual, normed, inv_std, low
):
    step = pl.program_id(0)
    for core in range(2):
        here, there = slice(core * half, (core + 1) * half), slice((1 - core) * half, (2 - core) * half)

        @pl.when((where[0] == core) & (step == 0))
        def _():
            full_out[:, here] = w_mine[:, :half]
            full_out[:, there] = w_other[:, :half]

        @pl.when(where[0] == core)
        def _():
            attended[:, here] = mine[:, :half]
            attended[:, there] = other[:, :half]

    value = tokens[...].astype(F32) + jnp.dot(attended[...], full_out[...], preferred_element_type=F32) + rows[6:7, :]

    @pl.when(step < pl.num_programs(0) // 2)
    def _():
        residual[...] = value

    n, inv_std[...] = normalize(value)
    normed[...] = n.astype(BF16)
    low[...] = (n * rows[1:2, :] + rows[3:4, :]).astype(BF16)


def project_and_norm(place, tokens, mine, other, w_mine, w_other, rows):
    count, width = tokens.shape
    blocks = 4
    block = count // blocks
    own = lambda columns: pl.BlockSpec((block, columns), lambda i: (i, 0))
    still = lambda shape: pl.BlockSpec(shape, lambda i: (0, 0), pipeline_mode=pl.Buffered(1))
    wide = jax.ShapeDtypeStruct((count, width), BF16)
    return pl.pallas_call(
        functools.partial(project_and_norm_kernel, width // 2),
        grid=(blocks,),
        in_specs=[
            scalar_spec(),
            own(width),
            own(mine.shape[1]),
            pl.BlockSpec((block, other.shape[1]), lambda i: ((i + blocks // 2) % blocks, 0)),
            still(w_mine.shape),
            still(w_other.shape),
            still(rows.shape),
        ],
        out_specs=[
            own(width),
            pl.BlockSpec((width, width), lambda i: (0, 0)),
            pl.BlockSpec((block, width), lambda i: (jnp.minimum(i, blocks // 2 - 1), 0)),
            own(width),
            own(1),
            own(width),
        ],
        out_shape=[
            wide,
            jax.ShapeDtypeStruct((width, width), BF16),
            jax.ShapeDtypeStruct((count // 2, width), F32),
            wide,
            jax.ShapeDtypeStruct((count, 1), F32),
            wide,
        ],
        compiler_params=vmem(32),
        cost_estimate=pl.CostEstimate(flops=count * width, bytes_accessed=count * width, transcendentals=0),
    )(place.spot, tokens, mine, other, w_mine, w_other, rows)


def sum_devices(place, value):
    ways = [place.core, place.along_x, place.along_y]
    step = 1
    while step < place.planes:
        ways.append(functools.partial(place.along_z, step=step))
        step *= 2
    for way in ways:
        value, other = yield value, way(value)
        value = value + other
    return value


def norm_back_kernel(
    half, where, part, arrived, upstream, normed, inv_std, gain, weights, own_columns, d_attended, own_rows, sums
):
    step = pl.program_id(0)
    e = part[...].astype(F32) + arrived[...].astype(F32)
    n = normed[...].astype(F32)
    scaled = e * gain[...]
    first_mean = jnp.mean(scaled, axis=-1, keepdims=True)
    second_mean = jnp.mean(scaled * n, axis=-1, keepdims=True)
    cot = upstream[...].astype(F32)
    d = cot + inv_std[...] * (scaled - first_mean - n * second_mean)
    d_low = d.astype(BF16)
    rows_here = weights[pl.ds(pl.multiple_of(where[0] * half, 16), half), :]
    d_attended[...] = lax.dot_general(
        d_low, rows_here, (((1,), (1,)), ((), ())), preferred_element_type=F32
    ).astype(BF16)
    for core in range(2):

        @pl.when(where[0] == core)
        def _():
            own_columns[...] = d_low[:, core * half : (core + 1) * half]

    @pl.when(step < pl.num_programs(0) // 2)
    def _():
        own_rows[...] = d

    rows = jnp.concatenate([jnp.sum(v, axis=0, keepdims=True) for v in (e * n, e, d, cot)] + [jnp.zeros((4, e.shape[1]), F32)])

    @pl.when(step == 0)
    def _():
        sums[...] = rows

    @pl.when(step > 0)
    def _():
        sums[...] += rows


def norm_back_second(place, part, arrived, upstream, normed, inv_std, gain, weights):
    tokens, width = part.shape
    size = tokens // 4
    by_row = pl.BlockSpec((size, width), lambda i: (i, 0))
    turned = pl.BlockSpec((size, width), lambda i: ((i + 2) % 4, 0))
    return pl.pallas_call(
        functools.partial(norm_back_kernel, width // 2),
        grid=(4,),
        in_specs=[
            scalar_spec(),
            by_row,
            turned,
            by_row,
            by_row,
            pl.BlockSpec((size, 1), lambda i: (i, 0)),
            pl.BlockSpec((1, width), lambda i: (0, 0)),
            pl.BlockSpec((width, width), lambda i: (0, 0), pipeline_mode=pl.Buffered(1)),
        ],
        out_specs=[
            pl.BlockSpec((size, width // 2), lambda i: (i, 0)),
            pl.BlockSpec((size, width // 2), lambda i: (i, 0)),
            pl.BlockSpec((size, width), lambda i: (jnp.minimum(i, 1), 0)),
            pl.BlockSpec((8, width), lambda i: (0, 0)),
        ],
        out_shape=[
            jax.ShapeDtypeStruct((tokens, width // 2), BF16),
            jax.ShapeDtypeStruct((tokens, width // 2), BF16),
            jax.ShapeDtypeStruct((tokens // 2, width), F32),
            jax.ShapeDtypeStruct((8, width), F32),
        ],
        compiler_params=vmem(58),
    )(place.spot, part, arrived, upstream, normed, inv_std, gain, weights)


def rider_rows_kernel(hidden, up_shard, up_cols, where, pack, by_width, by_hidden, out):
    width = out.shape[1]
    half, half_hidden = width // 2, by_hidden.shape[1]
    shard = width // (hidden // up_shard)
    out[...] = jnp.zeros_like(out)
    for core in range(2):

        @pl.when(where[0] == core)
        def _():
            here = slice(core * half, (core + 1) * half)
            out[0:1, here] = pack[0:1, :half]
            out[1:2, here] = pack[0:1, 2 * half :]
            if core == 0:
                out[2:6, :] = by_width[:4, :]
            for owner in range(hidden // up_shard):
                for row in range(up_cols):
                    start = owner * up_shard + row * shard
                    first = max(start, core * half_hidden)
                    last = min(start + shard, (owner + 1) * up_shard, (core + 1) * half_hidden, hidden)
                    if first < last:
                        at = owner * shard + first - start
                        out[6 + row : 7 + row, at : at + last - first] = by_hidden[
                            0:1, first - core * half_hidden : last - core * half_hidden
                        ]


def rider_rows(place, pack, by_width, by_hidden, hidden, up_shard, up_cols):
    return pl.pallas_call(
        functools.partial(rider_rows_kernel, hidden, up_shard, up_cols),
        in_specs=[scalar_spec()] + [whole_spec()] * 3,
        out_specs=whole_spec(),
        out_shape=jax.ShapeDtypeStruct((-(-(6 + up_cols) // 8) * 8, by_width.shape[1]), F32),
        compiler_params=vmem(16),
    )(place.spot, pack, by_width, by_hidden)


def norm_back_first_kernel(part, arrived, d_resid, normed, inv_std, gain, grad, sums):
    e = part[...].astype(F32) + arrived[...].astype(F32)
    n = normed[...].astype(F32)
    scaled = e * gain[...]
    first_mean = jnp.mean(scaled, axis=-1, keepdims=True)
    second_mean = jnp.mean(scaled * n, axis=-1, keepdims=True)
    grad[...] = (d_resid[...] + inv_std[...] * (scaled - first_mean - n * second_mean)).astype(BF16)
    rows = jnp.concatenate([jnp.sum(v, axis=0, keepdims=True) for v in (e * n, e)] + [jnp.zeros((6, e.shape[1]), F32)])

    @pl.when(pl.program_id(0) == 0)
    def _():
        sums[...] = rows

    @pl.when(pl.program_id(0) > 0)
    def _():
        sums[...] += rows


def norm_back_first(part, arrived, d_resid, normed, inv_std, gain):
    tokens, width = arrived.shape
    size = tokens // 4
    by_row = pl.BlockSpec((size, width), lambda i: (i, 0))
    return pl.pallas_call(
        norm_back_first_kernel,
        grid=(4,),
        in_specs=[by_row] * 4 + [pl.BlockSpec((size, 1), lambda i: (i, 0)), pl.BlockSpec((1, width), lambda i: (0, 0))],
        out_specs=[by_row, pl.BlockSpec((8, width), lambda i: (0, 0))],
        out_shape=[jax.ShapeDtypeStruct((tokens, width), BF16), jax.ShapeDtypeStruct((8, width), F32)],
        compiler_params=vmem(24),
    )(part, arrived, d_resid, normed, inv_std, gain)


def normalize(values):
    row_mean = jnp.mean(values, axis=-1, keepdims=True)
    centred = values - row_mean
    variance = jnp.mean(centred * centred, axis=-1, keepdims=True)
    inv_std = lax.rsqrt(variance + EPSILON)
    return centred * inv_std, inv_std


def layer_norm(values, gain_row, shift_row):
    row_mean = jnp.mean(values, axis=-1, keepdims=True)
    centred = values - row_mean
    variance = jnp.mean(centred * centred, axis=-1, keepdims=True)
    inv_std = lax.rsqrt(variance + EPSILON)
    normed = centred * inv_std
    return (normed * gain_row + shift_row, normed, inv_std)


def norm_back(upstream, normed, inv_std, gain_row):
    scaled = upstream * gain_row
    first_mean = jnp.mean(scaled, axis=-1, keepdims=True)
    second_mean = jnp.mean(scaled * normed, axis=-1, keepdims=True)
    return inv_std * (scaled - first_mean - normed * second_mean)


def gelu_and_slope(values):
    square = values * values
    tangent = jnp.tanh(GELU_SCALE * values * (1.0 + GELU_CUBE * square))
    half = 0.5 * (1.0 + tangent)
    slope = half + 0.5 * values * (1.0 - tangent * tangent) * GELU_SCALE * (1.0 + 3.0 * GELU_CUBE * square)
    return values * half, slope


def dot(a, b):
    return jnp.dot(a, b, preferred_element_type=F32)


def dot_t(a, b):
    return lax.dot_general(a, b, (((1,), (1,)), ((), ())), preferred_element_type=F32)


def t_dot(a, b):
    return lax.dot_general(a, b, (((0,), (0,)), ((), ())), preferred_element_type=F32)


def image_on_chip(inputs, key_mask, w_qkv, w_out, w_up, w_down, norm_gains, biases, up_bias, cotangent):
    place = Place()
    img_count, tok_count, width = inputs.shape
    shard = w_qkv.shape[0]
    fsdp = lax.axis_size("fsdp")
    half_width = width // 2
    hidden = w_up.shape[1]
    half_hidden = -(-hidden // 2 // LANES) * LANES
    up_shard = up_bias.shape[0]
    up_cols = -(-up_shard // shard)

    def halves_hidden(w):
        padded = jnp.pad(w, ((0, 0), (0, 2 * half_hidden - hidden)))
        return jnp.stack([padded[:, :half_hidden], padded[:, half_hidden:]])

    small = jnp.concatenate(
        [
            norm_gains,
            biases,
            jnp.pad(up_bias, (0, up_cols * shard - up_shard)).reshape(up_cols, shard),
        ]
    )
    n_small = small.shape[0]
    spare = -(3 * half_width) % LANES
    extra = jnp.pad(small.T, ((0, 0), (0, spare - n_small)))
    c = place.c

    give, keep = halve(place, w_qkv, extra)
    qkv = Transfer(spread(place, give, keep))
    tokens_in = Transfer(to_image(place, pick(inputs, place.x), pick(inputs, 1 - place.x)))
    w_out, w_up, w_down, cotangent = close_round(qkv, hold=(w_out, w_up, w_down, cotangent))
    close_round(qkv)

    out_pad = -half_width % LANES
    out_cols = half_width + out_pad
    out_halves = jnp.pad(jnp.moveaxis(w_out.reshape(shard, 2, half_width), 1, 0), ((0, 0), (0, 0), (0, out_pad)))
    down_halves = halves_hidden(w_down.T)
    down = Transfer(spread(place, pick(down_halves, 1 - c), pick(down_halves, c)))
    rest = jnp.concatenate([out_halves, halves_hidden(w_up)], axis=2)
    out_up = Transfer(spread(place, pick(rest, 1 - c), pick(rest, c), corner=True))
    upstream_parts = pick(cotangent, place.x), pick(cotangent, 1 - place.x)
    close_round(out_up)
    key_mask, *upstream_parts = close_round(qkv, tokens_in, out_up, hold=(key_mask, *upstream_parts))

    upstream_in = Transfer(to_image(place, *upstream_parts))
    other_mask = place.core(key_mask)
    close_round(qkv, tokens_in, down)

    live_keys = image_order(place, pick(jnp.where(c == place.y, key_mask, other_mask), place.x))
    mask_bias = jnp.where(live_keys > 0, 0.0, NEG_FILL).astype(F32)[:, None]
    (mask_bias,) = close_round(qkv, out_up, down, upstream_in, hold=(mask_bias,))

    full_first = assemble(place, qkv.result, 0, 3 * half_width + spare)
    full_qkv = full_first[:, : 3 * half_width]
    small_rows, qkv_shift = vectors(place, full_first, 3 * half_width, 16)
    gain_rows, bias_rows = small_rows[:2], small_rows[2:8]
    up_shift = (
        small_rows[8 : 8 + up_cols].reshape(up_cols, fsdp, shard).transpose(1, 0, 2).reshape(fsdp, up_cols * shard)[:, :up_shard]
    ).reshape(hidden)
    up_shift = pick(jnp.pad(up_shift, (0, 2 * half_hidden - hidden)).reshape(2, half_hidden), c)
    tokens, first_normed, first_inv, first_low, packed = norm_and_project(
        *tokens_in.result, full_first, qkv_shift, small_rows, 3 * half_width
    )
    (packed,) = close_round(out_up, upstream_in, hold=(packed,))

    attended_half, raised, inv_total = attention_forward(packed, mask_bias)
    (attended_half,) = close_round(out_up, down, hold=(attended_half,))

    half_out = assemble(place, out_up.result, 0, out_cols)
    attended, full_out, residual_half, second_normed, second_inv, second_low = project_and_norm(
        place, tokens, attended_half, place.core(attended_half), half_out, place.core(half_out), small_rows
    )
    half = residual_half.shape[0]
    (second_low,) = close_round(down, hold=(second_low,))

    full_up = assemble(place, out_up.result, out_cols, half_hidden)
    active, slope = gelu_and_slope(dot(second_low, full_up) + up_shift)
    active, slope = active.astype(BF16), slope.astype(BF16)
    active, slope = close_round(down, hold=(active, slope))

    upstream = jnp.concatenate(upstream_in.result)
    dw_down = t_dot(upstream, active).astype(BF16)
    down_grad = Transfer(collect_lines(place, dw_down))
    full_down = assemble(place, down.result, 0, half_hidden)
    d_active = dot(upstream, full_down)
    d_upper = (d_active * slope.astype(F32)).astype(BF16)
    d_second_part = dot_t(d_upper, full_up).astype(BF16)
    (d_second_part,) = close_round(hold=(d_second_part,))

    d_second_other = place.core(d_second_part)
    *dw_up, d_upper_sums = weight_grad(place, [(second_low, d_upper)], with_sums=True)
    down_part = dot_t(active, full_down).astype(BF16)
    down_sum = down_part[:half].astype(F32) + place.core(down_part[half:]).astype(F32)
    layer_half = (residual_half + down_sum + bias_rows[5]).astype(BF16)
    *dw_up, d_second_other, layer_half = close_round(hold=(*dw_up, d_second_other, layer_half))

    up_grad = Transfer(collect(place, dw_up))
    layer_out = Transfer(from_image(place, layer_half))
    d_resid_columns, d_attended, d_resid_half, by_width = norm_back_second(
        place, d_second_part, d_second_other, upstream, second_normed, second_inv, gain_rows[1:], full_out
    )
    d_packed = attention_backward(packed, d_attended, attended_half, raised, inv_total)
    (d_packed,) = close_round(up_grad, layer_out, hold=(d_packed,))

    pack_sum = dot(jnp.ones((8, d_packed.shape[0]), BF16), d_packed)
    riders = rider_rows(place, pack_sum, by_width, d_upper_sums, hidden, up_shard, up_cols)
    dw_last = weight_grad(place, [(first_low, d_packed), (attended, d_resid_columns)], riders)
    *dw_last, d_packed = close_round(up_grad, down_grad, hold=(*dw_last, d_packed))

    last_grad = Transfer(collect(place, dw_last))
    d_first_part = dot_t(d_packed, full_qkv).astype(BF16)
    grad_half, first_sums = norm_back_first(
        d_first_part,
        place.core(d_first_part[half:]),
        d_resid_half,
        first_normed,
        first_inv,
        gain_rows[:1],
    )
    late = Transfer(sum_devices(place, first_sums[:2].reshape(-1, LANES)))
    (grad_half,) = close_round(last_grad, down_grad, late, hold=(grad_half,))

    def write_hidden(lower, higher, out):
        out[:, :half_hidden] = lower[:, :half_hidden]
        out[:, half_hidden:] = higher[:, : hidden - half_hidden]

    def write_last(lower, higher, qkv_out, proj, rest):
        for i in range(3):
            here = slice(i * half_width, (i + 1) * half_width)
            qkv_out[:, i * width : i * width + half_width] = lower[:, here]
            qkv_out[:, i * width + half_width : (i + 1) * width] = higher[:, here]
        here = slice(3 * half_width, 4 * half_width)
        proj[:, :half_width] = lower[:, here]
        proj[:, half_width:] = higher[:, here]
        rest[...] = lower[:, 4 * half_width :] + higher[:, 4 * half_width :]

    close_round(up_grad, last_grad, down_grad, late)
    grad_in = Transfer(from_image(place, grad_half))
    close_round(up_grad, last_grad, down_grad, late, grad_in)
    grad_in, layer_out = close_round(
        up_grad, last_grad, down_grad, late, hold=(grad_in.result, layer_out.result)
    )
    close_round(up_grad, last_grad, down_grad, late)
    (grad_up,) = finish(place, up_grad.result, write_hidden, [(shard, hidden)])
    (grad_down,) = finish(place, down_grad.result, write_hidden, [(shard, hidden)])
    grad_up, grad_down = close_round(last_grad, hold=(grad_up, grad_down))
    grad_qkv, grad_proj, rest_sums = finish(
        place, last_grad.result, write_last, [(shard, 3 * width), (shard, width), (shard, LANES)]
    )
    rows = rest_sums[:, : 6 + up_cols].T
    first_rows = lax.dynamic_slice_in_dim(late.result.reshape(2, width), lax.axis_index("fsdp") * shard, shard, axis=1)
    grad_upbias = rows[6:].reshape(up_cols * shard)[:up_shard]
    grad_gains = jnp.stack([first_rows[0], rows[2]])
    grad_biases = jnp.stack([first_rows[1], rows[3], rows[0], rows[1], rows[4], rows[5]])
    return (layer_out, grad_in, grad_qkv, grad_proj, grad_up, grad_down.T, grad_gains, grad_biases, grad_upbias)


def for_sending(array):
    return jax.tree.map(lambda a: a.astype(jnp.bfloat16) if a.dtype == jnp.float32 else a, array)


def gelu_tanh(values):
    return (
        0.5
        * values
        * (1.0 + jnp.tanh(GELU_SCALE * (values + GELU_CUBE * values * values * values)))
    )


def gelu_slope(values):
    tangent = jnp.tanh(GELU_SCALE * (values + GELU_CUBE * values * values * values))
    return 0.5 * (1.0 + tangent) + 0.5 * values * (1.0 - tangent * tangent) * GELU_SCALE * (
        1.0 + 3.0 * GELU_CUBE * values * values
    )


def block_scores(q_block, keys_full, live, score_scale):
    scores = (
        jnp.einsum("qhd,khd->hqk", q_block, keys_full, preferred_element_type=jnp.float32)
        * score_scale
    )
    return jnp.where(live[None, None, :] > 0, scores, NEG_FILL)


def forward_image(pieces, block_rows, score_scale):
    query, keys_full, values_full, live = pieces
    out_parts = []
    total_parts = []
    for start in range(0, query.shape[0], block_rows):
        masked = block_scores(query[start : start + block_rows], keys_full, live, score_scale)
        top_score = jnp.max(masked, axis=-1, keepdims=True)
        log_total = top_score + jnp.log(
            jnp.sum(jnp.exp(masked - top_score), axis=-1, keepdims=True)
        )
        probs_low = jnp.exp(masked - log_total).astype(jnp.bfloat16)
        out_parts.append(
            jnp.einsum(
                "hqk,khd->qhd", probs_low, values_full, preferred_element_type=jnp.float32
            ).astype(jnp.bfloat16)
        )
        total_parts.append(log_total)
    return (jnp.concatenate(out_parts, axis=0), jnp.concatenate(total_parts, axis=1))


def backward_image(pieces, block_rows, score_scale):
    query, keys_full, values_full, live, log_totals, d_heads = pieces
    dq_parts = []
    dk_total = jnp.zeros(keys_full.shape, jnp.float32)
    dv_total = jnp.zeros(values_full.shape, jnp.float32)
    for start in range(0, query.shape[0], block_rows):
        q_block = query[start : start + block_rows]
        d_block = d_heads[start : start + block_rows]
        masked = block_scores(q_block, keys_full, live, score_scale)
        probs = jnp.exp(masked - log_totals[:, start : start + block_rows])
        probs_low = probs.astype(jnp.bfloat16)
        d_probs = jnp.einsum(
            "qhd,khd->hqk", d_block, values_full, preferred_element_type=jnp.float32
        )
        row_dot = jnp.sum(probs * d_probs, axis=-1, keepdims=True)
        d_scores = (probs * (d_probs - row_dot)).astype(jnp.bfloat16)
        dq_block = (
            jnp.einsum("hqk,khd->qhd", d_scores, keys_full, preferred_element_type=jnp.float32)
            * score_scale
        )
        dq_parts.append(dq_block.astype(jnp.bfloat16))
        dk_total = dk_total + jnp.einsum(
            "hqk,qhd->khd", d_scores, q_block, preferred_element_type=jnp.float32
        )
        dv_total = dv_total + jnp.einsum(
            "hqk,qhd->khd", probs_low, d_block, preferred_element_type=jnp.float32
        )
    return (
        jnp.concatenate(dq_parts, axis=0),
        (dk_total * score_scale).astype(jnp.bfloat16),
        dv_total.astype(jnp.bfloat16),
    )


def heads_over_seq(inputs, key_mask, w_qkv, w_out, w_up, w_down, norm_gains, biases, up_bias, cotangent):
    img_count, tok_count, width = inputs.shape
    seq_len = key_mask.shape[1]
    row_count = img_count * tok_count
    head_cols = width // lax.axis_size("seq")
    local_heads = head_cols // HEAD_DIM
    block_rows = min(QBLOCK, seq_len)
    score_scale = 1.0 / math.sqrt(HEAD_DIM)
    gathered = (
        lax.all_gather(w_qkv, "fsdp", axis=0, tiled=True),
        lax.all_gather(w_out, "fsdp", axis=0, tiled=True),
        lax.all_gather(w_up, "fsdp", axis=0, tiled=True),
        lax.all_gather(w_down, "fsdp", axis=1, tiled=True),
        lax.all_gather(norm_gains, "fsdp", axis=1, tiled=True),
        lax.all_gather(biases, "fsdp", axis=1, tiled=True),
        lax.all_gather(up_bias, "fsdp", axis=0, tiled=True),
    )
    full_qkv, full_out, full_up, full_down, full_gains, full_biases, full_upbias = gathered
    gain_rows = full_gains.astype(jnp.float32)
    bias_rows = full_biases.astype(jnp.float32)
    up_shift = full_upbias.astype(jnp.float32)
    qkv_shift = jnp.concatenate([bias_rows[2], jnp.zeros((width,), jnp.float32), bias_rows[3]])
    tok_wide = inputs.reshape(row_count, width).astype(jnp.float32)
    first_out, first_normed, first_inv = layer_norm(tok_wide, gain_rows[0], bias_rows[0])
    first_low = first_out.astype(jnp.bfloat16)
    packed = (jnp.dot(first_low, full_qkv, preferred_element_type=jnp.float32) + qkv_shift).astype(
        jnp.bfloat16
    )
    by_heads = lax.all_to_all(
        packed.reshape(img_count, tok_count, 3, width),
        "seq",
        split_axis=3,
        concat_axis=1,
        tiled=True,
    )
    query = by_heads[:, :, 0].reshape(img_count, seq_len, local_heads, HEAD_DIM)
    keys_full = by_heads[:, :, 1].reshape(img_count, seq_len, local_heads, HEAD_DIM)
    values_full = by_heads[:, :, 2].reshape(img_count, seq_len, local_heads, HEAD_DIM)

    def run_forward(pieces):
        return forward_image(pieces, block_rows, score_scale)

    attended_heads, log_totals = lax.map(run_forward, (query, keys_full, values_full, key_mask))
    attended = lax.all_to_all(
        for_sending(attended_heads.reshape(img_count, seq_len, head_cols)),
        "seq",
        split_axis=1,
        concat_axis=2,
        tiled=True,
    ).reshape(row_count, width)
    residual = (
        tok_wide + jnp.dot(attended, full_out, preferred_element_type=jnp.float32) + bias_rows[4]
    )
    second_out, second_normed, second_inv = layer_norm(residual, gain_rows[1], bias_rows[1])
    second_low = second_out.astype(jnp.bfloat16)
    upper = jnp.dot(second_low, full_up, preferred_element_type=jnp.float32) + up_shift
    active = gelu_tanh(upper).astype(jnp.bfloat16)
    layer_out = (
        residual + jnp.dot(active, full_down, preferred_element_type=jnp.float32) + bias_rows[5]
    ).astype(jnp.bfloat16)
    back_qkv, back_out, back_up, back_down, back_gains, back_biases, back_upbias = gathered
    back_gain_rows = back_gains.astype(jnp.float32)
    upstream = cotangent.reshape(row_count, width)
    grad_wide = upstream.astype(jnp.float32)
    d_active = jnp.dot(upstream, back_down.T, preferred_element_type=jnp.float32)
    dw_down = jnp.dot(active.T, upstream, preferred_element_type=jnp.float32)
    d_upper = (d_active * gelu_slope(upper)).astype(jnp.bfloat16)
    dw_up = jnp.dot(second_low.T, d_upper, preferred_element_type=jnp.float32)
    d_second = jnp.dot(d_upper, back_up.T, preferred_element_type=jnp.float32)
    d_resid = grad_wide + norm_back(d_second, second_normed, second_inv, back_gain_rows[1])
    d_resid_low = d_resid.astype(jnp.bfloat16)
    dw_out = jnp.dot(attended.T, d_resid_low, preferred_element_type=jnp.float32)
    d_attended = jnp.dot(d_resid_low, back_out.T, preferred_element_type=jnp.float32).astype(
        jnp.bfloat16
    )
    d_heads = lax.all_to_all(
        d_attended.reshape(img_count, tok_count, width),
        "seq",
        split_axis=2,
        concat_axis=1,
        tiled=True,
    ).reshape(img_count, seq_len, local_heads, HEAD_DIM)

    def run_backward(pieces):
        return backward_image(pieces, block_rows, score_scale)

    dq_heads, dk_heads, dv_heads = lax.map(
        run_backward, (query, keys_full, values_full, key_mask, log_totals, d_heads)
    )
    stacked = jnp.stack(
        [
            dq_heads.reshape(img_count, seq_len, head_cols),
            dk_heads.reshape(img_count, seq_len, head_cols),
            dv_heads.reshape(img_count, seq_len, head_cols),
        ],
        axis=2,
    )
    d_packed = (
        lax.all_to_all(for_sending(stacked), "seq", split_axis=1, concat_axis=3, tiled=True)
        .astype(stacked.dtype)
        .reshape(row_count, 3 * width)
    )
    d_pack_wide = d_packed.astype(jnp.float32)
    dw_qkv = jnp.dot(first_low.T, d_packed, preferred_element_type=jnp.float32)
    d_first = jnp.dot(d_packed, back_qkv.T, preferred_element_type=jnp.float32)
    grad_in = (d_resid + norm_back(d_first, first_normed, first_inv, back_gain_rows[0])).astype(
        jnp.bfloat16
    )
    d_gains = jnp.stack(
        [jnp.sum(d_first * first_normed, axis=0), jnp.sum(d_second * second_normed, axis=0)]
    )
    d_biases = jnp.stack(
        [
            jnp.sum(d_first, axis=0),
            jnp.sum(d_second, axis=0),
            jnp.sum(d_pack_wide[:, :width], axis=0),
            jnp.sum(d_pack_wide[:, 2 * width :], axis=0),
            jnp.sum(d_resid, axis=0),
            jnp.sum(grad_wide, axis=0),
        ]
    )
    d_upbias = jnp.sum(d_upper.astype(jnp.float32), axis=0)
    owned = (
        lax.psum_scatter(dw_qkv, "fsdp", scatter_dimension=0, tiled=True),
        lax.psum_scatter(dw_out, "fsdp", scatter_dimension=0, tiled=True),
        lax.psum_scatter(dw_up, "fsdp", scatter_dimension=0, tiled=True),
        lax.psum_scatter(dw_down, "fsdp", scatter_dimension=1, tiled=True),
        lax.psum_scatter(d_gains, "fsdp", scatter_dimension=1, tiled=True),
        lax.psum_scatter(d_biases, "fsdp", scatter_dimension=1, tiled=True),
        lax.psum_scatter(d_upbias, "fsdp", scatter_dimension=0, tiled=True),
    )
    summed = lax.psum((owned[0], owned[1], owned[2], owned[3], owned[4], owned[5], owned[6]), "seq")
    grad_qkv, grad_proj, grad_up, grad_down, grad_gains, grad_biases, grad_upbias = summed
    return (
        layer_out.reshape(img_count, tok_count, width),
        grad_in.reshape(img_count, tok_count, width),
        grad_qkv,
        grad_proj,
        grad_up,
        grad_down,
        grad_gains,
        grad_biases,
        grad_upbias,
    )


def solution(mesh):
    in_specs = (
        P("fsdp", "seq", None),
        P("fsdp", None),
        P("fsdp", None),
        P("fsdp", None),
        P("fsdp", None),
        P(None, "fsdp"),
        P(None, "fsdp"),
        P(None, "fsdp"),
        P("fsdp"),
        P("fsdp", "seq", None),
    )
    out_specs = (
        P("fsdp", "seq", None),
        P("fsdp", "seq", None),
        P("fsdp", None),
        P("fsdp", None),
        P("fsdp", None),
        P(None, "fsdp"),
        P(None, "fsdp"),
        P(None, "fsdp"),
        P("fsdp"),
    )

    def layer(*args):
        images = args[0].shape[0] // mesh.shape["fsdp"]
        planes = mesh.shape["fsdp"] // 2
        fits = mesh.shape["seq"] == 4 and images == 2 and planes * 2 == mesh.shape["fsdp"] and planes & (planes - 1) == 0
        plan = image_on_chip if fits else heads_over_seq
        return jax.shard_map(plan, mesh=mesh, in_specs=in_specs, out_specs=out_specs, check_vma=False)(*args)

    return layer
```
